32 devices in a mesh: dp: 4 (over z), dom: 8 (over y, x, core).
Axes of the slice: x: 2, y: 2, z: 4, core: 2. Of those that a mesh axis runs over, the one named last changes fastest.
Arguments:
- grad_out: bfloat16 [4, 24, 512, 256], P('dp', 'dom'), may hold values from -6 to 6
- pre_act: bfloat16 [4, 24, 512, 256], P('dp', 'dom'), may hold values from -6 to 6
- conv_weight: bfloat16 [27, 256, 256], replicated, may hold values from -0.078125 to 0.078125
- down_weight: bfloat16 [8, 128, 256], replicated, may hold values from -0.1875 to 0.1875
- fine_act: bfloat16 [4, 192, 512, 128], P('dp', 'dom'), may hold values from -6 to 6
- neighbours: int32 [4, 24, 27], P('dp', 'dom'), may hold values from -1 to 2, as said below
- octant_routes: int32 [4, 8, 3, 8], P('dp', 'dom'), may hold values from -1 to 23, as said below
Outputs:
- fine_grad: bfloat16 [4, 192, 512, 128], P('dp', 'dom')
- conv_weight_grad: float32 [6912, 256], P('dp')
- down_weight_grad: float32 [1024, 256], P('dp')
The draws below stay inside these ranges and needn't reach their ends.
Inputs may be any that keep to these rules, and one draw needn't show every extreme that they name: `neighbours`: each device of a scene group has between half of 3 (rounded up) and 3 live slots, always the first ones, and some device of each scene group has all 3 live. A live slot's entry 13 is itself; entry 9(a+1)+3(b+1)+(c+1) is the slot, on the device a steps along dom, of the block displaced by (a, b, c) block edges within a slab of 3 x 3 positions, or -1 where that block is empty or outside the scene group; dead slots hold -1 in all 27 entries; the relation is symmetric. `octant_routes`: row (d, k) lists what device d sends to the device d + k - 1 along dom, taken cyclically: entries 8 s + o name octant o of slot s; each live slot's 8 octants stand together, in order, in exactly one row; live entries come first, then -1. A row holds at most 8 entries, and some row of the fullest device holds exactly 8. Dead slots are never named.
All inputs are finite; a program needn't handle non-finite values.
Results may differ from the reference program's by a relative error of at most 0.0065.
Values may be sent and summed in bfloat16 or wider, within the bound.
No kernel may reach another device: no remote copies, remote signals or barrier semaphores. Data moves between devices by JAX's collectives and lax.ppermute only.
A program may use at most 128 MiB of HBM per device.

```python
import math
import jax
import jax.numpy as jnp
from jax import lax

C = 256
CF = 128
BE = 8
GRID_Y = 3
GRID_Z = 3
CAP = 3
PEER = 8
FSLOT = 24
VOX = 512
OCT = 64
SCENES = 4
BLOCKS = 24
FINE = 192
N_DOM = 8


def geometry(key):
    base = jax.random.fold_in(key, 17)
    streams = jax.random.split(base, 4)
    lowest = (CAP + 1) // 2
    counts = jax.random.randint(streams[0], (SCENES, N_DOM), lowest, CAP + 1)
    fullest = jax.random.randint(streams[1], (SCENES, 1), 0, N_DOM)
    counts = jnp.where(jnp.arange(N_DOM)[None, :] == fullest, CAP, counts)
    places = GRID_Y * GRID_Z
    scores = jax.random.randint(streams[2], (SCENES, N_DOM, places), 0, 1 << 20) * places + jnp.arange(places)[None, None, :]
    order = jnp.argsort(scores, axis=-1, stable=True)[..., :CAP].astype(jnp.int32)
    slot_ids = jnp.arange(CAP, dtype=jnp.int32)
    live = slot_ids[None, None, :] < counts[..., None]
    match = (order[..., None] == jnp.arange(places)[None, None, None, :]) & live[..., None]
    occupant = jnp.max(jnp.where(match, slot_ids[None, None, :, None], -1), axis=2).astype(jnp.int32)
    return (order, live, occupant, streams[3])


def draw_neighbours(key, part):
    order, live, occupant, spare = geometry(key)
    places = GRID_Y * GRID_Z
    pos_y = order // GRID_Z
    pos_z = order % GRID_Z
    device = jnp.zeros_like(order) + jnp.arange(N_DOM, dtype=jnp.int32)[None, :, None]
    flat_occupant = occupant.reshape(SCENES, N_DOM * places)
    entries = []
    for step_x in (-1, 0, 1):
        for step_y in (-1, 0, 1):
            for step_z in (-1, 0, 1):
                near_d = device + step_x
                near_y = pos_y + step_y
                near_z = pos_z + step_z
                valid = (near_d >= 0) & (near_d < N_DOM) & (near_y >= 0) & (near_y < GRID_Y) & (near_z >= 0) & (near_z < GRID_Z) & live
                flat = jnp.clip(near_d, 0, N_DOM - 1) * places + jnp.clip(near_y, 0, GRID_Y - 1) * GRID_Z + jnp.clip(near_z, 0, GRID_Z - 1)
                found = jnp.take_along_axis(flat_occupant, flat.reshape(SCENES, -1), axis=1).reshape(flat.shape)
                entries.append(jnp.where(valid, found, -1))
    stacked = jnp.stack(entries, axis=-1).astype(jnp.int32)
    return stacked.reshape(SCENES, N_DOM * CAP, 27)


def draw_octant_routes(key, part):
    order, live, occupant, spare = geometry(key)
    rotate = jax.random.randint(spare, (SCENES, N_DOM, 1), 0, 3)
    slot_ids = jnp.arange(CAP, dtype=jnp.int32)
    heading = (slot_ids[None, None, :] + rotate) % 3
    earlier = (heading[..., :, None] == heading[..., None, :]) & live[..., None, :] & (slot_ids[None, :] < slot_ids[:, None])[None, None]
    rank = jnp.sum(earlier.astype(jnp.int32), axis=-1)
    eighth = jnp.arange(8, dtype=jnp.int32)
    target = rank[..., None] * 8 + eighth
    value = slot_ids[:, None] * 8 + eighth[None, :]
    headings = jnp.arange(3, dtype=jnp.int32)
    places = jnp.arange(PEER, dtype=jnp.int32)
    hit = (heading[:, :, None, None, :, None] == headings[None, None, :, None, None, None]) & (target[:, :, None, None, :, :] == places[None, None, None, :, None, None]) & live[:, :, None, None, :, None]
    routes = jnp.max(jnp.where(hit, value[None, None, None, None], -1), axis=(-2, -1))
    return routes.astype(jnp.int32)


def block_levels(key, extent, cuts, least, largest):
    def one(dim, blocks):
        draws = jax.random.uniform(jax.random.fold_in(jax.random.fold_in(key, 6), dim), (blocks,), jnp.float32, least / len(cuts), largest / len(cuts))
        return jnp.repeat(jnp.exp(draws), extent[dim] // blocks).reshape((-1,) + (1,) * (len(extent) - dim - 1))

    gain = one(*cuts[0])
    for cut in cuts[1:]:
        gain = gain * one(*cut)
    return gain


def normal_values(key, dims, spread, limit, cuts=(), kind=jnp.bfloat16):
    values = jax.random.normal(key, dims, jnp.float32) * spread
    if len(cuts) > 0:
        values = block_levels(key, dims, cuts, -0.22, 0.18) * values
    return jnp.clip(values, min=-limit, max=limit).astype(kind)


def setup_inputs(seed: int = 0) -> dict:
    splits = jax.random.split(jax.random.key(seed), 8)
    grad_out = normal_values(splits[0], (SCENES, BLOCKS, VOX, C), 1.0, 6.0, ((0, 4), (1, 8)))
    pre_act = normal_values(splits[1], (SCENES, BLOCKS, VOX, C), 1.0, 6.0, ((0, 4), (1, 8)))
    conv_weight = normal_values(splits[2], (27, C, C), (27 * C) ** -0.5, 0.078125)
    down_weight = normal_values(splits[3], (8, CF, C), (8 * CF) ** -0.5, 0.1875)
    fine_act = normal_values(splits[4], (SCENES, FINE, VOX, CF), 1.0, 6.0, ((0, 4), (1, 8)))
    neighbours = draw_neighbours(jax.random.fold_in(splits[7], 71), 0)
    octant_routes = draw_octant_routes(jax.random.fold_in(splits[7], 71), 0)
    return {"grad_out": grad_out, "pre_act": pre_act, "conv_weight": conv_weight, "down_weight": down_weight, "fine_act": fine_act, "neighbours": neighbours, "octant_routes": octant_routes}


def pick_rows(source, slot_index):
    extended = jnp.concatenate([source, jnp.zeros_like(source[:1])], axis=0)
    return extended[jnp.where(slot_index < 0, source.shape[0], slot_index).astype(jnp.int32)]

def assemble(own_blocks, lower_faces, upper_faces, block_links):
    block_edge = own_blocks.shape[1]
    sources = (lower_faces, own_blocks, upper_faces)
    ranges = ((block_edge - 1, block_edge), (0, block_edge), (0, 1))
    parts_x = []
    for shift_x in range(3):
        parts_y = []
        for shift_y in range(3):
            parts_z = []
            for shift_z in range(3):
                portion = pick_rows(sources[shift_x], block_links[:, 9 * shift_x + 3 * shift_y + shift_z])
                portion = portion[:, :, ranges[shift_y][0]:ranges[shift_y][1], ranges[shift_z][0]:ranges[shift_z][1]]
                parts_z.append(portion)
            parts_y.append(jnp.concatenate(parts_z, axis=3))
        parts_x.append(jnp.concatenate(parts_y, axis=2))
    return jnp.concatenate(parts_x, axis=1)

def correlate(grad_pad, act_pad, weight):
    block_edge = grad_pad.shape[1] - 2
    channels = grad_pad.shape[-1]

    def window(padded, start_x, start_y, start_z):
        return padded[:, start_x:start_x + block_edge, start_y:start_y + block_edge, start_z:start_z + block_edge].reshape(-1, channels)
    centre_grad = window(grad_pad, 1, 1, 1)
    input_grad = jnp.zeros((centre_grad.shape[0], weight.shape[1]), jnp.float32)
    weight_grads = []
    for position in range(27):
        tap_x = position // 9 - 1
        tap_y = position // 3 % 3 - 1
        tap_z = position % 3 - 1
        input_grad = input_grad + jnp.dot(window(grad_pad, 1 - tap_x, 1 - tap_y, 1 - tap_z), weight[position].T, preferred_element_type=jnp.float32)
        weight_grads.append(jnp.dot(window(act_pad, 1 + tap_x, 1 + tap_y, 1 + tap_z).T, centre_grad, preferred_element_type=jnp.float32))
    return (input_grad, jnp.stack(weight_grads))

def split_octants(blocks):
    count_blocks = blocks.shape[0]
    half_edge = blocks.shape[1] // 2
    channels = blocks.shape[-1]
    parted = blocks.reshape(count_blocks, 2, half_edge, 2, half_edge, 2, half_edge, channels)
    parted = parted.transpose(0, 1, 3, 5, 2, 4, 6, 7)
    return parted.reshape(count_blocks * 8, half_edge * half_edge * half_edge, channels)

def reference(grad_out, pre_act, conv_weight, down_weight, fine_act, neighbours, octant_routes):

    def faces(blocks):
        zero_face = jnp.zeros_like(blocks[:1, :, :1])
        lower = jnp.concatenate([zero_face, blocks[:-1, :, BE - 1:BE]], axis=0)
        upper = jnp.concatenate([blocks[1:, :, 0:1], zero_face], axis=0)
        return (lower, upper)

    def scene(items):
        grad_scene, pre_scene, link_scene, route_scene, fine_scene = items
        grad_blocks = grad_scene.reshape(N_DOM, CAP, BE, BE, BE, C)
        act_blocks = jnp.maximum(pre_scene, 0).reshape(N_DOM, CAP, BE, BE, BE, C)
        block_links = link_scene.reshape(N_DOM, CAP, 27)
        lower_grad, upper_grad = faces(grad_blocks)
        lower_act, upper_act = faces(act_blocks)
        grad_pad = jax.vmap(assemble)(grad_blocks, lower_grad, upper_grad, block_links)
        act_pad = jax.vmap(assemble)(act_blocks, lower_act, upper_act, block_links)
        grad_pad = grad_pad.reshape((N_DOM * CAP,) + grad_pad.shape[2:])
        act_pad = act_pad.reshape((N_DOM * CAP,) + act_pad.shape[2:])
        input_grad, conv_part = correlate(grad_pad, act_pad, conv_weight)
        grad_in = jnp.where(pre_scene.reshape(-1, C) > 0, input_grad, 0.0).astype(jnp.bfloat16)
        octants = split_octants(grad_in.reshape(N_DOM * CAP, BE, BE, BE, C))
        receivers = jnp.arange(N_DOM, dtype=jnp.int32)[:, None]
        headings = jnp.arange(3, dtype=jnp.int32)[None, :]
        senders = ((receivers - headings + 1 + N_DOM) % N_DOM).astype(jnp.int32)
        entries = route_scene[senders, headings]
        flat = jnp.where(entries < 0, -1, senders[..., None] * (CAP * 8) + entries).astype(jnp.int32)
        octant_grad = pick_rows(octants, flat.reshape(-1)).reshape(N_DOM * FSLOT, OCT, C)
        fine_split = fine_scene.reshape(N_DOM * FSLOT, 8, OCT, CF)
        fine_grad = jnp.einsum('fcj,qij->fqci', octant_grad.astype(jnp.float32), down_weight.astype(jnp.float32), precision=lax.Precision.HIGHEST)
        fine_grad = fine_grad.astype(jnp.bfloat16).reshape(N_DOM * FSLOT, VOX, CF)
        down_part = jnp.einsum('fqci,fcj->qij', fine_split.astype(jnp.float32), octant_grad.astype(jnp.float32), precision=lax.Precision.HIGHEST)
        return (fine_grad, conv_part, down_part)
    fine_grad, conv_parts, down_parts = lax.map(scene, (grad_out, pre_act, neighbours, octant_routes, fine_act))
    factor = 1.0 / math.sqrt(SCENES * BLOCKS * VOX)
    conv_total = lax.optimization_barrier(jnp.sum(conv_parts, axis=0)).reshape(27 * C, C) * factor
    down_total = lax.optimization_barrier(jnp.sum(down_parts, axis=0)).reshape(8 * CF, C) * factor
    return (fine_grad, conv_total, down_total)
```

```python
import functools
import math

import jax
import jax.numpy as jnp
from jax import lax
from jax.experimental import pallas as pl
from jax.experimental.pallas import tpu as pltpu
from jax.sharding import PartitionSpec as P

BE = 8
PLANE = BE * BE
HALF = BE // 2
F32 = jnp.float32
BF16 = jnp.bfloat16
MIB = 1 << 20

VMEM = pl.BlockSpec(memory_space=pltpu.VMEM)
SMEM = pl.BlockSpec(memory_space=pltpu.SMEM)
ANY = pl.BlockSpec(memory_space=pl.ANY)


def params(mib):
    return pltpu.CompilerParams(vmem_limit_bytes=mib * MIB)


def relative(index, step, count):
    if count & (count - 1) == 0:
        return index ^ step
    return lax.rem(index + step, count)


def source_of(index, step, count):
    if count & (count - 1) == 0:
        return index ^ step
    return (index - step) % count if isinstance(index, int) else lax.rem(index + count - step, count)


def exchange(value, axis, step, stride):
    count = lax.axis_size(axis) // stride
    pairs = []
    for index in range(lax.axis_size(axis)):
        high, low = divmod(index, stride)
        other = high ^ step if count & (count - 1) == 0 else (high + step) % count
        pairs.append((index, other * stride + low))
    return lax.ppermute(value, axis, pairs)


def fetch(ref, slot, start, rows):
    value = ref[jnp.maximum(slot, 0), pl.ds(start, rows), :].astype(F32)
    return jnp.where(slot >= 0, value, 0.0)


def spread(links_ref, ref, start, step_x, slot, row, win_ref):
    channels = ref.shape[-1]

    def link(step_y, step_z):
        return links_ref[slot, 9 * (step_x + 1) + 3 * (step_y + 1) + step_z + 1]

    columns = {}
    for step_z in (-1, 0, 1):
        below = fetch(ref, link(-1, step_z), start + PLANE - 16, 16).reshape(2, BE, channels)[1:]
        middle = fetch(ref, link(0, step_z), start, PLANE).reshape(BE, BE, channels)
        above = fetch(ref, link(1, step_z), start, 16).reshape(2, BE, channels)[:1]
        columns[step_z] = jnp.concatenate([below, middle, above], axis=0)
    place_z = lax.broadcasted_iota(jnp.int32, columns[0].shape, 1)
    shifted = {
        0: columns[0],
        -1: jnp.where(
            place_z == 0, pltpu.roll(columns[-1], 1, axis=1), pltpu.roll(columns[0], 1, axis=1)
        ),
        1: jnp.where(
            place_z == BE - 1,
            pltpu.roll(columns[1], BE - 1, axis=1),
            pltpu.roll(columns[0], BE - 1, axis=1),
        ),
    }
    for tap_y in (-1, 0, 1):
        for tap_z in (-1, 0, 1):
            tap = 3 * (tap_y + 1) + tap_z + 1
            value = shifted[-tap_z][1 - tap_y : 1 - tap_y + BE].reshape(PLANE, channels)
            win_ref[pl.ds(row, PLANE), tap * channels : (tap + 1) * channels] = value.astype(BF16)


def build_windows(links_ref, own_ref, low_ref, high_ref, win_ref):
    slots = own_ref.shape[0]

    def edge(slot, carry):
        spread(links_ref, low_ref, 0, -1, slot, pl.multiple_of(slot * PLANE, PLANE), win_ref)
        row = ((BE + 1) * slots + slot) * PLANE
        spread(links_ref, high_ref, 0, 1, slot, pl.multiple_of(row, PLANE), win_ref)
        return carry

    def inner(step, carry):
        x = step // slots
        slot = step - x * slots
        row = (x + 1) * slots * PLANE + slot * PLANE
        start = pl.multiple_of(x * PLANE, PLANE)
        spread(links_ref, own_ref, start, 0, slot, pl.multiple_of(row, PLANE), win_ref)
        return carry

    lax.fori_loop(0, slots, edge, 0)
    lax.fori_loop(0, BE * slots, inner, 0)


def input_kernel(
    links_ref, routes_ref, own_ref, low_ref, high_ref, pre_ref, weight_ref,
    to_lower_ref, stay_ref, to_upper_ref,
    win_ref, taps_ref, acc_ref, octants_ref, tap_sems, out_sems,
):
    slots, voxels, channels = own_ref.shape
    places = routes_ref.shape[1]
    groups = places // 8
    copies = []
    for tap in range(27):
        index_x, rest = divmod(tap, 9)
        copy = pltpu.make_async_copy(
            weight_ref.at[tap],
            taps_ref.at[index_x, :, rest * channels : (rest + 1) * channels],
            tap_sems.at[tap],
        )
        copy.start()
        copies.append(copy)
    build_windows(links_ref, own_ref, low_ref, high_ref, win_ref)
    for copy in copies:
        copy.wait()
    slab = slots * PLANE
    rows = BE * slab
    half = rows // 2

    def multiply(part, carry):
        start = part * half
        total = None
        for index_x in range(3):
            offset = pl.multiple_of(start + (2 - index_x) * slab, PLANE)
            term = lax.dot_general(
                win_ref[pl.ds(offset, half), :],
                taps_ref[index_x],
                (((1,), (1,)), ((), ())),
                preferred_element_type=F32,
            )
            total = term if total is None else total + term
        acc_ref[pl.ds(pl.multiple_of(start, PLANE), half), :] = total
        return carry

    lax.fori_loop(0, 2, multiply, 0)
    octants_ref[...] = jnp.zeros_like(octants_ref)
    place_z = lax.broadcasted_iota(jnp.int32, (BE // 2, BE, channels), 1)
    for slot in range(slots):
        group = jnp.int32(3 * groups)
        for row in range(3):
            for part in range(groups):
                group = jnp.where(
                    routes_ref[row, 8 * part] == 8 * slot, row * groups + part, group
                )

        def finish(x, carry):
            value = acc_ref[pl.ds(pl.multiple_of(x * slab + slot * PLANE, PLANE), PLANE), :]
            pre = pre_ref[slot, pl.ds(pl.multiple_of(x * PLANE, PLANE), PLANE), :].astype(F32)
            value = jnp.where(pre > 0, value, 0.0).reshape(BE // 2, 2, BE, channels)
            even, odd = value[:, 0], value[:, 1]
            near = jnp.where(place_z < HALF, even, pltpu.roll(odd, HALF, axis=1))
            far = jnp.where(place_z < HALF, pltpu.roll(even, HALF, axis=1), odd)
            side = x // HALF
            row = (x - side * HALF) * 16
            for side_y in range(2):
                for side_z, piece in enumerate((near, far)):
                    block = piece[2 * side_y : 2 * side_y + 2].reshape(16, channels).astype(BF16)
                    start = (4 * side + 2 * side_y + side_z) * PLANE + row
                    octants_ref[group, pl.ds(pl.multiple_of(start, 16), 16), :] = block
            return carry

        lax.fori_loop(0, BE, finish, 0)
    outs = []
    for row, ref in enumerate((to_lower_ref, stay_ref, to_upper_ref)):
        copy = pltpu.make_async_copy(
            octants_ref.at[pl.ds(row * groups, groups)], ref, out_sems.at[row]
        )
        copy.start()
        outs.append(copy)
    for copy in outs:
        copy.wait()


def input_gradient(links, routes, own, low, high, pre, weight):
    slots, voxels, channels = own.shape
    groups = routes.shape[1] // 8
    rows = slots * voxels
    out = jax.ShapeDtypeStruct((groups, voxels, channels), BF16)
    return pl.pallas_call(
        input_kernel,
        out_shape=(out, out, out),
        in_specs=[SMEM, SMEM, VMEM, VMEM, VMEM, VMEM, ANY],
        out_specs=(ANY, ANY, ANY),
        scratch_shapes=[
            pltpu.VMEM((slots * PLANE * (BE + 2), 9 * channels), BF16),
            pltpu.VMEM((3, channels, 9 * channels), BF16),
            pltpu.VMEM((rows, channels), F32),
            pltpu.VMEM((3 * groups + 1, voxels, channels), BF16),
            pltpu.SemaphoreType.DMA((27,)),
            pltpu.SemaphoreType.DMA((3,)),
        ],
        compiler_params=params(48),
        cost_estimate=pl.CostEstimate(
            flops=2 * rows * 27 * channels * channels, bytes_accessed=8 * MIB, transcendentals=0
        ),
        name="input_gradient",
    )(links, routes, own, low, high, pre, weight)


def filter_kernel(
    shard_rows, where_ref, links_ref, own_ref, low_ref, high_ref, pre_ref,
    keep_ref, send_ref, win_ref, act_ref,
):
    slots, voxels, channels = own_ref.shape
    slab = slots * PLANE
    rows = BE * slab
    lanes = channels // 2
    for pair in range(BE // 2):
        parts = []
        for x in (2 * pair, 2 * pair + 1):
            for slot in range(slots):
                parts.append(pre_ref[slot, x * PLANE : (x + 1) * PLANE, :])
        block = jnp.maximum(jnp.concatenate(parts, axis=0).astype(F32), 0.0)
        act_ref[:, pair * 2 * slab : (pair + 1) * 2 * slab] = block.T.astype(BF16)
    build_windows(links_ref, own_ref, low_ref, high_ref, win_ref)
    first = lax.rem(where_ref[0], 2) == 0
    unit = math.gcd(channels, shard_rows)

    def step(index_x, carry):
        offset = pl.multiple_of((2 - index_x) * slab, PLANE)
        for rest in range(9):
            total = jnp.dot(
                act_ref[...],
                win_ref[pl.ds(offset, rows), rest * channels : (rest + 1) * channels],
                preferred_element_type=F32,
            )
            left, right = total[:, :lanes], total[:, lanes:]
            keep = jnp.where(first, left, right).astype(BF16)
            send = jnp.where(first, right, left).astype(BF16)
            for part in range(channels // unit):
                row = (index_x * 9 + rest) * channels + part * unit
                shard = row // shard_rows
                start = pl.multiple_of(row - shard * shard_rows, unit)
                span = slice(part * unit, (part + 1) * unit)
                keep_ref[shard, pl.ds(start, unit), :] = keep[span]
                send_ref[shard, pl.ds(start, unit), :] = send[span]
        return carry

    lax.fori_loop(0, 3, step, 0)


def filter_gradient(shards, where, links, own, low, high, pre):
    slots, voxels, channels = own.shape
    shard_rows = 27 * channels // shards
    rows = slots * voxels
    out = jax.ShapeDtypeStruct((shards, shard_rows, channels // 2), BF16)
    return pl.pallas_call(
        functools.partial(filter_kernel, shard_rows),
        out_shape=(out, out),
        in_specs=[SMEM, SMEM, VMEM, VMEM, VMEM, VMEM],
        out_specs=(VMEM, VMEM),
        scratch_shapes=[
            pltpu.VMEM((slots * PLANE * (BE + 2), 9 * channels), BF16),
            pltpu.VMEM((channels, rows), BF16),
        ],
        compiler_params=params(48),
        cost_estimate=pl.CostEstimate(
            flops=2 * rows * 27 * channels * channels, bytes_accessed=8 * MIB, transcendentals=0
        ),
        name="filter_gradient",
    )(where, links, own, low, high, pre)


def fine_kernel(
    where_ref, upper_ref, stay_ref, lower_ref, weight_ref, act_ref,
    grad_ref, keep_ref, send_ref, acc_ref,
):
    step = pl.program_id(0)
    fine, voxels, fine_channels = act_ref.shape
    channels = upper_ref.shape[-1]
    taps = weight_ref.shape[0]
    cells = voxels // taps

    @pl.when(step == 0)
    def _():
        acc_ref[...] = jnp.zeros_like(acc_ref)

    def work(ref):
        octants = ref[0]
        product = lax.dot_general(
            octants,
            weight_ref[...].reshape(taps * fine_channels, channels),
            (((1,), (1,)), ((), ())),
            preferred_element_type=F32,
        ).astype(BF16)
        wide = []
        for place in range(fine):
            for tap in range(taps):
                grad_ref[place, tap * cells : (tap + 1) * cells, :] = product[
                    place * cells : (place + 1) * cells,
                    tap * fine_channels : (tap + 1) * fine_channels,
                ]
            wide.append(
                jnp.concatenate(
                    [act_ref[place, tap * cells : (tap + 1) * cells, :] for tap in range(taps)],
                    axis=1,
                )
            )
        acc_ref[...] += jnp.dot(
            octants.T, jnp.concatenate(wide, axis=0), preferred_element_type=F32
        )

    for row, ref in enumerate((upper_ref, stay_ref, lower_ref)):
        pl.when(step == row)(functools.partial(work, ref))

    @pl.when(step == pl.num_programs(0) - 1)
    def _():
        first = lax.rem(where_ref[0], 2) == 0
        total = acc_ref[...].T
        lanes = channels // 2
        left, right = total[:, :lanes], total[:, lanes:]
        keep_ref[...] = jnp.where(first, left, right).astype(BF16).reshape(keep_ref.shape)
        send_ref[...] = jnp.where(first, right, left).astype(BF16).reshape(send_ref.shape)


def fine_gradient(shards, where, from_upper, stay, from_lower, weight, fine_act):
    fine, voxels, fine_channels = fine_act.shape
    groups, _, channels = stay.shape
    taps = weight.shape[0]
    per_row = 8
    whole = pl.BlockSpec((1, voxels, channels), lambda i: (0, 0, 0))
    out = jax.ShapeDtypeStruct((shards, taps * fine_channels // shards, channels // 2), BF16)
    same = pl.BlockSpec(out.shape, lambda i: (0, 0, 0))
    block = pl.BlockSpec((per_row, voxels, fine_channels), lambda i: (i, 0, 0))
    return pl.pallas_call(
        fine_kernel,
        grid=(3,),
        out_shape=(jax.ShapeDtypeStruct(fine_act.shape, BF16), out, out),
        in_specs=[
            SMEM, whole, whole, whole,
            pl.BlockSpec(weight.shape, lambda i: (0, 0, 0)),
            block,
        ],
        out_specs=(block, same, same),
        scratch_shapes=[pltpu.VMEM((channels, taps * fine_channels), F32)],
        compiler_params=params(40),
        cost_estimate=pl.CostEstimate(
            flops=4 * fine * voxels * fine_channels * channels, bytes_accessed=8 * MIB,
            transcendentals=0,
        ),
        name="fine_gradient",
    )(where, from_upper, stay, from_lower, weight, fine_act)


def pair_kernel(count, piece, where_ref, *refs):
    keeps, gots, outs = refs[:2], refs[2:4], refs[4 : 4 + count]
    scratch = refs[4 + count]
    shards = scratch.shape[0]
    start = 0
    for keep_ref, got_ref in zip(keeps, gots):
        rows = keep_ref.shape[1]
        scratch[:, start : start + rows, :] = keep_ref[...].astype(F32) + got_ref[...].astype(F32)
        start += rows
    high = where_ref[0] // 2
    for step, ref in enumerate(outs):
        row = pl.multiple_of(relative(high, step, count) * piece, 16)
        ref[...] = scratch[:, pl.ds(row, piece), :].astype(ref.dtype)


def pair_sum(where, count, piece, keeps, gots):
    shards, _, lanes = keeps[0].shape
    shape = (shards, piece, lanes)
    return pl.pallas_call(
        functools.partial(pair_kernel, count, piece),
        out_shape=[jax.ShapeDtypeStruct(shape, F32 if step == 0 else BF16) for step in range(count)],
        in_specs=[SMEM] + [VMEM] * 4,
        out_specs=[VMEM] * count,
        scratch_shapes=[pltpu.VMEM((shards, piece * count, lanes), F32)],
        compiler_params=params(40),
        name="pair_sum",
    )(where, *keeps, *gots)


def plane_kernel(count, where_ref, *refs):
    shards = refs[0].shape[0]
    outs = refs[count:]
    for step, ref in enumerate(outs):
        shard = relative(where_ref[1], step, shards)
        total = refs[0][shard].astype(F32)
        for part in refs[1:count]:
            total = total + part[shard].astype(F32)
        ref[...] = total.astype(ref.dtype)


def plane_sum(where, parts):
    shards, piece, lanes = parts[0].shape
    return pl.pallas_call(
        functools.partial(plane_kernel, len(parts)),
        out_shape=[
            jax.ShapeDtypeStruct((piece, lanes), F32 if step == 0 else BF16)
            for step in range(shards)
        ],
        in_specs=[SMEM] + [VMEM] * len(parts),
        out_specs=[VMEM] * shards,
        compiler_params=params(40),
        name="plane_sum",
    )(where, *parts)


def slab_kernel(factor, *refs):
    total = refs[0][...]
    for part in refs[1:-1]:
        total = total + part[...].astype(F32)
    refs[-1][...] = (total * factor).astype(BF16)


def slab_sum(factor, parts):
    return pl.pallas_call(
        functools.partial(slab_kernel, factor),
        out_shape=jax.ShapeDtypeStruct(parts[0].shape, BF16),
        in_specs=[VMEM] * len(parts),
        out_specs=VMEM,
        compiler_params=params(40),
        name="slab_sum",
    )(*parts)


def gather_kernel(count, where_ref, *refs):
    near, far = refs[:count], refs[count : 2 * count]
    conv_ref, down_ref, scratch = refs[2 * count :]
    piece, lanes = near[0].shape
    high = where_ref[0] // 2
    low = lax.rem(where_ref[0], 2)
    for side, parts in ((low, near), (1 - low, far)):
        lane = pl.multiple_of(side * lanes, lanes)
        for step, ref in enumerate(parts):
            row = pl.multiple_of(source_of(high, step, count) * piece, 16)
            scratch[pl.ds(row, piece), pl.ds(lane, lanes)] = ref[...].astype(F32)
    conv_rows = conv_ref.shape[0]
    conv_ref[...] = scratch[:conv_rows]
    down_ref[...] = scratch[conv_rows : conv_rows + down_ref.shape[0]]


def gather_up(where, conv_rows, down_rows, near, far):
    piece, lanes = near[0].shape
    count = len(near)
    return pl.pallas_call(
        functools.partial(gather_kernel, count),
        out_shape=(
            jax.ShapeDtypeStruct((conv_rows, 2 * lanes), F32),
            jax.ShapeDtypeStruct((down_rows, 2 * lanes), F32),
        ),
        in_specs=[SMEM] + [VMEM] * (2 * count),
        out_specs=(VMEM, VMEM),
        scratch_shapes=[pltpu.VMEM((count * piece, 2 * lanes), F32)],
        compiler_params=params(40),
        name="gather_up",
    )(where, *near, *far)


def body(grad_out, pre_act, conv_weight, down_weight, fine_act, neighbours, octant_routes):
    own = grad_out[0]
    pre = pre_act[0]
    links = neighbours[0]
    routes = octant_routes[0, 0]
    slots, voxels, channels = own.shape
    devices = lax.axis_size("dom")
    shards = lax.axis_size("dp")
    where = jnp.stack([lax.axis_index("dom"), lax.axis_index("dp")]).astype(jnp.int32)

    forward = [(i, i + 1) for i in range(devices - 1)]
    backward = [(i + 1, i) for i in range(devices - 1)]
    low = lax.ppermute(own[:, voxels - PLANE :], "dom", forward)
    high = lax.ppermute(own[:, :PLANE], "dom", backward)

    to_lower, stay, to_upper = input_gradient(links, routes, own, low, high, pre, conv_weight)
    ring = [(i, (i + 1) % devices) for i in range(devices)]
    from_upper = lax.ppermute(to_lower, "dom", [(b, a) for a, b in ring])
    from_lower = lax.ppermute(to_upper, "dom", ring)
    conv_keep, conv_send = filter_gradient(shards, where, links, own, low, high, pre)
    fine_grad, down_keep, down_send = fine_gradient(
        shards, where, from_upper, stay, from_lower, down_weight, fine_act[0]
    )

    count = devices // 2
    conv_rows, down_rows = conv_keep.shape[1], down_keep.shape[1]
    piece = -(-(conv_rows + down_rows) // (16 * count)) * 16
    swap = [(i, i ^ 1) for i in range(devices)]
    conv_got = lax.ppermute(conv_send, "dom", swap)
    down_got = lax.ppermute(down_send, "dom", swap)
    parts = pair_sum(where, count, piece, (conv_keep, down_keep), (conv_got, down_got))
    parts = [parts[0]] + [exchange(parts[step], "dom", step, 2) for step in range(1, count)]
    parts = plane_sum(where, parts)
    parts = [parts[0]] + [exchange(parts[step], "dp", step, 1) for step in range(1, shards)]
    factor = 1.0 / math.sqrt(shards * devices * slots * voxels)
    mine = slab_sum(factor, parts)
    near = [mine] + [exchange(mine, "dom", step, 2) for step in range(1, count)]
    far = [lax.ppermute(value, "dom", swap) for value in near]
    conv_grad, down_grad = gather_up(where, conv_rows, down_rows, near, far)
    return (fine_grad[None], conv_grad, down_grad)


def solution(mesh):
    return jax.shard_map(
        body,
        mesh=mesh,
        in_specs=(
            P("dp", "dom", None, None),
            P("dp", "dom", None, None),
            P(),
            P(),
            P("dp", "dom", None, None),
            P("dp", "dom", None),
            P("dp", "dom", None, None),
        ),
        out_specs=(P("dp", "dom", None, None), P("dp", None), P("dp", None)),
        check_vma=False,
    )
```

```python
import functools
import math

import jax
import jax.numpy as jnp
from jax import lax
from jax.experimental import pallas as pl
from jax.experimental.pallas import tpu as pltpu
from jax.sharding import PartitionSpec as P

BE = 8
PLANE = BE * BE
HALF = BE // 2
F32 = jnp.float32
BF16 = jnp.bfloat16
MIB = 1 << 20

VMEM = pl.BlockSpec(memory_space=pltpu.VMEM)
SMEM = pl.BlockSpec(memory_space=pltpu.SMEM)
ANY = pl.BlockSpec(memory_space=pl.ANY)


def params(mib):
    return pltpu.CompilerParams(vmem_limit_bytes=mib * MIB)


def relative(index, step, count):
    if count & (count - 1) == 0:
        return index ^ step
    return lax.rem(index + step, count)


def source_of(index, step, count):
    if count & (count - 1) == 0:
        return index ^ step
    return (index - step) % count if isinstance(index, int) else lax.rem(index + count - step, count)


def exchange(value, axis, step, stride):
    count = lax.axis_size(axis) // stride
    pairs = []
    for index in range(lax.axis_size(axis)):
        high, low = divmod(index, stride)
        other = high ^ step if count & (count - 1) == 0 else (high + step) % count
        pairs.append((index, other * stride + low))
    return lax.ppermute(value, axis, pairs)


def fetch(ref, slot, start, rows):
    value = ref[jnp.maximum(slot, 0), pl.ds(start, rows), :].astype(F32)
    return jnp.where(slot >= 0, value, 0.0)


def spread(links_ref, ref, start, step_x, slot, row, win_ref):
    channels = ref.shape[-1]

    def link(step_y, step_z):
        return links_ref[slot, 9 * (step_x + 1) + 3 * (step_y + 1) + step_z + 1]

    columns = {}
    for step_z in (-1, 0, 1):
        below = fetch(ref, link(-1, step_z), start + PLANE - 16, 16).reshape(2, BE, channels)[1:]
        middle = fetch(ref, link(0, step_z), start, PLANE).reshape(BE, BE, channels)
        above = fetch(ref, link(1, step_z), start, 16).reshape(2, BE, channels)[:1]
        columns[step_z] = jnp.concatenate([below, middle, above], axis=0)
    place_z = lax.broadcasted_iota(jnp.int32, columns[0].shape, 1)
    shifted = {
        0: columns[0],
        -1: jnp.where(
            place_z == 0, pltpu.roll(columns[-1], 1, axis=1), pltpu.roll(columns[0], 1, axis=1)
        ),
        1: jnp.where(
            place_z == BE - 1,
            pltpu.roll(columns[1], BE - 1, axis=1),
            pltpu.roll(columns[0], BE - 1, axis=1),
        ),
    }
    for tap_y in (-1, 0, 1):
        for tap_z in (-1, 0, 1):
            tap = 3 * (tap_y + 1) + tap_z + 1
            value = shifted[-tap_z][1 - tap_y : 1 - tap_y + BE].reshape(PLANE, channels)
            win_ref[pl.ds(row, PLANE), tap * channels : (tap + 1) * channels] = value.astype(BF16)


def build_windows(links_ref, own_ref, low_ref, high_ref, win_ref):
    slots = own_ref.shape[0]

    def edge(slot, carry):
        spread(links_ref, low_ref, 0, -1, slot, pl.multiple_of(slot * PLANE, PLANE), win_ref)
        row = ((BE + 1) * slots + slot) * PLANE
        spread(links_ref, high_ref, 0, 1, slot, pl.multiple_of(row, PLANE), win_ref)
        return carry

    def inner(step, carry):
        x = step // slots
        slot = step - x * slots
        row = (x + 1) * slots * PLANE + slot * PLANE
        start = pl.multiple_of(x * PLANE, PLANE)
        spread(links_ref, own_ref, start, 0, slot, pl.multiple_of(row, PLANE), win_ref)
        return carry

    lax.fori_loop(0, slots, edge, 0)
    lax.fori_loop(0, BE * slots, inner, 0)


def input_kernel(
    links_ref, routes_ref, own_ref, low_ref, high_ref, pre_ref, weight_ref, after_ref,
    to_lower_ref, stay_ref, to_upper_ref,
    win_ref, taps_ref, acc_ref, octants_ref, tap_sems, out_sems,
):
    slots, voxels, channels = own_ref.shape
    places = routes_ref.shape[1]
    groups = places // 8
    copies = []
    for tap in range(27):
        index_x, rest = divmod(tap, 9)
        copy = pltpu.make_async_copy(
            weight_ref.at[tap],
            taps_ref.at[index_x, :, rest * channels : (rest + 1) * channels],
            tap_sems.at[tap],
        )
        copy.start()
        copies.append(copy)
    build_windows(links_ref, own_ref, low_ref, high_ref, win_ref)
    for copy in copies:
        copy.wait()
    slab = slots * PLANE
    rows = BE * slab
    half = rows // 2

    def multiply(part, carry):
        start = part * half
        total = None
        for index_x in range(3):
            offset = pl.multiple_of(start + (2 - index_x) * slab, PLANE)
            term = lax.dot_general(
                win_ref[pl.ds(offset, half), :],
                taps_ref[index_x],
                (((1,), (1,)), ((), ())),
                preferred_element_type=F32,
            )
            total = term if total is None else total + term
        acc_ref[pl.ds(pl.multiple_of(start, PLANE), half), :] = total
        return carry

    lax.fori_loop(0, 2, multiply, 0)
    octants_ref[...] = jnp.zeros_like(octants_ref)
    place_z = lax.broadcasted_iota(jnp.int32, (BE // 2, BE, channels), 1)
    for slot in range(slots):
        group = jnp.int32(3 * groups)
        for row in range(3):
            for part in range(groups):
                group = jnp.where(
                    routes_ref[row, 8 * part] == 8 * slot, row * groups + part, group
                )

        def finish(x, carry):
            value = acc_ref[pl.ds(pl.multiple_of(x * slab + slot * PLANE, PLANE), PLANE), :]
            pre = pre_ref[slot, pl.ds(pl.multiple_of(x * PLANE, PLANE), PLANE), :].astype(F32)
            value = jnp.where(pre > 0, value, 0.0).reshape(BE // 2, 2, BE, channels)
            even, odd = value[:, 0], value[:, 1]
            near = jnp.where(place_z < HALF, even, pltpu.roll(odd, HALF, axis=1))
            far = jnp.where(place_z < HALF, pltpu.roll(even, HALF, axis=1), odd)
            side = x // HALF
            row = (x - side * HALF) * 16
            for side_y in range(2):
                for side_z, piece in enumerate((near, far)):
                    block = piece[2 * side_y : 2 * side_y + 2].reshape(16, channels).astype(BF16)
                    start = (4 * side + 2 * side_y + side_z) * PLANE + row
                    octants_ref[group, pl.ds(pl.multiple_of(start, 16), 16), :] = block
            return carry

        lax.fori_loop(0, BE, finish, 0)
    outs = []
    for row, ref in enumerate((to_lower_ref, stay_ref, to_upper_ref)):
        copy = pltpu.make_async_copy(
            octants_ref.at[pl.ds(row * groups, groups)], ref, out_sems.at[row]
        )
        copy.start()
        outs.append(copy)
    for copy in outs:
        copy.wait()


def input_gradient(links, routes, own, low, high, pre, weight, after):
    slots, voxels, channels = own.shape
    groups = routes.shape[1] // 8
    rows = slots * voxels
    out = jax.ShapeDtypeStruct((groups, voxels, channels), BF16)
    return pl.pallas_call(
        input_kernel,
        out_shape=(out, out, out),
        in_specs=[SMEM, SMEM, VMEM, VMEM, VMEM, VMEM, ANY, ANY],
        out_specs=(ANY, ANY, ANY),
        scratch_shapes=[
            pltpu.VMEM((slots * PLANE * (BE + 2), 9 * channels), BF16),
            pltpu.VMEM((3, channels, 9 * channels), BF16),
            pltpu.VMEM((rows, channels), F32),
            pltpu.VMEM((3 * groups + 1, voxels, channels), BF16),
            pltpu.SemaphoreType.DMA((27,)),
            pltpu.SemaphoreType.DMA((3,)),
        ],
        compiler_params=params(48),
        cost_estimate=pl.CostEstimate(
            flops=2 * rows * 27 * channels * channels, bytes_accessed=8 * MIB, transcendentals=0
        ),
        name="input_gradient",
    )(links, routes, own, low, high, pre, weight, after)


def filter_kernel(
    shard_rows, links_ref, own_ref, low_ref, high_ref, pre_ref,
    keep_a_ref, keep_b_ref, send_a_ref, send_b_ref, win_ref, act_ref,
):
    slots, voxels, channels = own_ref.shape
    slab = slots * PLANE
    rows = BE * slab
    lanes = channels // 2
    for pair in range(BE // 2):
        parts = []
        for x in (2 * pair, 2 * pair + 1):
            for slot in range(slots):
                parts.append(pre_ref[slot, x * PLANE : (x + 1) * PLANE, :])
        block = jnp.maximum(jnp.concatenate(parts, axis=0).astype(F32), 0.0)
        act_ref[:, pair * 2 * slab : (pair + 1) * 2 * slab] = block.T.astype(BF16)
    build_windows(links_ref, own_ref, low_ref, high_ref, win_ref)
    first = lax.rem(lax.axis_index("dom"), 2) == 0
    unit = math.gcd(channels, shard_rows)
    cut = keep_a_ref.shape[1]

    def step(index_x, carry):
        offset = pl.multiple_of((2 - index_x) * slab, PLANE)
        for rest in range(9):
            total = jnp.dot(
                act_ref[...],
                win_ref[pl.ds(offset, rows), rest * channels : (rest + 1) * channels],
                preferred_element_type=F32,
            )
            left, right = total[:, :lanes], total[:, lanes:]
            keep = jnp.where(first, left, right).astype(BF16)
            send = jnp.where(first, right, left).astype(BF16)
            for part in range(channels // unit):
                row = (index_x * 9 + rest) * channels + part * unit
                shard = row // shard_rows
                start = pl.multiple_of(row - shard * shard_rows, unit)
                span = slice(part * unit, (part + 1) * unit)
                @pl.when(start < cut)
                def _():
                    keep_a_ref[shard, pl.ds(start, unit), :] = keep[span]
                    send_a_ref[shard, pl.ds(start, unit), :] = send[span]

                @pl.when(start >= cut)
                def _():
                    late = pl.multiple_of(start - cut, unit)
                    keep_b_ref[shard, pl.ds(late, unit), :] = keep[span]
                    send_b_ref[shard, pl.ds(late, unit), :] = send[span]

        return carry

    lax.fori_loop(0, 3, step, 0)


def piece_rows(rows, count):
    return -(-rows // (16 * count)) * 16


def filter_gradient(shards, count, links, own, low, high, pre):
    slots, voxels, channels = own.shape
    shard_rows = 27 * channels // shards
    rows = slots * voxels
    cut = count * piece_rows(shard_rows // 2, count)
    rest = count * piece_rows(shard_rows - cut, count)
    first = jax.ShapeDtypeStruct((shards, cut, channels // 2), BF16)
    second = jax.ShapeDtypeStruct((shards, rest, channels // 2), BF16)
    return pl.pallas_call(
        functools.partial(filter_kernel, shard_rows),
        out_shape=(first, second, first, second),
        in_specs=[SMEM, VMEM, VMEM, VMEM, VMEM],
        out_specs=(VMEM, VMEM, VMEM, VMEM),
        scratch_shapes=[
            pltpu.VMEM((slots * PLANE * (BE + 2), 9 * channels), BF16),
            pltpu.VMEM((channels, rows), BF16),
        ],
        compiler_params=params(48),
        cost_estimate=pl.CostEstimate(
            flops=2 * rows * 27 * channels * channels, bytes_accessed=8 * MIB, transcendentals=0
        ),
        name="filter_gradient",
    )(links, own, low, high, pre)


def fine_kernel(
    upper_ref, stay_ref, lower_ref, weight_ref, act_ref,
    grad_ref, keep_ref, send_ref, acc_ref,
):
    step = pl.program_id(0)
    fine, voxels, fine_channels = act_ref.shape
    channels = upper_ref.shape[-1]
    taps = weight_ref.shape[0]
    cells = voxels // taps

    @pl.when(step == 0)
    def _():
        acc_ref[...] = jnp.zeros_like(acc_ref)

    def work(ref):
        octants = ref[0]
        product = lax.dot_general(
            octants,
            weight_ref[...].reshape(taps * fine_channels, channels),
            (((1,), (1,)), ((), ())),
            preferred_element_type=F32,
        ).astype(BF16)
        wide = []
        for place in range(fine):
            for tap in range(taps):
                grad_ref[place, tap * cells : (tap + 1) * cells, :] = product[
                    place * cells : (place + 1) * cells,
                    tap * fine_channels : (tap + 1) * fine_channels,
                ]
            wide.append(
                jnp.concatenate(
                    [act_ref[place, tap * cells : (tap + 1) * cells, :] for tap in range(taps)],
                    axis=1,
                )
            )
        acc_ref[...] += jnp.dot(
            octants.T, jnp.concatenate(wide, axis=0), preferred_element_type=F32
        )

    for row, ref in enumerate((upper_ref, stay_ref, lower_ref)):
        pl.when(step == row)(functools.partial(work, ref))

    @pl.when(step == pl.num_programs(0) - 1)
    def _():
        first = lax.rem(lax.axis_index("dom"), 2) == 0
        total = acc_ref[...].T
        lanes = channels // 2
        left, right = total[:, :lanes], total[:, lanes:]
        shards = keep_ref.shape[0]
        rows = total.shape[0] // shards
        keep_ref[:, :rows, :] = (
            jnp.where(first, left, right).astype(BF16).reshape(shards, rows, lanes)
        )
        send_ref[:, :rows, :] = (
            jnp.where(first, right, left).astype(BF16).reshape(shards, rows, lanes)
        )


def fine_gradient(shards, count, from_upper, stay, from_lower, weight, fine_act):
    fine, voxels, fine_channels = fine_act.shape
    groups, _, channels = stay.shape
    taps = weight.shape[0]
    per_row = 8
    whole = pl.BlockSpec((1, voxels, channels), lambda i: (0, 0, 0))
    rows = taps * fine_channels // shards
    padded = count * piece_rows(rows, count)
    out = jax.ShapeDtypeStruct((shards, padded, channels // 2), BF16)
    same = pl.BlockSpec(out.shape, lambda i: (0, 0, 0))
    block = pl.BlockSpec((per_row, voxels, fine_channels), lambda i: (i, 0, 0))
    return pl.pallas_call(
        fine_kernel,
        grid=(3,),
        out_shape=(jax.ShapeDtypeStruct(fine_act.shape, BF16), out, out),
        in_specs=[
            whole, whole, whole,
            pl.BlockSpec(weight.shape, lambda i: (0, 0, 0)),
            block,
        ],
        out_specs=(block, same, same),
        scratch_shapes=[pltpu.VMEM((channels, taps * fine_channels), F32)],
        compiler_params=params(40),
        cost_estimate=pl.CostEstimate(
            flops=4 * fine * voxels * fine_channels * channels, bytes_accessed=8 * MIB,
            transcendentals=0,
        ),
        name="fine_gradient",
    )(from_upper, stay, from_lower, weight, fine_act)


def cost(*arrays):
    moved = sum(math.prod(x.shape) * jnp.dtype(x.dtype).itemsize for x in arrays)
    return pl.CostEstimate(flops=moved, bytes_accessed=moved, transcendentals=0)


def pair_kernel(count, keep_ref, got_ref, *outs):
    piece = outs[0].shape[1]
    high = lax.axis_index("dom") // 2
    for step, ref in enumerate(outs):
        rows = pl.ds(pl.multiple_of(relative(high, step, count) * piece, 16), piece)
        total = keep_ref[:, rows, :].astype(F32) + got_ref[:, rows, :].astype(F32)
        ref[...] = total.astype(ref.dtype)


def pair_sum(count, keep, got):
    shards, rows, lanes = keep.shape
    shape = (shards, rows // count, lanes)
    outs = [jax.ShapeDtypeStruct(shape, F32 if step == 0 else BF16) for step in range(count)]
    return pl.pallas_call(
        functools.partial(pair_kernel, count),
        out_shape=outs,
        in_specs=[VMEM] * 2,
        out_specs=[VMEM] * count,
        compiler_params=params(32),
        cost_estimate=cost(keep, got, *outs),
        name="pair_sum",
    )(keep, got)


def plane_kernel(count, streams, *refs):
    parts, outs = refs[: count * streams], refs[count * streams :]
    shards = parts[0].shape[0]
    for step, ref in enumerate(outs):
        shard = relative(lax.axis_index("dp"), step, shards)
        start = 0
        for stream in range(streams):
            group = parts[stream * count : (stream + 1) * count]
            total = group[0][shard].astype(F32)
            for part in group[1:]:
                total = total + part[shard].astype(F32)
            rows = total.shape[0]
            ref[start : start + rows, :] = total.astype(ref.dtype)
            start += rows


def plane_sum(streams):
    parts = [part for stream in streams for part in stream]
    shards, _, lanes = parts[0].shape
    piece = sum(stream[0].shape[1] for stream in streams)
    outs = [
        jax.ShapeDtypeStruct((piece, lanes), F32 if step == 0 else BF16) for step in range(shards)
    ]
    return pl.pallas_call(
        functools.partial(plane_kernel, len(streams[0]), len(streams)),
        out_shape=outs,
        in_specs=[VMEM] * len(parts),
        out_specs=[VMEM] * shards,
        compiler_params=params(32),
        cost_estimate=cost(*parts, *outs),
        name="plane_sum",
    )(*parts)


def slab_kernel(factor, *refs):
    total = refs[0][...]
    for part in refs[1:-1]:
        total = total + part[...].astype(F32)
    refs[-1][...] = (total * factor).astype(BF16)


def slab_sum(factor, parts):
    return pl.pallas_call(
        functools.partial(slab_kernel, factor),
        out_shape=jax.ShapeDtypeStruct(parts[0].shape, BF16),
        in_specs=[VMEM] * len(parts),
        out_specs=VMEM,
        compiler_params=params(32),
        cost_estimate=cost(*parts),
        name="slab_sum",
    )(*parts)


def gather_kernel(count, layout, *refs):
    inputs = refs[: 2 * count * len(layout)]
    conv_ref, down_ref, *scratches = refs[len(inputs) :]
    lanes = inputs[0].shape[1]
    high = lax.axis_index("dom") // 2
    low = lax.rem(lax.axis_index("dom"), 2)
    scratch = iter(scratches)
    for chunk, streams in enumerate(layout):
        parts = inputs[2 * count * chunk : 2 * count * (chunk + 1)]
        start = 0
        for output, first, piece in streams:
            whole = next(scratch)
            for side, group in ((low, parts[:count]), (1 - low, parts[count:])):
                lane = pl.ds(pl.multiple_of(side * lanes, lanes), lanes)
                for step, ref in enumerate(group):
                    row = pl.multiple_of(source_of(high, step, count) * piece, 16)
                    whole[pl.ds(row, piece), lane] = ref[start : start + piece, :].astype(F32)
            out_ref = (conv_ref, down_ref)[output]
            rows = min(count * piece, out_ref.shape[0] - first)
            out_ref[first : first + rows, :] = whole[:rows, :]
            start += piece


def gather_up(shapes, layout, chunks):
    inputs = [part for near, far in chunks for part in near + far]
    count = len(chunks[0][0])
    lanes = inputs[0].shape[1]
    outs = [jax.ShapeDtypeStruct(shape, F32) for shape in shapes]
    return pl.pallas_call(
        functools.partial(gather_kernel, count, layout),
        out_shape=outs,
        in_specs=[VMEM] * len(inputs),
        out_specs=[VMEM] * 2,
        scratch_shapes=[
            pltpu.VMEM((count * piece, 2 * lanes), F32)
            for streams in layout
            for _, _, piece in streams
        ],
        compiler_params=params(32),
        cost_estimate=cost(*inputs, *outs),
        name="gather_up",
    )(*inputs)


def body(grad_out, pre_act, conv_weight, down_weight, fine_act, neighbours, octant_routes):
    own = grad_out[0]
    pre = pre_act[0]
    links = neighbours[0]
    routes = octant_routes[0, 0]
    slots, voxels, channels = own.shape
    devices = lax.axis_size("dom")
    shards = lax.axis_size("dp")

    forward = [(i, i + 1) for i in range(devices - 1)]
    backward = [(i + 1, i) for i in range(devices - 1)]
    low = lax.ppermute(own[:, voxels - PLANE :], "dom", forward)
    high = lax.ppermute(own[:, :PLANE], "dom", backward)

    count = devices // 2
    swap = [(i, i ^ 1) for i in range(devices)]
    ring = [(i, (i + 1) % devices) for i in range(devices)]
    factor = 1.0 / math.sqrt(shards * devices * slots * voxels)

    def across_plane(keep, send):
        parts = pair_sum(count, keep, lax.ppermute(send, "dom", swap))
        return [parts[0]] + [exchange(parts[step], "dom", step, 2) for step in range(1, count)]

    def finish(streams):
        parts = plane_sum(streams)
        parts = [parts[0]] + [exchange(parts[step], "dp", step, 1) for step in range(1, shards)]
        mine = slab_sum(factor, parts)
        near = [mine] + [exchange(mine, "dom", step, 2) for step in range(1, count)]
        return near, [lax.ppermute(value, "dom", swap) for value in near]

    keep_a, keep_b, send_a, send_b = filter_gradient(shards, count, links, own, low, high, pre)
    stream_a = across_plane(keep_a, send_a)
    stream_b = across_plane(keep_b, send_b)
    to_lower, stay, to_upper = input_gradient(
        links, routes, own, low, high, pre, conv_weight, stream_b[0]
    )
    from_upper = lax.ppermute(to_lower, "dom", [(b, a) for a, b in ring])
    from_lower = lax.ppermute(to_upper, "dom", ring)
    fine_grad, down_keep, down_send = fine_gradient(
        shards, count, from_upper, stay, from_lower, down_weight, fine_act[0]
    )
    stream_d = across_plane(down_keep, down_send)
    chunk_a = finish([stream_a])
    chunk_b = finish([stream_b, stream_d])
    conv_rows = 27 * channels // shards
    down_rows = down_weight.shape[0] * down_weight.shape[1] // shards
    piece_a, piece_b, piece_d = (s[0].shape[1] for s in (stream_a, stream_b, stream_d))
    layout = (((0, 0, piece_a),), ((0, count * piece_a, piece_b), (1, 0, piece_d)))
    conv_grad, down_grad = gather_up(
        ((conv_rows, channels), (down_rows, channels)), layout, (chunk_a, chunk_b)
    )
    return (fine_grad[None], conv_grad, down_grad)


def solution(mesh):
    return jax.shard_map(
        body,
        mesh=mesh,
        in_specs=(
            P("dp", "dom", None, None),
            P("dp", "dom", None, None),
            P(),
            P(),
            P("dp", "dom", None, None),
            P("dp", "dom", None),
            P("dp", "dom", None, None),
        ),
        out_specs=(P("dp", "dom", None, None), P("dp", None), P("dp", None)),
        check_vma=False,
    )
```

```python
import functools
import math

import jax
import jax.numpy as jnp
from jax import lax
from jax.experimental import pallas as pl
from jax.experimental.pallas import tpu as pltpu
from jax.sharding import PartitionSpec as P

BE = 8
PLANE = BE * BE
HALF = BE // 2
F32 = jnp.float32
BF16 = jnp.bfloat16
MIB = 1 << 20

VMEM = pl.BlockSpec(memory_space=pltpu.VMEM)
SMEM = pl.BlockSpec(memory_space=pltpu.SMEM)
ANY = pl.BlockSpec(memory_space=pl.ANY)


def params(mib):
    return pltpu.CompilerParams(vmem_limit_bytes=mib * MIB)


def relative(index, step, count):
    if count & (count - 1) == 0:
        return index ^ step
    return lax.rem(index + step, count)


def source_of(index, step, count):
    if count & (count - 1) == 0:
        return index ^ step
    return (index - step) % count if isinstance(index, int) else lax.rem(index + count - step, count)


def exchange(value, axis, step, stride):
    count = lax.axis_size(axis) // stride
    pairs = []
    for index in range(lax.axis_size(axis)):
        high, low = divmod(index, stride)
        other = high ^ step if count & (count - 1) == 0 else (high + step) % count
        pairs.append((index, other * stride + low))
    return lax.ppermute(value, axis, pairs)


def fetch(ref, slot, start, rows):
    value = ref[jnp.maximum(slot, 0), pl.ds(start, rows), :].astype(F32)
    return jnp.where(slot >= 0, value, 0.0)


def spread(links_ref, ref, start, step_x, slot, row, win_ref):
    channels = ref.shape[-1]

    def link(step_y, step_z):
        return links_ref[slot, 9 * (step_x + 1) + 3 * (step_y + 1) + step_z + 1]

    columns = {}
    for step_z in (-1, 0, 1):
        below = fetch(ref, link(-1, step_z), start + PLANE - 16, 16).reshape(2, BE, channels)[1:]
        middle = fetch(ref, link(0, step_z), start, PLANE).reshape(BE, BE, channels)
        above = fetch(ref, link(1, step_z), start, 16).reshape(2, BE, channels)[:1]
        columns[step_z] = jnp.concatenate([below, middle, above], axis=0)
    place_z = lax.broadcasted_iota(jnp.int32, columns[0].shape, 1)
    shifted = {
        0: columns[0],
        -1: jnp.where(
            place_z == 0, pltpu.roll(columns[-1], 1, axis=1), pltpu.roll(columns[0], 1, axis=1)
        ),
        1: jnp.where(
            place_z == BE - 1,
            pltpu.roll(columns[1], BE - 1, axis=1),
            pltpu.roll(columns[0], BE - 1, axis=1),
        ),
    }
    for tap_y in (-1, 0, 1):
        for tap_z in (-1, 0, 1):
            tap = 3 * (tap_y + 1) + tap_z + 1
            value = shifted[-tap_z][1 - tap_y : 1 - tap_y + BE].reshape(PLANE, channels)
            win_ref[pl.ds(row, PLANE), tap * channels : (tap + 1) * channels] = value.astype(BF16)


def build_windows(links_ref, own_ref, low_ref, high_ref, win_ref):
    slots = own_ref.shape[0]

    def edge(slot, carry):
        spread(links_ref, low_ref, 0, -1, slot, pl.multiple_of(slot * PLANE, PLANE), win_ref)
        row = ((BE + 1) * slots + slot) * PLANE
        spread(links_ref, high_ref, 0, 1, slot, pl.multiple_of(row, PLANE), win_ref)
        return carry

    def inner(step, carry):
        x = step // slots
        slot = step - x * slots
        row = (x + 1) * slots * PLANE + slot * PLANE
        start = pl.multiple_of(x * PLANE, PLANE)
        spread(links_ref, own_ref, start, 0, slot, pl.multiple_of(row, PLANE), win_ref)
        return carry

    lax.fori_loop(0, slots, edge, 0)
    lax.fori_loop(0, BE * slots, inner, 0)


def conv_kernel(
    shard_rows, links_ref, routes_ref, own_ref, low_ref, high_ref, pre_ref, weight_ref,
    to_lower_ref, stay_ref, to_upper_ref, keep_ref, send_ref,
    win_ref, taps_ref, acc_ref, act_ref, octants_ref, tap_sems, out_sems,
):
    slots, voxels, channels = own_ref.shape
    groups = routes_ref.shape[1] // 8
    slab = slots * PLANE
    rows = BE * slab
    copies = []
    for tap in range(27):
        index_x, rest = divmod(tap, 9)
        copy = pltpu.make_async_copy(
            weight_ref.at[tap],
            taps_ref.at[index_x, :, rest * channels : (rest + 1) * channels],
            tap_sems.at[tap],
        )
        copy.start()
        copies.append(copy)
    build_windows(links_ref, own_ref, low_ref, high_ref, win_ref)
    for copy in copies:
        copy.wait()

    half = rows // 2

    def multiply(part, carry):
        start = part * half
        total = None
        for index_x in range(3):
            offset = pl.multiple_of(start + (2 - index_x) * slab, PLANE)
            term = lax.dot_general(
                win_ref[pl.ds(offset, half), :],
                taps_ref[index_x],
                (((1,), (1,)), ((), ())),
                preferred_element_type=F32,
            )
            total = term if total is None else total + term
        acc_ref[pl.ds(pl.multiple_of(start, PLANE), half), :] = total
        return carry

    lax.fori_loop(0, 2, multiply, 0)
    octants_ref[...] = jnp.zeros_like(octants_ref)
    place_z = lax.broadcasted_iota(jnp.int32, (BE // 2, BE, channels), 1)
    for slot in range(slots):
        group = jnp.int32(3 * groups)
        for row in range(3):
            for part in range(groups):
                group = jnp.where(
                    routes_ref[row, 8 * part] == 8 * slot, row * groups + part, group
                )

        def finish(x, carry):
            value = acc_ref[pl.ds(pl.multiple_of(x * slab + slot * PLANE, PLANE), PLANE), :]
            pre = pre_ref[slot, pl.ds(pl.multiple_of(x * PLANE, PLANE), PLANE), :].astype(F32)
            value = jnp.where(pre > 0, value, 0.0).reshape(BE // 2, 2, BE, channels)
            even, odd = value[:, 0], value[:, 1]
            near = jnp.where(place_z < HALF, even, pltpu.roll(odd, HALF, axis=1))
            far = jnp.where(place_z < HALF, pltpu.roll(even, HALF, axis=1), odd)
            side = x // HALF
            row = (x - side * HALF) * 16
            for side_y in range(2):
                for side_z, piece in enumerate((near, far)):
                    block = piece[2 * side_y : 2 * side_y + 2].reshape(16, channels).astype(BF16)
                    start = (4 * side + 2 * side_y + side_z) * PLANE + row
                    octants_ref[group, pl.ds(pl.multiple_of(start, 16), 16), :] = block
            return carry

        lax.fori_loop(0, BE, finish, 0)
    outs = []
    for row, ref in enumerate((to_lower_ref, stay_ref, to_upper_ref)):
        copy = pltpu.make_async_copy(
            octants_ref.at[pl.ds(row * groups, groups)], ref, out_sems.at[row]
        )
        copy.start()
        outs.append(copy)

    for pair in range(BE // 2):
        parts = []
        for x in (2 * pair, 2 * pair + 1):
            for slot in range(slots):
                parts.append(pre_ref[slot, x * PLANE : (x + 1) * PLANE, :])
        block = jnp.maximum(jnp.concatenate(parts, axis=0).astype(F32), 0.0)
        act_ref[:, pair * 2 * slab : (pair + 1) * 2 * slab] = block.T.astype(BF16)
    first = lax.rem(lax.axis_index("dom"), 2) == 0
    lanes = channels // 2
    unit = math.gcd(channels, shard_rows)

    def step(index_x, carry):
        offset = pl.multiple_of((2 - index_x) * slab, PLANE)
        for rest in range(9):
            total = jnp.dot(
                act_ref[...],
                win_ref[pl.ds(offset, rows), rest * channels : (rest + 1) * channels],
                preferred_element_type=F32,
            )
            left, right = total[:, :lanes], total[:, lanes:]
            keep = jnp.where(first, left, right).astype(BF16)
            send = jnp.where(first, right, left).astype(BF16)
            for part in range(channels // unit):
                row = (index_x * 9 + rest) * channels + part * unit
                shard = row // shard_rows
                start = pl.multiple_of(row - shard * shard_rows, unit)
                span = slice(part * unit, (part + 1) * unit)
                keep_ref[shard, pl.ds(start, unit), :] = keep[span]
                send_ref[shard, pl.ds(start, unit), :] = send[span]
        return carry

    lax.fori_loop(0, 3, step, 0)
    for copy in outs:
        copy.wait()


def conv_gradients(shards, links, routes, own, low, high, pre, weight):
    slots, voxels, channels = own.shape
    groups = routes.shape[1] // 8
    rows = slots * voxels
    shard_rows = 27 * channels // shards
    octants = jax.ShapeDtypeStruct((groups, voxels, channels), BF16)
    part = jax.ShapeDtypeStruct((shards, shard_rows, channels // 2), BF16)
    return pl.pallas_call(
        functools.partial(conv_kernel, shard_rows),
        out_shape=(octants, octants, octants, part, part),
        in_specs=[SMEM, SMEM, VMEM, VMEM, VMEM, VMEM, ANY],
        out_specs=(ANY, ANY, ANY, VMEM, VMEM),
        scratch_shapes=[
            pltpu.VMEM((slots * PLANE * (BE + 2), 9 * channels), BF16),
            pltpu.VMEM((3, channels, 9 * channels), BF16),
            pltpu.VMEM((rows, channels), F32),
            pltpu.VMEM((channels, rows), BF16),
            pltpu.VMEM((3 * groups + 1, voxels, channels), BF16),
            pltpu.SemaphoreType.DMA((27,)),
            pltpu.SemaphoreType.DMA((3,)),
        ],
        compiler_params=params(48),
        cost_estimate=pl.CostEstimate(
            flops=4 * rows * 27 * channels * channels, bytes_accessed=8 * MIB, transcendentals=0
        ),
        name="conv_gradients",
    )(links, routes, own, low, high, pre, weight)


def fine_kernel(
    factor, groups, upper_ref, stay_ref, lower_ref, weight_ref, act_ref, after_ref,
    grad_ref, down_ref, acc_ref,
):
    step = pl.program_id(0)
    fine, voxels, fine_channels = act_ref.shape
    channels = upper_ref.shape[-1]
    taps = weight_ref.shape[0]
    cells = voxels // taps

    @pl.when(step == 0)
    def _():
        acc_ref[...] = jnp.zeros_like(acc_ref)

    def work(ref):
        octants = ref[0]
        product = lax.dot_general(
            octants,
            weight_ref[...].reshape(taps * fine_channels, channels),
            (((1,), (1,)), ((), ())),
            preferred_element_type=F32,
        ).astype(BF16)
        wide = []
        for place in range(fine):
            for tap in range(taps):
                grad_ref[place, tap * cells : (tap + 1) * cells, :] = product[
                    place * cells : (place + 1) * cells,
                    tap * fine_channels : (tap + 1) * fine_channels,
                ]
            wide.append(
                jnp.concatenate(
                    [act_ref[place, tap * cells : (tap + 1) * cells, :] for tap in range(taps)],
                    axis=1,
                )
            )
        acc_ref[...] += jnp.dot(
            octants.T, jnp.concatenate(wide, axis=0), preferred_element_type=F32
        )

    for row, ref in enumerate((upper_ref, stay_ref, lower_ref)):
        pl.when(step // groups == row)(functools.partial(work, ref))

    @pl.when(step == pl.num_programs(0) - 1)
    def _():
        down_ref[...] = acc_ref[...].T * factor


def fine_gradient(factor, from_upper, stay, from_lower, weight, fine_act, after):
    fine, voxels, fine_channels = fine_act.shape
    groups, _, channels = stay.shape
    taps = weight.shape[0]
    whole = pl.BlockSpec((1, voxels, channels), lambda i: (i % groups, 0, 0))
    down = jax.ShapeDtypeStruct((taps * fine_channels, channels), F32)
    block = pl.BlockSpec((8, voxels, fine_channels), lambda i: (i, 0, 0))
    return pl.pallas_call(
        functools.partial(fine_kernel, factor, groups),
        grid=(3 * groups,),
        out_shape=(jax.ShapeDtypeStruct(fine_act.shape, BF16), down),
        in_specs=[
            whole, whole, whole,
            pl.BlockSpec(weight.shape, lambda i: (0, 0, 0)),
            block,
            ANY,
        ],
        out_specs=(block, pl.BlockSpec(down.shape, lambda i: (0, 0))),
        scratch_shapes=[pltpu.VMEM((channels, taps * fine_channels), F32)],
        compiler_params=params(40),
        cost_estimate=pl.CostEstimate(
            flops=4 * fine * voxels * fine_channels * channels, bytes_accessed=8 * MIB,
            transcendentals=0,
        ),
        name="fine_gradient",
    )(from_upper, stay, from_lower, weight, fine_act, after)


def piece_rows(rows, count):
    return -(-rows // (16 * count)) * 16


def cost(*arrays):
    moved = sum(math.prod(x.shape) * jnp.dtype(x.dtype).itemsize for x in arrays)
    return pl.CostEstimate(flops=moved, bytes_accessed=moved, transcendentals=0)


def shapes_of(count, shape):
    return [jax.ShapeDtypeStruct(shape, F32 if step == 0 else BF16) for step in range(count)]


def pair_kernel(count, keep_ref, got_ref, *outs):
    planes, slabs = outs[:count], outs[count:]
    shards, rows, _ = keep_ref.shape
    piece = planes[0].shape[1]
    high = lax.axis_index("dom") // 2
    for step, ref in enumerate(planes):
        span = pl.ds(pl.multiple_of(relative(high, step, count) * piece, 16), piece)
        total = keep_ref[:, span, :].astype(F32) + got_ref[:, span, :].astype(F32)
        ref[...] = total.astype(ref.dtype)
    cut = count * piece
    for step, ref in enumerate(slabs):
        shard = relative(lax.axis_index("dp"), step, shards)
        total = keep_ref[shard, cut:, :].astype(F32) + got_ref[shard, cut:, :].astype(F32)
        ref[: rows - cut, :] = total.astype(ref.dtype)


def pair_sum(count, keep, got):
    shards, rows, lanes = keep.shape
    piece = 2 * rows // (3 * 16 * count) * 16
    rest = count * piece_rows(rows - count * piece, count)
    outs = shapes_of(count, (shards, piece, lanes)) + shapes_of(shards, (rest, lanes))
    outs = pl.pallas_call(
        functools.partial(pair_kernel, count),
        out_shape=outs,
        in_specs=[VMEM] * 2,
        out_specs=[VMEM] * len(outs),
        compiler_params=params(32),
        cost_estimate=cost(keep, got, *outs),
        name="pair_sum",
    )(keep, got)
    return outs[:count], outs[count:]


def middle_kernel(count, shards, *refs):
    planes, slabs = refs[:count], refs[count : count + shards]
    to_slabs = refs[count + shards : count + 2 * shards]
    to_planes = refs[count + 2 * shards :]
    for step, ref in enumerate(to_slabs):
        shard = relative(lax.axis_index("dp"), step, shards)
        total = planes[0][shard]
        for part in planes[1:]:
            total = total + part[shard].astype(F32)
        ref[...] = total.astype(ref.dtype)
    piece = to_planes[0].shape[0]
    high = lax.axis_index("dom") // 2
    for step, ref in enumerate(to_planes):
        span = pl.ds(pl.multiple_of(relative(high, step, count) * piece, 16), piece)
        total = slabs[0][span, :]
        for part in slabs[1:]:
            total = total + part[span, :].astype(F32)
        ref[...] = total.astype(ref.dtype)


def middle_sum(planes, slabs):
    count, shards = len(planes), len(slabs)
    _, piece, lanes = planes[0].shape
    outs = shapes_of(shards, (piece, lanes)) + shapes_of(count, (slabs[0].shape[0] // count, lanes))
    parts = [*planes, *slabs]
    outs = pl.pallas_call(
        functools.partial(middle_kernel, count, shards),
        out_shape=outs,
        in_specs=[VMEM] * len(parts),
        out_specs=[VMEM] * len(outs),
        compiler_params=params(32),
        cost_estimate=cost(*parts, *outs),
        name="middle_sum",
    )(*parts)
    return outs[:shards], outs[shards:]


def last_kernel(factor, shards, *refs):
    out_ref = refs[-1]
    start = 0
    for group in (refs[:shards], refs[shards:-1]):
        total = group[0][...]
        for part in group[1:]:
            total = total + part[...].astype(F32)
        rows = total.shape[0]
        out_ref[start : start + rows, :] = (total * factor).astype(BF16)
        start += rows


def last_sum(factor, slabs, planes):
    piece, lanes = slabs[0].shape
    parts = [*slabs, *planes]
    return pl.pallas_call(
        functools.partial(last_kernel, factor, len(slabs)),
        out_shape=jax.ShapeDtypeStruct((piece + planes[0].shape[0], lanes), BF16),
        in_specs=[VMEM] * len(parts),
        out_specs=VMEM,
        compiler_params=params(32),
        cost_estimate=cost(*parts),
        name="last_sum",
    )(*parts)


def gather_kernel(count, pieces, *refs):
    near, far = refs[:count], refs[count : 2 * count]
    out_ref, *scratches = refs[2 * count :]
    lanes = near[0].shape[1]
    high = lax.axis_index("dom") // 2
    low = lax.rem(lax.axis_index("dom"), 2)
    start, first = 0, 0
    for piece, whole in zip(pieces, scratches):
        for side, group in ((low, near), (1 - low, far)):
            lane = pl.ds(pl.multiple_of(side * lanes, lanes), lanes)
            for step, ref in enumerate(group):
                row = pl.multiple_of(source_of(high, step, count) * piece, 16)
                whole[pl.ds(row, piece), lane] = ref[start : start + piece, :].astype(F32)
        rows = min(count * piece, out_ref.shape[0] - first)
        out_ref[first : first + rows, :] = whole[:rows, :]
        start += piece
        first += rows


def gather_up(rows, pieces, near, far):
    count = len(near)
    lanes = near[0].shape[1]
    out = jax.ShapeDtypeStruct((rows, 2 * lanes), F32)
    return pl.pallas_call(
        functools.partial(gather_kernel, count, pieces),
        out_shape=out,
        in_specs=[VMEM] * (2 * count),
        out_specs=VMEM,
        scratch_shapes=[pltpu.VMEM((count * piece, 2 * lanes), F32) for piece in pieces],
        compiler_params=params(32),
        cost_estimate=cost(*near, *far, out),
        name="gather_up",
    )(*near, *far)


def body(grad_out, pre_act, conv_weight, down_weight, fine_act, neighbours, octant_routes):
    own = grad_out[0]
    pre = pre_act[0]
    links = neighbours[0]
    routes = octant_routes[0, 0]
    slots, voxels, channels = own.shape
    devices = lax.axis_size("dom")
    shards = lax.axis_size("dp")
    count = devices // 2
    factor = 1.0 / math.sqrt(shards * devices * slots * voxels)

    forward = [(i, i + 1) for i in range(devices - 1)]
    backward = [(i + 1, i) for i in range(devices - 1)]
    ring = [(i, (i + 1) % devices) for i in range(devices)]
    swap = [(i, i ^ 1) for i in range(devices)]

    def spread_out(parts, axis, stride):
        return [parts[0]] + [
            exchange(parts[step], axis, step, stride) for step in range(1, len(parts))
        ]

    low = lax.ppermute(own[:, voxels - PLANE :], "dom", forward)
    high = lax.ppermute(own[:, :PLANE], "dom", backward)
    to_lower, stay, to_upper, keep, send = conv_gradients(
        shards, links, routes, own, low, high, pre, conv_weight
    )
    planes, slabs = pair_sum(count, keep, lax.ppermute(send, "dom", swap))
    first = planes[0]
    planes = spread_out(planes, "dom", 2)
    slabs = spread_out(slabs, "dp", 1)

    from_upper = lax.ppermute(to_lower, "dom", [(b, a) for a, b in ring])
    from_lower = lax.ppermute(to_upper, "dom", ring)
    fine_grad, down_part = fine_gradient(
        factor, from_upper, stay, from_lower, down_weight, fine_act[0], first
    )
    down_sum = lax.psum(down_part, ("dp", "dom"))
    down_rows = down_sum.shape[0] // shards
    down_grad = lax.dynamic_slice_in_dim(
        down_sum, lax.axis_index("dp") * down_rows, down_rows, 0
    )

    to_slabs, to_planes = middle_sum(planes, slabs)
    pieces = (to_slabs[0].shape[0], to_planes[0].shape[0])
    mine = last_sum(factor, spread_out(to_slabs, "dp", 1), spread_out(to_planes, "dom", 2))
    near = spread_out([mine] * count, "dom", 2)
    far = [lax.ppermute(value, "dom", swap) for value in near]
    conv_grad = gather_up(27 * channels // shards, pieces, near, far)
    return (fine_grad[None], conv_grad, down_grad)


def solution(mesh):
    return jax.shard_map(
        body,
        mesh=mesh,
        in_specs=(
            P("dp", "dom", None, None),
            P("dp", "dom", None, None),
            P(),
            P(),
            P("dp", "dom", None, None),
            P("dp", "dom", None),
            P("dp", "dom", None, None),
        ),
        out_specs=(P("dp", "dom", None, None), P("dp", None), P("dp", None)),
        check_vma=False,
    )
```

```python
import functools
import math

import jax
import jax.numpy as jnp
from jax import lax
from jax.experimental import pallas as pl
from jax.experimental.pallas import tpu as pltpu
from jax.sharding import PartitionSpec as P

BE = 8
PLANE = BE * BE
HALF = BE // 2
F32 = jnp.float32
BF16 = jnp.bfloat16
MIB = 1 << 20

VMEM = pl.BlockSpec(memory_space=pltpu.VMEM)
SMEM = pl.BlockSpec(memory_space=pltpu.SMEM)
ANY = pl.BlockSpec(memory_space=pl.ANY)


def params(mib):
    return pltpu.CompilerParams(vmem_limit_bytes=mib * MIB)


def relative(index, step, count):
    if count & (count - 1) == 0:
        return index ^ step
    return lax.rem(index + step, count)


def source_of(index, step, count):
    if count & (count - 1) == 0:
        return index ^ step
    return (index - step) % count if isinstance(index, int) else lax.rem(index + count - step, count)


def exchange(value, axis, step, stride):
    count = lax.axis_size(axis) // stride
    pairs = []
    for index in range(lax.axis_size(axis)):
        high, low = divmod(index, stride)
        other = high ^ step if count & (count - 1) == 0 else (high + step) % count
        pairs.append((index, other * stride + low))
    return lax.ppermute(value, axis, pairs)


def fetch(ref, slot, start, rows):
    value = ref[jnp.maximum(slot, 0), pl.ds(start, rows), :].astype(F32)
    return jnp.where(slot >= 0, value, 0.0)


def spread(links_ref, ref, start, step_x, slot, row, win_ref):
    channels = ref.shape[-1]

    def link(step_y, step_z):
        return links_ref[slot, 9 * (step_x + 1) + 3 * (step_y + 1) + step_z + 1]

    columns = {}
    for step_z in (-1, 0, 1):
        below = fetch(ref, link(-1, step_z), start + PLANE - 16, 16).reshape(2, BE, channels)[1:]
        middle = fetch(ref, link(0, step_z), start, PLANE).reshape(BE, BE, channels)
        above = fetch(ref, link(1, step_z), start, 16).reshape(2, BE, channels)[:1]
        columns[step_z] = jnp.concatenate([below, middle, above], axis=0)
    place_z = lax.broadcasted_iota(jnp.int32, columns[0].shape, 1)
    shifted = {
        0: columns[0],
        -1: jnp.where(
            place_z == 0, pltpu.roll(columns[-1], 1, axis=1), pltpu.roll(columns[0], 1, axis=1)
        ),
        1: jnp.where(
            place_z == BE - 1,
            pltpu.roll(columns[1], BE - 1, axis=1),
            pltpu.roll(columns[0], BE - 1, axis=1),
        ),
    }
    for tap_y in (-1, 0, 1):
        for tap_z in (-1, 0, 1):
            tap = 3 * (tap_y + 1) + tap_z + 1
            value = shifted[-tap_z][1 - tap_y : 1 - tap_y + BE].reshape(PLANE, channels)
            win_ref[pl.ds(row, PLANE), tap * channels : (tap + 1) * channels] = value.astype(BF16)


def build_windows(links_ref, own_ref, low_ref, high_ref, win_ref):
    slots = own_ref.shape[0]

    def edge(slot, carry):
        spread(links_ref, low_ref, 0, -1, slot, pl.multiple_of(slot * PLANE, PLANE), win_ref)
        row = ((BE + 1) * slots + slot) * PLANE
        spread(links_ref, high_ref, 0, 1, slot, pl.multiple_of(row, PLANE), win_ref)
        return carry

    def inner(step, carry):
        x = step // slots
        slot = step - x * slots
        row = (x + 1) * slots * PLANE + slot * PLANE
        start = pl.multiple_of(x * PLANE, PLANE)
        spread(links_ref, own_ref, start, 0, slot, pl.multiple_of(row, PLANE), win_ref)
        return carry

    lax.fori_loop(0, slots, edge, 0)
    lax.fori_loop(0, BE * slots, inner, 0)


def input_kernel(
    links_ref, routes_ref, own_ref, low_ref, high_ref, pre_ref, weight_ref,
    windows_ref, to_lower_ref, stay_ref, to_upper_ref,
    win_ref, taps_ref, acc_ref, octants_ref, tap_sems, out_sems,
):
    slots, voxels, channels = own_ref.shape
    places = routes_ref.shape[1]
    groups = places // 8
    copies = []
    for tap in range(27):
        index_x, rest = divmod(tap, 9)
        copy = pltpu.make_async_copy(
            weight_ref.at[tap],
            taps_ref.at[index_x, :, rest * channels : (rest + 1) * channels],
            tap_sems.at[tap],
        )
        copy.start()
        copies.append(copy)
    build_windows(links_ref, own_ref, low_ref, high_ref, win_ref)
    for copy in copies:
        copy.wait()
    outs = [pltpu.make_async_copy(win_ref, windows_ref, out_sems.at[3])]
    outs[0].start()
    slab = slots * PLANE
    rows = BE * slab
    half = rows // 2

    def multiply(part, carry):
        start = part * half
        total = None
        for index_x in range(3):
            offset = pl.multiple_of(start + (2 - index_x) * slab, PLANE)
            term = lax.dot_general(
                win_ref[pl.ds(offset, half), :],
                taps_ref[index_x],
                (((1,), (1,)), ((), ())),
                preferred_element_type=F32,
            )
            total = term if total is None else total + term
        acc_ref[pl.ds(pl.multiple_of(start, PLANE), half), :] = total
        return carry

    lax.fori_loop(0, 2, multiply, 0)
    octants_ref[...] = jnp.zeros_like(octants_ref)
    place_z = lax.broadcasted_iota(jnp.int32, (BE // 2, BE, channels), 1)
    for slot in range(slots):
        group = jnp.int32(3 * groups)
        for row in range(3):
            for part in range(groups):
                group = jnp.where(
                    routes_ref[row, 8 * part] == 8 * slot, row * groups + part, group
                )

        def finish(x, carry):
            value = acc_ref[pl.ds(pl.multiple_of(x * slab + slot * PLANE, PLANE), PLANE), :]
            pre = pre_ref[slot, pl.ds(pl.multiple_of(x * PLANE, PLANE), PLANE), :].astype(F32)
            value = jnp.where(pre > 0, value, 0.0).reshape(BE // 2, 2, BE, channels)
            even, odd = value[:, 0], value[:, 1]
            near = jnp.where(place_z < HALF, even, pltpu.roll(odd, HALF, axis=1))
            far = jnp.where(place_z < HALF, pltpu.roll(even, HALF, axis=1), odd)
            side = x // HALF
            row = (x - side * HALF) * 16
            for side_y in range(2):
                for side_z, piece in enumerate((near, far)):
                    block = piece[2 * side_y : 2 * side_y + 2].reshape(16, channels).astype(BF16)
                    start = (4 * side + 2 * side_y + side_z) * PLANE + row
                    octants_ref[group, pl.ds(pl.multiple_of(start, 16), 16), :] = block
            return carry

        lax.fori_loop(0, BE, finish, 0)
    for row, ref in enumerate((to_lower_ref, stay_ref, to_upper_ref)):
        copy = pltpu.make_async_copy(
            octants_ref.at[pl.ds(row * groups, groups)], ref, out_sems.at[row]
        )
        copy.start()
        outs.append(copy)
    for copy in outs:
        copy.wait()


def input_gradient(links, routes, own, low, high, pre, weight):
    slots, voxels, channels = own.shape
    groups = routes.shape[1] // 8
    rows = slots * voxels
    out = jax.ShapeDtypeStruct((groups, voxels, channels), BF16)
    windows = jax.ShapeDtypeStruct((slots * PLANE * (BE + 2), 9 * channels), BF16)
    return pl.pallas_call(
        input_kernel,
        out_shape=(windows, out, out, out),
        in_specs=[SMEM, SMEM, VMEM, VMEM, VMEM, VMEM, ANY],
        out_specs=(ANY, ANY, ANY, ANY),
        scratch_shapes=[
            pltpu.VMEM(windows.shape, BF16),
            pltpu.VMEM((3, channels, 9 * channels), BF16),
            pltpu.VMEM((rows, channels), F32),
            pltpu.VMEM((3 * groups + 1, voxels, channels), BF16),
            pltpu.SemaphoreType.DMA((27,)),
            pltpu.SemaphoreType.DMA((4,)),
        ],
        compiler_params=params(48),
        cost_estimate=pl.CostEstimate(
            flops=2 * rows * 27 * channels * channels, bytes_accessed=8 * MIB, transcendentals=0
        ),
        name="input_gradient",
    )(links, routes, own, low, high, pre, weight)


def filter_kernel(shard_rows, win_ref, pre_ref, keep_ref, send_ref, act_ref):
    slots, _, channels = pre_ref.shape
    slab = slots * PLANE
    rows = BE * slab
    lanes = channels // 2
    rest = pl.program_id(0)

    @pl.when(rest == 0)
    def _():
        for pair in range(BE // 2):
            parts = []
            for x in (2 * pair, 2 * pair + 1):
                for slot in range(slots):
                    parts.append(pre_ref[slot, x * PLANE : (x + 1) * PLANE, :])
            block = jnp.maximum(jnp.concatenate(parts, axis=0).astype(F32), 0.0)
            act_ref[:, pair * 2 * slab : (pair + 1) * 2 * slab] = block.T.astype(BF16)

    first = lax.rem(lax.axis_index("dom"), 2) == 0
    unit = math.gcd(channels, shard_rows)
    for index_x in range(3):
        offset = (2 - index_x) * slab
        total = jnp.dot(
            act_ref[...], win_ref[offset : offset + rows, :], preferred_element_type=F32
        )
        left, right = total[:, :lanes], total[:, lanes:]
        keep = jnp.where(first, left, right).astype(BF16)
        send = jnp.where(first, right, left).astype(BF16)
        for part in range(channels // unit):
            row = (index_x * 9 + rest) * channels + part * unit
            shard = row // shard_rows
            start = pl.multiple_of(row - shard * shard_rows, unit)
            span = slice(part * unit, (part + 1) * unit)
            keep_ref[shard, pl.ds(start, unit), :] = keep[span]
            send_ref[shard, pl.ds(start, unit), :] = send[span]


def filter_gradient(shards, windows, pre):
    slots, voxels, channels = pre.shape
    shard_rows = 27 * channels // shards
    rows = slots * voxels
    out = jax.ShapeDtypeStruct((shards, shard_rows, channels // 2), BF16)
    same = pl.BlockSpec(out.shape, lambda i: (0, 0, 0))
    return pl.pallas_call(
        functools.partial(filter_kernel, shard_rows),
        grid=(9,),
        out_shape=(out, out),
        in_specs=[
            pl.BlockSpec((windows.shape[0], channels), lambda i: (0, i)),
            pl.BlockSpec(pre.shape, lambda i: (0, 0, 0)),
        ],
        out_specs=(same, same),
        scratch_shapes=[pltpu.VMEM((channels, rows), BF16)],
        compiler_params=params(40),
        cost_estimate=pl.CostEstimate(
            flops=2 * rows * 27 * channels * channels, bytes_accessed=12 * MIB, transcendentals=0
        ),
        name="filter_gradient",
    )(windows, pre)


def fine_kernel(
    groups, upper_ref, stay_ref, lower_ref, weight_ref, act_ref,
    grad_ref, keep_ref, send_ref, acc_ref,
):
    step = pl.program_id(0)
    fine, voxels, fine_channels = act_ref.shape
    channels = upper_ref.shape[-1]
    taps = weight_ref.shape[0]
    cells = voxels // taps

    @pl.when(step == 0)
    def _():
        acc_ref[...] = jnp.zeros_like(acc_ref)

    def work(ref):
        octants = ref[0]
        product = lax.dot_general(
            octants,
            weight_ref[...].reshape(taps * fine_channels, channels),
            (((1,), (1,)), ((), ())),
            preferred_element_type=F32,
        ).astype(BF16)
        wide = []
        for place in range(fine):
            for tap in range(taps):
                grad_ref[place, tap * cells : (tap + 1) * cells, :] = product[
                    place * cells : (place + 1) * cells,
                    tap * fine_channels : (tap + 1) * fine_channels,
                ]
            wide.append(
                jnp.concatenate(
                    [act_ref[place, tap * cells : (tap + 1) * cells, :] for tap in range(taps)],
                    axis=1,
                )
            )
        acc_ref[...] += jnp.dot(
            octants.T, jnp.concatenate(wide, axis=0), preferred_element_type=F32
        )

    for row, ref in enumerate((upper_ref, stay_ref, lower_ref)):
        pl.when(step // groups == row)(functools.partial(work, ref))

    @pl.when(step == pl.num_programs(0) - 1)
    def _():
        total = acc_ref[...].T
        first = lax.rem(lax.axis_index("dom"), 2) == 0
        lanes = channels // 2
        shards = keep_ref.shape[0]
        rows = total.shape[0] // shards
        left = total[:, :lanes].reshape(shards, rows, lanes)
        right = total[:, lanes:].reshape(shards, rows, lanes)
        keep_ref[:, :rows, :] = jnp.where(first, left, right).astype(BF16)
        send_ref[:, :rows, :] = jnp.where(first, right, left).astype(BF16)


def fine_gradient(shards, count, from_upper, stay, from_lower, weight, fine_act):
    fine, voxels, fine_channels = fine_act.shape
    groups, _, channels = stay.shape
    taps = weight.shape[0]
    whole = pl.BlockSpec((1, voxels, channels), lambda i: (i % groups, 0, 0))
    rows = count * piece_rows(taps * fine_channels // shards, count)
    down = jax.ShapeDtypeStruct((shards, rows, channels // 2), BF16)
    same = pl.BlockSpec(down.shape, lambda i: (0, 0, 0))
    block = pl.BlockSpec((8, voxels, fine_channels), lambda i: (i, 0, 0))
    return pl.pallas_call(
        functools.partial(fine_kernel, groups),
        grid=(3 * groups,),
        out_shape=(jax.ShapeDtypeStruct(fine_act.shape, BF16), down, down),
        in_specs=[
            whole, whole, whole,
            pl.BlockSpec(weight.shape, lambda i: (0, 0, 0)),
            block,
        ],
        out_specs=(block, same, same),
        scratch_shapes=[pltpu.VMEM((channels, taps * fine_channels), F32)],
        compiler_params=params(40),
        cost_estimate=pl.CostEstimate(
            flops=64 * fine * voxels * fine_channels * channels, bytes_accessed=8 * MIB,
            transcendentals=0,
        ),
        name="fine_gradient",
    )(from_upper, stay, from_lower, weight, fine_act)


def piece_rows(rows, count):
    return -(-rows // (16 * count)) * 16


def cost(*arrays):
    moved = sum(math.prod(x.shape) * jnp.dtype(x.dtype).itemsize for x in arrays)
    return pl.CostEstimate(flops=moved, bytes_accessed=moved, transcendentals=0)


def shapes_of(count, shape):
    return [jax.ShapeDtypeStruct(shape, F32 if step == 0 else BF16) for step in range(count)]


def pair_kernel(count, conv_ref, conv_got_ref, down_ref, down_got_ref, plane_ref, *slabs):
    shards, rows, _ = conv_ref.shape
    down_piece = down_ref.shape[1] // count
    piece = plane_ref.shape[2] - down_piece
    for place in range(count):
        for keep_ref, got_ref, size, start in (
            (conv_ref, conv_got_ref, piece, 0),
            (down_ref, down_got_ref, down_piece, piece),
        ):
            span = slice(place * size, (place + 1) * size)
            total = keep_ref[:, span, :].astype(F32) + got_ref[:, span, :].astype(F32)
            plane_ref[place, :, start : start + size, :] = total.astype(BF16)
    cut = count * piece
    for step, ref in enumerate(slabs):
        shard = relative(lax.axis_index("dp"), step, shards)
        total = conv_ref[shard, cut:, :].astype(F32) + conv_got_ref[shard, cut:, :].astype(F32)
        ref[: rows - cut, :] = total.astype(ref.dtype)


def pair_sum(count, conv, conv_got, down, down_got):
    shards, rows, lanes = conv.shape
    down_piece = down.shape[1] // count
    unit = 16 * count
    piece = 16 * round((2 * (rows + down.shape[1]) / 3 - down.shape[1]) / unit)
    rest = count * piece_rows(rows - count * piece, count)
    outs = [jax.ShapeDtypeStruct((count, shards, piece + down_piece, lanes), BF16)]
    outs += shapes_of(shards, (rest, lanes))
    outs = pl.pallas_call(
        functools.partial(pair_kernel, count),
        out_shape=outs,
        in_specs=[VMEM] * 4,
        out_specs=[VMEM] * len(outs),
        compiler_params=params(32),
        cost_estimate=cost(conv, conv_got, *outs),
        name="pair_sum",
    )(conv, conv_got, down, down_got)
    return outs[0], outs[1:], (piece, down_piece, rest // count)


def middle_kernel(shards, plane_ref, *refs):
    slabs, to_slabs_ref, to_planes = refs[:shards], refs[shards], refs[shards + 1 :]
    count = plane_ref.shape[0]
    for shard in range(shards):
        total = plane_ref[0, shard].astype(F32)
        for place in range(1, count):
            total = total + plane_ref[place, shard].astype(F32)
        to_slabs_ref[shard] = total.astype(BF16)
    piece = to_planes[0].shape[0]
    high = lax.axis_index("dom") // 2
    for step, ref in enumerate(to_planes):
        span = pl.ds(pl.multiple_of(relative(high, step, count) * piece, 16), piece)
        total = slabs[0][span, :]
        for part in slabs[1:]:
            total = total + part[span, :].astype(F32)
        ref[...] = total.astype(ref.dtype)


def middle_sum(planes, slabs):
    count, shards, piece, lanes = planes.shape
    outs = [jax.ShapeDtypeStruct((shards, piece, lanes), BF16)]
    outs += shapes_of(count, (slabs[0].shape[0] // count, lanes))
    parts = [planes, *slabs]
    outs = pl.pallas_call(
        functools.partial(middle_kernel, shards),
        out_shape=outs,
        in_specs=[VMEM] * len(parts),
        out_specs=[VMEM] * len(outs),
        compiler_params=params(32),
        cost_estimate=cost(*parts, *outs),
        name="middle_sum",
    )(*parts)
    return outs[0], outs[1:]


def last_kernel(factor, slabs_ref, *refs):
    planes, out_ref = refs[:-1], refs[-1]
    piece = slabs_ref.shape[1]
    total = slabs_ref[0].astype(F32)
    for shard in range(1, slabs_ref.shape[0]):
        total = total + slabs_ref[shard].astype(F32)
    out_ref[:piece, :] = (total * factor).astype(BF16)
    total = planes[0][...]
    for part in planes[1:]:
        total = total + part[...].astype(F32)
    out_ref[piece:, :] = (total * factor).astype(BF16)


def last_sum(factor, slabs, planes):
    _, piece, lanes = slabs.shape
    parts = [slabs, *planes]
    return pl.pallas_call(
        functools.partial(last_kernel, factor),
        out_shape=jax.ShapeDtypeStruct((piece + planes[0].shape[0], lanes), BF16),
        in_specs=[VMEM] * len(parts),
        out_specs=VMEM,
        compiler_params=params(32),
        cost_estimate=cost(*parts),
        name="last_sum",
    )(*parts)


def gather_kernel(count, pieces, *refs):
    near, far = refs[:count], refs[count : 2 * count]
    conv_ref, down_ref, *scratches = refs[2 * count :]
    lanes = near[0].shape[1]
    high = lax.axis_index("dom") // 2
    low = lax.rem(lax.axis_index("dom"), 2)
    start = 0
    firsts = (0, 0, count * pieces[0])
    for piece, first, out_ref, whole in zip(
        pieces, firsts, (conv_ref, down_ref, conv_ref), scratches
    ):
        for side, group in ((low, near), (1 - low, far)):
            lane = pl.ds(pl.multiple_of(side * lanes, lanes), lanes)
            for step, ref in enumerate(group):
                row = pl.multiple_of(source_of(high, step, count) * piece, 16)
                whole[pl.ds(row, piece), lane] = ref[start : start + piece, :].astype(F32)
        rows = min(count * piece, out_ref.shape[0] - first)
        out_ref[first : first + rows, :] = whole[:rows, :]
        start += piece


def gather_up(conv_rows, down_rows, pieces, near, far):
    count = len(near)
    lanes = near[0].shape[1]
    outs = [jax.ShapeDtypeStruct((rows, 2 * lanes), F32) for rows in (conv_rows, down_rows)]
    return pl.pallas_call(
        functools.partial(gather_kernel, count, pieces),
        out_shape=outs,
        in_specs=[VMEM] * (2 * count),
        out_specs=[VMEM] * 2,
        scratch_shapes=[pltpu.VMEM((count * piece, 2 * lanes), F32) for piece in pieces],
        compiler_params=params(32),
        cost_estimate=cost(*near, *far, *outs),
        name="gather_up",
    )(*near, *far)


def body(grad_out, pre_act, conv_weight, down_weight, fine_act, neighbours, octant_routes):
    own = grad_out[0]
    pre = pre_act[0]
    links = neighbours[0]
    routes = octant_routes[0, 0]
    slots, voxels, channels = own.shape
    devices = lax.axis_size("dom")
    shards = lax.axis_size("dp")
    count = devices // 2
    factor = 1.0 / math.sqrt(shards * devices * slots * voxels)

    forward = [(i, i + 1) for i in range(devices - 1)]
    backward = [(i + 1, i) for i in range(devices - 1)]
    ring = [(i, (i + 1) % devices) for i in range(devices)]
    swap = [(i, i ^ 1) for i in range(devices)]

    def spread_out(parts, axis, stride):
        return [parts[0]] + [
            exchange(parts[step], axis, step, stride) for step in range(1, len(parts))
        ]

    low = lax.ppermute(own[:, voxels - PLANE :], "dom", forward)
    high = lax.ppermute(own[:, :PLANE], "dom", backward)
    windows, to_lower, stay, to_upper = input_gradient(
        links, routes, own, low, high, pre, conv_weight
    )
    from_upper = lax.ppermute(to_lower, "dom", [(b, a) for a, b in ring])
    from_lower = lax.ppermute(to_upper, "dom", ring)
    conv_keep, conv_send = filter_gradient(shards, windows, pre)
    fine_grad, down_keep, down_send = fine_gradient(
        shards, count, from_upper, stay, from_lower, down_weight, fine_act[0]
    )
    conv_got = lax.ppermute(conv_send, "dom", swap)
    down_got = lax.ppermute(down_send, "dom", swap)

    planes, slabs, pieces = pair_sum(count, conv_keep, conv_got, down_keep, down_got)
    same_core = [[2 * high + low for high in range(count)] for low in range(2)]
    slabs = spread_out(slabs, "dp", 1)
    planes = lax.all_to_all(planes, "dom", 0, 0, axis_index_groups=same_core)
    to_slabs, to_planes = middle_sum(planes, slabs)
    to_planes = spread_out(to_planes, "dom", 2)
    to_slabs = lax.all_to_all(to_slabs, "dp", 0, 0)
    mine = last_sum(factor, to_slabs, to_planes)
    near = spread_out([mine] * count, "dom", 2)
    far = [lax.ppermute(value, "dom", swap) for value in near]
    conv_rows = 27 * channels // shards
    down_rows = down_weight.shape[0] * down_weight.shape[1] // shards
    conv_grad, down_grad = gather_up(conv_rows, down_rows, pieces, near, far)
    return (fine_grad[None], conv_grad, down_grad)


def solution(mesh):
    return jax.shard_map(
        body,
        mesh=mesh,
        in_specs=(
            P("dp", "dom", None, None),
            P("dp", "dom", None, None),
            P(),
            P(),
            P("dp", "dom", None, None),
            P("dp", "dom", None),
            P("dp", "dom", None, None),
        ),
        out_specs=(P("dp", "dom", None, None), P("dp", None), P("dp", None)),
        check_vma=False,
    )
```

```python
import functools
import math

import jax
import jax.numpy as jnp
from jax import lax
from jax.experimental import pallas as pl
from jax.experimental.pallas import tpu as pltpu
from jax.sharding import PartitionSpec as P

BE = 8
PLANE = BE * BE
HALF = BE // 2
F32 = jnp.float32
BF16 = jnp.bfloat16
MIB = 1 << 20

VMEM = pl.BlockSpec(memory_space=pltpu.VMEM)
SMEM = pl.BlockSpec(memory_space=pltpu.SMEM)
ANY = pl.BlockSpec(memory_space=pl.ANY)
HBM = pl.BlockSpec(memory_space=pltpu.HBM)


def params(mib):
    return pltpu.CompilerParams(vmem_limit_bytes=mib * MIB)


def relative(index, step, count):
    if count & (count - 1) == 0:
        return index ^ step
    return lax.rem(index + step, count)


def source_of(index, step, count):
    if count & (count - 1) == 0:
        return index ^ step
    return (index - step) % count if isinstance(index, int) else lax.rem(index + count - step, count)


def exchange(value, axis, step, stride):
    count = lax.axis_size(axis) // stride
    pairs = []
    for index in range(lax.axis_size(axis)):
        high, low = divmod(index, stride)
        other = high ^ step if count & (count - 1) == 0 else (high + step) % count
        pairs.append((index, other * stride + low))
    return lax.ppermute(value, axis, pairs)


def fetch(ref, slot, start, rows):
    value = ref[jnp.maximum(slot, 0), pl.ds(start, rows), :].astype(F32)
    return jnp.where(slot >= 0, value, 0.0)


def spread(table_ref, ref, start, step_x, slot, row, win_ref):
    channels = ref.shape[-1]

    def link(step_y, step_z):
        return table_ref[27 * slot + 9 * (step_x + 1) + 3 * (step_y + 1) + step_z + 1]

    columns = {}
    for step_z in (-1, 0, 1):
        below = fetch(ref, link(-1, step_z), start + PLANE - 16, 16).reshape(2, BE, channels)[1:]
        middle = fetch(ref, link(0, step_z), start, PLANE).reshape(BE, BE, channels)
        above = fetch(ref, link(1, step_z), start, 16).reshape(2, BE, channels)[:1]
        columns[step_z] = jnp.concatenate([below, middle, above], axis=0)
    place_z = lax.broadcasted_iota(jnp.int32, columns[0].shape, 1)
    shifted = {
        0: columns[0],
        -1: jnp.where(
            place_z == 0, pltpu.roll(columns[-1], 1, axis=1), pltpu.roll(columns[0], 1, axis=1)
        ),
        1: jnp.where(
            place_z == BE - 1,
            pltpu.roll(columns[1], BE - 1, axis=1),
            pltpu.roll(columns[0], BE - 1, axis=1),
        ),
    }
    for tap_y in (-1, 0, 1):
        for tap_z in (-1, 0, 1):
            tap = 3 * (tap_y + 1) + tap_z + 1
            value = shifted[-tap_z][1 - tap_y : 1 - tap_y + BE].reshape(PLANE, channels)
            win_ref[pl.ds(row, PLANE), tap * channels : (tap + 1) * channels] = value.astype(BF16)


def build_windows(table_ref, own_ref, low_ref, high_ref, win_ref):
    slots = own_ref.shape[0]

    def edge(slot, carry):
        spread(table_ref, low_ref, 0, -1, slot, pl.multiple_of(slot * PLANE, PLANE), win_ref)
        row = ((BE + 1) * slots + slot) * PLANE
        spread(table_ref, high_ref, 0, 1, slot, pl.multiple_of(row, PLANE), win_ref)
        return carry

    def inner(step, carry):
        x = step // slots
        slot = step - x * slots
        row = (x + 1) * slots * PLANE + slot * PLANE
        start = pl.multiple_of(x * PLANE, PLANE)
        spread(table_ref, own_ref, start, 0, slot, pl.multiple_of(row, PLANE), win_ref)
        return carry

    lax.fori_loop(0, slots, edge, 0)
    lax.fori_loop(0, BE * slots, inner, 0)


def started(source, target, sem):
    copy = pltpu.make_async_copy(source, target, sem)
    copy.start()
    return copy


def input_kernel(
    places, table_ref, own_hbm, low_ref, high_ref, pre_hbm, weight_ref,
    to_lower_ref, stay_ref, to_upper_ref,
    own_ref, pre_ref, win_ref, taps_ref, acc_ref, octants_ref,
    in_sems, tap_sems, out_sems,
):
    slots, voxels, channels = own_ref.shape
    groups = places // 8
    own_copy = started(own_hbm.at[0], own_ref, in_sems.at[1])
    copies = []
    for tap in range(27):
        index_x, rest = divmod(tap, 9)
        lanes = slice(rest * channels, (rest + 1) * channels)
        copies.append(
            started(weight_ref.at[tap], taps_ref.at[index_x, :, lanes], tap_sems.at[tap])
        )
    pre_copy = started(pre_hbm.at[0], pre_ref, in_sems.at[2])
    own_copy.wait()
    build_windows(table_ref, own_ref, low_ref, high_ref, win_ref)
    for copy in copies:
        copy.wait()
    slab = slots * PLANE
    rows = BE * slab
    half = rows // 2

    def multiply(part, carry):
        start = part * half
        total = None
        for index_x in range(3):
            offset = pl.multiple_of(start + (2 - index_x) * slab, PLANE)
            term = lax.dot_general(
                win_ref[pl.ds(offset, half), :],
                taps_ref[index_x],
                (((1,), (1,)), ((), ())),
                preferred_element_type=F32,
            )
            total = term if total is None else total + term
        acc_ref[pl.ds(pl.multiple_of(start, PLANE), half), :] = total
        return carry

    lax.fori_loop(0, 2, multiply, 0)
    pre_copy.wait()
    octants_ref[...] = jnp.zeros_like(octants_ref)
    place_z = lax.broadcasted_iota(jnp.int32, (BE // 2, BE, channels), 1)
    for slot in range(slots):
        group = jnp.int32(3 * groups)
        for row in range(3):
            for part in range(groups):
                entry = table_ref[27 * slots + row * places + 8 * part]
                group = jnp.where(entry == 8 * slot, row * groups + part, group)

        def finish(x, carry):
            value = acc_ref[pl.ds(pl.multiple_of(x * slab + slot * PLANE, PLANE), PLANE), :]
            pre = pre_ref[slot, pl.ds(pl.multiple_of(x * PLANE, PLANE), PLANE), :].astype(F32)
            value = jnp.where(pre > 0, value, 0.0).reshape(BE // 2, 2, BE, channels)
            even, odd = value[:, 0], value[:, 1]
            near = jnp.where(place_z < HALF, even, pltpu.roll(odd, HALF, axis=1))
            far = jnp.where(place_z < HALF, pltpu.roll(even, HALF, axis=1), odd)
            side = x // HALF
            row = (x - side * HALF) * 16
            for side_y in range(2):
                for side_z, piece in enumerate((near, far)):
                    block = piece[2 * side_y : 2 * side_y + 2].reshape(16, channels).astype(BF16)
                    start = (4 * side + 2 * side_y + side_z) * PLANE + row
                    octants_ref[group, pl.ds(pl.multiple_of(start, 16), 16), :] = block
            return carry

        lax.fori_loop(0, BE, finish, 0)
    outs = []
    for row, ref in enumerate((to_lower_ref, stay_ref, to_upper_ref)):
        copy = pltpu.make_async_copy(
            octants_ref.at[pl.ds(row * groups, groups)], ref, out_sems.at[row]
        )
        copy.start()
        outs.append(copy)
    for copy in outs:
        copy.wait()


def input_gradient(table, places, own, low, high, pre, weight):
    _, slots, voxels, channels = own.shape
    groups = places // 8
    rows = slots * voxels
    out = jax.ShapeDtypeStruct((groups, voxels, channels), BF16)
    return pl.pallas_call(
        functools.partial(input_kernel, places),
        out_shape=(out, out, out),
        in_specs=[SMEM, HBM, VMEM, VMEM, HBM, HBM],
        out_specs=(ANY, ANY, ANY),
        scratch_shapes=[
            pltpu.VMEM(own.shape[1:], BF16),
            pltpu.VMEM(pre.shape[1:], BF16),
            pltpu.VMEM((slots * PLANE * (BE + 2), 9 * channels), BF16),
            pltpu.VMEM((3, channels, 9 * channels), BF16),
            pltpu.VMEM((rows, channels), F32),
            pltpu.VMEM((3 * groups + 1, voxels, channels), BF16),
            pltpu.SemaphoreType.DMA((3,)),
            pltpu.SemaphoreType.DMA((27,)),
            pltpu.SemaphoreType.DMA((3,)),
        ],
        compiler_params=params(62),
        cost_estimate=pl.CostEstimate(
            flops=2 * rows * 27 * channels * channels, bytes_accessed=8 * MIB, transcendentals=0
        ),
        name="input_gradient",
    )(table, own, low, high, pre, weight)


def filter_kernel(
    shard_rows, table_ref, own_hbm, low_ref, high_ref, pre_hbm,
    keep_ref, send_ref, own_ref, pre_ref, win_ref, act_ref, in_sems,
):
    slots, voxels, channels = own_ref.shape
    slab = slots * PLANE
    rows = BE * slab
    lanes = channels // 2
    pre_copy = started(pre_hbm.at[0], pre_ref, in_sems.at[2])
    own_copy = started(own_hbm.at[0], own_ref, in_sems.at[1])
    pre_copy.wait()
    for pair in range(BE // 2):
        parts = []
        for x in (2 * pair, 2 * pair + 1):
            for slot in range(slots):
                parts.append(pre_ref[slot, x * PLANE : (x + 1) * PLANE, :])
        block = jnp.maximum(jnp.concatenate(parts, axis=0).astype(F32), 0.0)
        act_ref[:, pair * 2 * slab : (pair + 1) * 2 * slab] = block.T.astype(BF16)
    own_copy.wait()
    build_windows(table_ref, own_ref, low_ref, high_ref, win_ref)
    first = lax.rem(lax.axis_index("dom"), 2) == 0
    unit = math.gcd(channels, shard_rows)

    def step(index_x, carry):
        offset = pl.multiple_of((2 - index_x) * slab, PLANE)
        for rest in range(9):
            total = jnp.dot(
                act_ref[...],
                win_ref[pl.ds(offset, rows), rest * channels : (rest + 1) * channels],
                preferred_element_type=F32,
            )
            left, right = total[:, :lanes], total[:, lanes:]
            keep = jnp.where(first, left, right).astype(BF16)
            send = jnp.where(first, right, left).astype(BF16)
            for part in range(channels // unit):
                row = (index_x * 9 + rest) * channels + part * unit
                shard = row // shard_rows
                start = pl.multiple_of(row - shard * shard_rows, unit)
                span = slice(part * unit, (part + 1) * unit)
                keep_ref[shard, pl.ds(start, unit), :] = keep[span]
                send_ref[shard, pl.ds(start, unit), :] = send[span]
        return carry

    lax.fori_loop(0, 3, step, 0)


def filter_gradient(shards, table, own, low, high, pre):
    _, slots, voxels, channels = own.shape
    shard_rows = 27 * channels // shards
    rows = slots * voxels
    out = jax.ShapeDtypeStruct((shards, shard_rows, channels // 2), BF16)
    return pl.pallas_call(
        functools.partial(filter_kernel, shard_rows),
        out_shape=(out, out),
        in_specs=[SMEM, HBM, VMEM, VMEM, HBM],
        out_specs=(VMEM, VMEM),
        scratch_shapes=[
            pltpu.VMEM(own.shape[1:], BF16),
            pltpu.VMEM(pre.shape[1:], BF16),
            pltpu.VMEM((slots * PLANE * (BE + 2), 9 * channels), BF16),
            pltpu.VMEM((channels, rows), BF16),
            pltpu.SemaphoreType.DMA((3,)),
        ],
        compiler_params=params(62),
        cost_estimate=pl.CostEstimate(
            flops=2 * rows * 27 * channels * channels, bytes_accessed=8 * MIB, transcendentals=0
        ),
        name="filter_gradient",
    )(table, own, low, high, pre)


def fine_kernel(
    groups, upper_ref, stay_ref, lower_ref, weight_ref, act_ref,
    grad_ref, keep_ref, send_ref, acc_ref,
):
    step = pl.program_id(0)
    fine, voxels, fine_channels = act_ref.shape
    channels = upper_ref.shape[-1]
    taps = weight_ref.shape[0]
    cells = voxels // taps

    @pl.when(step == 0)
    def _():
        acc_ref[...] = jnp.zeros_like(acc_ref)

    def work(ref):
        octants = ref[0]
        product = lax.dot_general(
            octants,
            weight_ref[...].reshape(taps * fine_channels, channels),
            (((1,), (1,)), ((), ())),
            preferred_element_type=F32,
        ).astype(BF16)
        wide = []
        for place in range(fine):
            for tap in range(taps):
                grad_ref[place, tap * cells : (tap + 1) * cells, :] = product[
                    place * cells : (place + 1) * cells,
                    tap * fine_channels : (tap + 1) * fine_channels,
                ]
            wide.append(
                jnp.concatenate(
                    [act_ref[place, tap * cells : (tap + 1) * cells, :] for tap in range(taps)],
                    axis=1,
                )
            )
        acc_ref[...] += jnp.dot(
            octants.T, jnp.concatenate(wide, axis=0), preferred_element_type=F32
        )

    for row, ref in enumerate((upper_ref, stay_ref, lower_ref)):
        pl.when(step // groups == row)(functools.partial(work, ref))

    @pl.when(step == pl.num_programs(0) - 1)
    def _():
        total = acc_ref[...].T
        first = lax.rem(lax.axis_index("dom"), 2) == 0
        lanes = channels // 2
        shards = keep_ref.shape[0]
        rows = total.shape[0] // shards
        left = total[:, :lanes].reshape(shards, rows, lanes)
        right = total[:, lanes:].reshape(shards, rows, lanes)
        keep_ref[:, :rows, :] = jnp.where(first, left, right).astype(BF16)
        send_ref[:, :rows, :] = jnp.where(first, right, left).astype(BF16)


def fine_gradient(shards, count, from_upper, stay, from_lower, weight, fine_act):
    fine, voxels, fine_channels = fine_act.shape
    groups, _, channels = stay.shape
    taps = weight.shape[0]
    whole = pl.BlockSpec((1, voxels, channels), lambda i: (i % groups, 0, 0))
    rows = count * piece_rows(taps * fine_channels // shards, count)
    down = jax.ShapeDtypeStruct((shards, rows, channels // 2), BF16)
    same = pl.BlockSpec(down.shape, lambda i: (0, 0, 0))
    block = pl.BlockSpec((8, voxels, fine_channels), lambda i: (i, 0, 0))
    return pl.pallas_call(
        functools.partial(fine_kernel, groups),
        grid=(3 * groups,),
        out_shape=(jax.ShapeDtypeStruct(fine_act.shape, BF16), down, down),
        in_specs=[
            whole, whole, whole,
            pl.BlockSpec(weight.shape, lambda i: (0, 0, 0)),
            block,
        ],
        out_specs=(block, same, same),
        scratch_shapes=[pltpu.VMEM((channels, taps * fine_channels), F32)],
        compiler_params=params(61),
        cost_estimate=pl.CostEstimate(
            flops=64 * fine * voxels * fine_channels * channels, bytes_accessed=8 * MIB,
            transcendentals=0,
        ),
        name="fine_gradient",
    )(from_upper, stay, from_lower, weight, fine_act)


def piece_rows(rows, count):
    return -(-rows // (16 * count)) * 16


def tree(values):
    while len(values) > 1:
        values = [
            values[i] + values[i + 1] if i + 1 < len(values) else values[i]
            for i in range(0, len(values), 2)
        ]
    return values[0]


def cost(*arrays):
    moved = sum(math.prod(x.shape) * jnp.dtype(x.dtype).itemsize for x in arrays)
    return pl.CostEstimate(flops=moved, bytes_accessed=moved, transcendentals=0)


def shapes_of(count, shape):
    return [jax.ShapeDtypeStruct(shape, F32 if step == 0 else BF16) for step in range(count)]


def pair_kernel(count, conv_ref, conv_got_ref, down_ref, down_got_ref, *outs):
    planes, slabs = outs[:count], outs[count:]
    shards, rows, _ = conv_ref.shape
    down_piece = down_ref.shape[1] // count
    piece = planes[0].shape[1] - down_piece
    cut = count * piece
    for step, ref in enumerate(slabs):
        shard = relative(lax.axis_index("dp"), step, shards)
        total = conv_ref[shard, cut:, :].astype(F32) + conv_got_ref[shard, cut:, :].astype(F32)
        ref[...] = total.astype(ref.dtype)
    high = lax.axis_index("dom") // 2
    for step, ref in enumerate(planes):
        place = relative(high, step, count)
        for keep_ref, got_ref, size, start in (
            (conv_ref, conv_got_ref, piece, 0),
            (down_ref, down_got_ref, down_piece, piece),
        ):
            span = pl.ds(pl.multiple_of(place * size, 16), size)
            total = keep_ref[:, span, :].astype(F32) + got_ref[:, span, :].astype(F32)
            ref[:, start : start + size, :] = total.astype(ref.dtype)


def pair_sum(count, conv, conv_got, down, down_got):
    shards, rows, lanes = conv.shape
    down_piece = down.shape[1] // count
    unit = 16 * count
    piece = 16 * round((2 * (rows + down.shape[1]) / 3 - down.shape[1]) / unit)
    outs = shapes_of(count, (shards, piece + down_piece, lanes))
    outs += shapes_of(shards, (rows - count * piece, lanes))
    outs = pl.pallas_call(
        functools.partial(pair_kernel, count),
        out_shape=outs,
        in_specs=[VMEM] * 4,
        out_specs=[VMEM] * len(outs),
        compiler_params=params(32),
        cost_estimate=cost(conv, conv_got, *outs),
        name="pair_sum",
    )(conv, conv_got, down, down_got)
    return outs[:count], outs[count:], (piece, down_piece)


def middle_kernel(count, shards, *refs):
    planes, slabs = refs[:count], refs[count : count + shards]
    to_slabs, mine_ref = refs[count + shards : -1], refs[-1]
    mine_ref[...] = tree([part[...].astype(F32) for part in slabs]).astype(BF16)
    for step, ref in enumerate(to_slabs):
        shard = relative(lax.axis_index("dp"), step, shards)
        ref[...] = tree([part[shard].astype(F32) for part in planes]).astype(ref.dtype)


def middle_sum(planes, slabs):
    count, shards = len(planes), len(slabs)
    _, piece, lanes = planes[0].shape
    outs = shapes_of(shards, (piece, lanes)) + [jax.ShapeDtypeStruct(slabs[0].shape, BF16)]
    parts = [*planes, *slabs]
    outs = pl.pallas_call(
        functools.partial(middle_kernel, count, shards),
        out_shape=outs,
        in_specs=[VMEM] * len(parts),
        out_specs=[VMEM] * len(outs),
        compiler_params=params(32),
        cost_estimate=cost(*parts, *outs),
        name="middle_sum",
    )(*parts)
    return outs[:shards], outs[shards]


def last_kernel(factor, shards, *refs):
    planes_ref, slabs_ref = refs[-2:]
    total = tree([part[...].astype(F32) for part in refs[:shards]])
    planes_ref[...] = (total * factor).astype(BF16)
    total = tree([part[...].astype(F32) for part in refs[shards:-2]])
    slabs_ref[...] = (total * factor).astype(BF16)


def last_sum(factor, slabs, planes):
    parts = [*slabs, *planes]
    return pl.pallas_call(
        functools.partial(last_kernel, factor, len(slabs)),
        out_shape=[
            jax.ShapeDtypeStruct(slabs[0].shape, BF16), jax.ShapeDtypeStruct(planes[0].shape, BF16)
        ],
        in_specs=[VMEM] * len(parts),
        out_specs=[VMEM] * 2,
        compiler_params=params(32),
        cost_estimate=cost(*parts),
        name="last_sum",
    )(*parts)


def gather_kernel(count, piece, down_piece, *refs):
    near, far = refs[:count], refs[count : 2 * count]
    rest_ref, rest_far_ref, conv_ref, down_ref, conv_whole, down_whole = refs[2 * count :]
    lanes = rest_ref.shape[1]
    cut = count * piece
    high = lax.axis_index("dom") // 2
    low = lax.rem(lax.axis_index("dom"), 2)
    for side, group, rest in ((low, near, rest_ref), (1 - low, far, rest_far_ref)):
        lane = pl.ds(pl.multiple_of(side * lanes, lanes), lanes)
        for step, ref in enumerate(group):
            place = source_of(high, step, count)
            row = pl.multiple_of(place * piece, 16)
            conv_whole[pl.ds(row, piece), lane] = ref[:piece, :].astype(F32)
            row = pl.multiple_of(place * down_piece, 16)
            down_whole[pl.ds(row, down_piece), lane] = ref[piece:, :].astype(F32)
        conv_whole[cut:, lane] = rest[...].astype(F32)
    conv_ref[...] = conv_whole[...]
    down_ref[...] = down_whole[: down_ref.shape[0]]


def gather_up(conv_rows, down_rows, pieces, near, far, rest, rest_far):
    count = len(near)
    lanes = rest.shape[1]
    outs = [jax.ShapeDtypeStruct((rows, 2 * lanes), F32) for rows in (conv_rows, down_rows)]
    return pl.pallas_call(
        functools.partial(gather_kernel, count, *pieces),
        out_shape=outs,
        in_specs=[VMEM] * (2 * count + 2),
        out_specs=[VMEM] * 2,
        scratch_shapes=[
            pltpu.VMEM((conv_rows, 2 * lanes), F32),
            pltpu.VMEM((count * pieces[1], 2 * lanes), F32),
        ],
        compiler_params=params(32),
        cost_estimate=cost(*near, *far, *outs),
        name="gather_up",
    )(*near, *far, rest, rest_far)


def body(grad_out, pre_act, conv_weight, down_weight, fine_act, neighbours, octant_routes):
    own = grad_out[0]
    places = octant_routes.shape[-1]
    table = jnp.concatenate([neighbours.reshape(-1), octant_routes.reshape(-1)])
    slots, voxels, channels = own.shape
    devices = lax.axis_size("dom")
    shards = lax.axis_size("dp")
    count = devices // 2
    factor = 1.0 / math.sqrt(shards * devices * slots * voxels)

    forward = [(i, i + 1) for i in range(devices - 1)]
    backward = [(i + 1, i) for i in range(devices - 1)]
    ring = [(i, (i + 1) % devices) for i in range(devices)]
    swap = [(i, i ^ 1) for i in range(devices)]

    def spread_out(parts, axis, stride):
        return [parts[0]] + [
            exchange(parts[step], axis, step, stride) for step in range(1, len(parts))
        ]

    low = lax.ppermute(own[:, voxels - PLANE :], "dom", forward)
    high = lax.ppermute(own[:, :PLANE], "dom", backward)
    to_lower, stay, to_upper = input_gradient(
        table, places, grad_out, low, high, pre_act, conv_weight
    )
    from_upper = lax.ppermute(to_lower, "dom", [(b, a) for a, b in ring])
    from_lower = lax.ppermute(to_upper, "dom", ring)
    conv_keep, conv_send = filter_gradient(shards, table, grad_out, low, high, pre_act)
    fine_grad, down_keep, down_send = fine_gradient(
        shards, count, from_upper, stay, from_lower, down_weight, fine_act[0]
    )
    conv_got = lax.ppermute(conv_send, "dom", swap)
    down_got = lax.ppermute(down_send, "dom", swap)

    planes, slabs, pieces = pair_sum(count, conv_keep, conv_got, down_keep, down_got)
    slabs = spread_out(slabs, "dp", 1)
    planes = spread_out(planes, "dom", 2)
    to_slabs, rest = middle_sum(planes, slabs)
    to_slabs = spread_out(to_slabs, "dp", 1)
    mine, rest = last_sum(factor, to_slabs, spread_out([rest] * count, "dom", 2))
    near = spread_out([mine] * count, "dom", 2)
    far = [lax.ppermute(value, "dom", swap) for value in near]
    rest_far = lax.ppermute(rest, "dom", swap)
    conv_rows = 27 * channels // shards
    down_rows = down_weight.shape[0] * down_weight.shape[1] // shards
    conv_grad, down_grad = gather_up(conv_rows, down_rows, pieces, near, far, rest, rest_far)
    return (fine_grad[None], conv_grad, down_grad)


def solution(mesh):
    return jax.shard_map(
        body,
        mesh=mesh,
        in_specs=(
            P("dp", "dom", None, None),
            P("dp", "dom", None, None),
            P(),
            P(),
            P("dp", "dom", None, None),
            P("dp", "dom", None),
            P("dp", "dom", None, None),
        ),
        out_specs=(P("dp", "dom", None, None), P("dp", None), P("dp", None)),
        check_vma=False,
    )
```

```python
import functools
import math

import jax
import jax.numpy as jnp
from jax import lax
from jax.experimental import pallas as pl
from jax.experimental.pallas import tpu as pltpu
from jax.sharding import PartitionSpec as P

BE = 8
PLANE = BE * BE
HALF = BE // 2
F32 = jnp.float32
BF16 = jnp.bfloat16
MIB = 1 << 20

VMEM = pl.BlockSpec(memory_space=pltpu.VMEM)
SMEM = pl.BlockSpec(memory_space=pltpu.SMEM)
ANY = pl.BlockSpec(memory_space=pl.ANY)
HBM = pl.BlockSpec(memory_space=pltpu.HBM)


def params(mib):
    return pltpu.CompilerParams(vmem_limit_bytes=int(mib * MIB))


def relative(index, step, count):
    if count & (count - 1) == 0:
        return index ^ step
    return lax.rem(index + step, count)


def source_of(index, step, count):
    if count & (count - 1) == 0:
        return index ^ step
    return (index - step) % count if isinstance(index, int) else lax.rem(index + count - step, count)


def exchange(value, axis, step, stride):
    count = lax.axis_size(axis) // stride
    pairs = []
    for index in range(lax.axis_size(axis)):
        high, low = divmod(index, stride)
        other = high ^ step if count & (count - 1) == 0 else (high + step) % count
        pairs.append((index, other * stride + low))
    return lax.ppermute(value, axis, pairs)


def started(source, target, sem):
    copy = pltpu.make_async_copy(source, target, sem)
    copy.start()
    return copy


GROUPS = (0, -1, 1)


def column_of(tap):
    _, rest = divmod(tap, 9)
    tap_y, tap_z = rest // 3 - 1, rest % 3 - 1
    return 3 * GROUPS.index(-tap_z) + tap_y + 1


def extend(ref, wide_ref):
    slots = ref.shape[0]
    wide_ref[:slots] = ref[...]
    wide_ref[slots] = jnp.zeros(ref.shape[1:], ref.dtype)


def spread(links_ref, ref, start, step_x, slot, row, shift, win_ref):
    channels = ref.shape[-1]
    empty = ref.shape[0] - 1

    def fetch(step_y, step_z, first, rows):
        found = links_ref[slot, 9 * (step_x + 1) + 3 * (step_y + 1) + step_z + 1]
        place = jnp.where(found < 0, empty, found)
        return ref[place, start + first : start + first + rows, :].astype(F32)

    def column(step_z):
        below = fetch(-1, step_z, PLANE - 16, 16).reshape(2, BE, channels)[1:]
        middle = fetch(0, step_z, 0, PLANE).reshape(BE, BE, channels)
        above = fetch(1, step_z, 0, 16).reshape(2, BE, channels)[:1]
        return jnp.concatenate([below, middle, above], axis=0)

    value = column(0)
    if shift != 0:
        turn = 1 if shift < 0 else BE - 1
        edge = 0 if shift < 0 else BE - 1
        place_z = lax.broadcasted_iota(jnp.int32, value.shape, 1)
        value = jnp.where(
            place_z == edge,
            pltpu.roll(column(shift), turn, axis=1),
            pltpu.roll(value, turn, axis=1),
        )
    for tap_y in (-1, 0, 1):
        lane = (3 * GROUPS.index(shift) + tap_y + 1) * channels
        part = value[1 - tap_y : 1 - tap_y + BE].reshape(PLANE, channels)
        win_ref[row : row + PLANE, lane : lane + channels] = part.astype(BF16)


def builders(links_ref, own_ref, low_ref, high_ref, win_ref, shift):
    slots = own_ref.shape[0] - 1
    calls = []
    for plane in range(BE + 2):
        if plane == 0:
            ref, start, step_x = low_ref, 0, -1
        elif plane == BE + 1:
            ref, start, step_x = high_ref, 0, 1
        else:
            ref, start, step_x = own_ref, (plane - 1) * PLANE, 0
        for slot in range(slots):
            row = (plane * slots + slot) * PLANE
            calls.append(
                functools.partial(
                    spread, links_ref, ref, start, step_x, slot, row, shift, win_ref
                )
            )
    return calls


def interleave(first, second):
    done = 0
    for index, call in enumerate(first):
        call()
        until = len(second) * (index + 1) // len(first)
        for other in second[done:until]:
            other()
        done = until


def input_kernel(
    links_ref, routes_ref, own_ref, low_ref, high_ref, pre_ref, weight_ref,
    to_lower_ref, stay_ref, to_upper_ref,
    own_wide, low_wide, high_wide, win_ref, taps_ref, acc_ref, octants_ref, tap_sems, out_sems,
):
    slots, voxels, channels = own_ref.shape
    groups = routes_ref.shape[1] // 8
    copies = []
    for tap in range(27):
        column = column_of(tap)
        lanes = slice(column * channels, (column + 1) * channels)
        copies.append(
            started(weight_ref.at[tap], taps_ref.at[tap // 9, :, lanes], tap_sems.at[tap])
        )
    for ref, wide in ((own_ref, own_wide), (low_ref, low_wide), (high_ref, high_wide)):
        extend(ref, wide)
    slab = slots * PLANE
    rows = BE * slab
    part = rows // 2

    def product(group, start):
        lanes = slice(3 * group * channels, 3 * (group + 1) * channels)
        total = None
        for index_x in range(3):
            offset = start + (2 - index_x) * slab
            term = lax.dot_general(
                win_ref[offset : offset + part, lanes],
                taps_ref[index_x, :, lanes],
                (((1,), (1,)), ((), ())),
                preferred_element_type=F32,
            )
            total = term if total is None else total + term
        if group > 0:
            total = total + acc_ref[start : start + part, :]
        acc_ref[start : start + part, :] = total

    def products(group):
        return [functools.partial(product, group, start) for start in range(0, rows, part)]

    sources = (links_ref, own_wide, low_wide, high_wide, win_ref)
    for call in builders(*sources, GROUPS[0]):
        call()
    for copy in copies:
        copy.wait()
    interleave(products(0), builders(*sources, GROUPS[1]))
    interleave(products(1), builders(*sources, GROUPS[2]))
    for call in products(2):
        call()

    octants_ref[...] = jnp.zeros_like(octants_ref)
    place_z = lax.broadcasted_iota(jnp.int32, (BE // 2, BE, channels), 1)
    for slot in range(slots):
        group = jnp.int32(3 * groups)
        for row in range(3):
            for place in range(groups):
                group = jnp.where(
                    routes_ref[row, 8 * place] == 8 * slot, row * groups + place, group
                )

        def finish(x, carry):
            value = acc_ref[pl.ds(pl.multiple_of(x * slab + slot * PLANE, PLANE), PLANE), :]
            pre = pre_ref[slot, pl.ds(pl.multiple_of(x * PLANE, PLANE), PLANE), :].astype(F32)
            value = jnp.where(pre > 0, value, 0.0).reshape(BE // 2, 2, BE, channels)
            even, odd = value[:, 0], value[:, 1]
            near = jnp.where(place_z < HALF, even, pltpu.roll(odd, HALF, axis=1))
            far = jnp.where(place_z < HALF, pltpu.roll(even, HALF, axis=1), odd)
            side = x // HALF
            row = (x - side * HALF) * 16
            for side_y in range(2):
                for side_z, piece in enumerate((near, far)):
                    block = piece[2 * side_y : 2 * side_y + 2].reshape(16, channels).astype(BF16)
                    start = (4 * side + 2 * side_y + side_z) * PLANE + row
                    octants_ref[group, pl.ds(pl.multiple_of(start, 16), 16), :] = block
            return carry

        lax.fori_loop(0, BE, finish, 0)
    outs = []
    for row, ref in enumerate((to_lower_ref, stay_ref, to_upper_ref)):
        outs.append(started(octants_ref.at[pl.ds(row * groups, groups)], ref, out_sems.at[row]))
    for copy in outs:
        copy.wait()


def wide_scratch(own, low):
    slots, voxels, channels = own.shape
    return [
        pltpu.VMEM((slots + 1, voxels, channels), BF16),
        pltpu.VMEM((slots + 1, low.shape[1], channels), BF16),
        pltpu.VMEM((slots + 1, low.shape[1], channels), BF16),
        pltpu.VMEM((slots * PLANE * (BE + 2), 9 * channels), BF16),
    ]


def input_gradient(links, routes, own, low, high, pre, weight):
    slots, voxels, channels = own.shape
    groups = routes.shape[1] // 8
    rows = slots * voxels
    out = jax.ShapeDtypeStruct((groups, voxels, channels), BF16)
    return pl.pallas_call(
        input_kernel,
        out_shape=(out, out, out),
        in_specs=[SMEM, SMEM, VMEM, VMEM, VMEM, VMEM, ANY],
        out_specs=(ANY, ANY, ANY),
        scratch_shapes=wide_scratch(own, low)
        + [
            pltpu.VMEM((3, channels, 9 * channels), BF16),
            pltpu.VMEM((rows, channels), F32),
            pltpu.VMEM((3 * groups + 1, voxels, channels), BF16),
            pltpu.SemaphoreType.DMA((27,)),
            pltpu.SemaphoreType.DMA((3,)),
        ],
        compiler_params=params(40),
        cost_estimate=pl.CostEstimate(
            flops=2 * rows * 27 * channels * channels, bytes_accessed=8 * MIB, transcendentals=0
        ),
        name="input_gradient",
    )(links, routes, own, low, high, pre, weight)


def filter_kernel(
    shard_rows, links_ref, own_ref, low_ref, high_ref, pre_ref,
    keep_ref, send_ref, own_wide, low_wide, high_wide, win_ref, act_ref,
):
    slots, voxels, channels = own_ref.shape
    slab = slots * PLANE
    rows = BE * slab
    lanes = channels // 2
    for ref, wide in ((own_ref, own_wide), (low_ref, low_wide), (high_ref, high_wide)):
        extend(ref, wide)

    def transpose(pair):
        parts = []
        for x in (2 * pair, 2 * pair + 1):
            for slot in range(slots):
                parts.append(pre_ref[slot, x * PLANE : (x + 1) * PLANE, :])
        block = jnp.maximum(jnp.concatenate(parts, axis=0).astype(F32), 0.0)
        act_ref[:, pair * 2 * slab : (pair + 1) * 2 * slab] = block.T.astype(BF16)

    first = lax.rem(lax.axis_index("dom"), 2) == 0
    unit = math.gcd(channels, shard_rows)

    def product(tap):
        offset = (2 - tap // 9) * slab
        column = column_of(tap) * channels
        total = jnp.dot(
            act_ref[...],
            win_ref[offset : offset + rows, column : column + channels],
            preferred_element_type=F32,
        )
        left, right = total[:, :lanes], total[:, lanes:]
        keep = jnp.where(first, left, right).astype(BF16)
        send = jnp.where(first, right, left).astype(BF16)
        for part in range(channels // unit):
            shard, start = divmod(tap * channels + part * unit, shard_rows)
            span = slice(part * unit, (part + 1) * unit)
            keep_ref[shard, start : start + unit, :] = keep[span]
            send_ref[shard, start : start + unit, :] = send[span]

    def products(group):
        taps = [tap for tap in range(27) if column_of(tap) // 3 == group]
        return [functools.partial(product, tap) for tap in taps]

    sources = (links_ref, own_wide, low_wide, high_wide, win_ref)
    turns = [functools.partial(transpose, pair) for pair in range(BE // 2)]
    interleave(turns, builders(*sources, GROUPS[0]))
    interleave(products(0), builders(*sources, GROUPS[1]))
    interleave(products(1), builders(*sources, GROUPS[2]))
    for call in products(2):
        call()


def filter_gradient(shards, links, own, low, high, pre):
    slots, voxels, channels = own.shape
    shard_rows = 27 * channels // shards
    rows = slots * voxels
    out = jax.ShapeDtypeStruct((shards, shard_rows, channels // 2), BF16)
    return pl.pallas_call(
        functools.partial(filter_kernel, shard_rows),
        out_shape=(out, out),
        in_specs=[SMEM, VMEM, VMEM, VMEM, VMEM],
        out_specs=(VMEM, VMEM),
        scratch_shapes=wide_scratch(own, low) + [pltpu.VMEM((channels, rows), BF16)],
        compiler_params=params(40),
        cost_estimate=pl.CostEstimate(
            flops=2 * rows * 27 * channels * channels, bytes_accessed=8 * MIB, transcendentals=0
        ),
        name="filter_gradient",
    )(links, own, low, high, pre)


def fine_kernel(
    groups, upper_ref, stay_ref, lower_ref, weight_ref, act_ref,
    grad_ref, keep_ref, send_ref, acc_ref,
):
    step = pl.program_id(0)
    fine, voxels, fine_channels = act_ref.shape
    channels = upper_ref.shape[-1]
    taps = weight_ref.shape[0]
    cells = voxels // taps

    @pl.when(step == 0)
    def _():
        acc_ref[...] = jnp.zeros_like(acc_ref)

    def work(ref):
        octants = ref[0]
        product = lax.dot_general(
            octants,
            weight_ref[...].reshape(taps * fine_channels, channels),
            (((1,), (1,)), ((), ())),
            preferred_element_type=F32,
        ).astype(BF16)
        wide = []
        for place in range(fine):
            for tap in range(taps):
                grad_ref[place, tap * cells : (tap + 1) * cells, :] = product[
                    place * cells : (place + 1) * cells,
                    tap * fine_channels : (tap + 1) * fine_channels,
                ]
            wide.append(
                jnp.concatenate(
                    [act_ref[place, tap * cells : (tap + 1) * cells, :] for tap in range(taps)],
                    axis=1,
                )
            )
        acc_ref[...] += jnp.dot(
            octants.T, jnp.concatenate(wide, axis=0), preferred_element_type=F32
        )

    for row, ref in enumerate((upper_ref, stay_ref, lower_ref)):
        pl.when(step // groups == row)(functools.partial(work, ref))

    @pl.when(step == pl.num_programs(0) - 1)
    def _():
        total = acc_ref[...].T
        first = lax.rem(lax.axis_index("dom"), 2) == 0
        lanes = channels // 2
        shards = keep_ref.shape[0]
        rows = total.shape[0] // shards
        left = total[:, :lanes].reshape(shards, rows, lanes)
        right = total[:, lanes:].reshape(shards, rows, lanes)
        keep_ref[:, :rows, :] = jnp.where(first, left, right).astype(BF16)
        send_ref[:, :rows, :] = jnp.where(first, right, left).astype(BF16)


def fine_gradient(shards, count, from_upper, stay, from_lower, weight, fine_act):
    fine, voxels, fine_channels = fine_act.shape
    groups, _, channels = stay.shape
    taps = weight.shape[0]
    whole = pl.BlockSpec((1, voxels, channels), lambda i: (i % groups, 0, 0))
    rows = count * piece_rows(taps * fine_channels // shards, count)
    down = jax.ShapeDtypeStruct((shards, rows, channels // 2), BF16)
    same = pl.BlockSpec(down.shape, lambda i: (0, 0, 0))
    block = pl.BlockSpec((8, voxels, fine_channels), lambda i: (i, 0, 0))
    return pl.pallas_call(
        functools.partial(fine_kernel, groups),
        grid=(3 * groups,),
        out_shape=(jax.ShapeDtypeStruct(fine_act.shape, BF16), down, down),
        in_specs=[
            whole, whole, whole,
            pl.BlockSpec(weight.shape, lambda i: (0, 0, 0)),
            block,
        ],
        out_specs=(block, same, same),
        scratch_shapes=[pltpu.VMEM((channels, taps * fine_channels), F32)],
        compiler_params=params(40),
        cost_estimate=pl.CostEstimate(
            flops=64 * fine * voxels * fine_channels * channels, bytes_accessed=8 * MIB,
            transcendentals=0,
        ),
        name="fine_gradient",
    )(from_upper, stay, from_lower, weight, fine_act)


def piece_rows(rows, count):
    return -(-rows // (16 * count)) * 16


def tree(values):
    while len(values) > 1:
        values = [
            values[i] + values[i + 1] if i + 1 < len(values) else values[i]
            for i in range(0, len(values), 2)
        ]
    return values[0]


def cost(*arrays):
    moved = sum(math.prod(x.shape) * jnp.dtype(x.dtype).itemsize for x in arrays)
    return pl.CostEstimate(flops=moved, bytes_accessed=moved, transcendentals=0)


def shapes_of(count, shape):
    return [jax.ShapeDtypeStruct(shape, F32 if step == 0 else BF16) for step in range(count)]


def pair_kernel(count, conv_ref, conv_got_ref, down_ref, down_got_ref, *outs):
    planes, slabs = outs[:count], outs[count:]
    shards, rows, _ = conv_ref.shape
    down_piece = down_ref.shape[1] // count
    piece = planes[0].shape[1] - down_piece
    cut = count * piece
    for step, ref in enumerate(slabs):
        shard = relative(lax.axis_index("dp"), step, shards)
        total = conv_ref[shard, cut:, :].astype(F32) + conv_got_ref[shard, cut:, :].astype(F32)
        ref[...] = total.astype(ref.dtype)
    high = lax.axis_index("dom") // 2
    for step, ref in enumerate(planes):
        place = relative(high, step, count)
        for keep_ref, got_ref, size, start in (
            (conv_ref, conv_got_ref, piece, 0),
            (down_ref, down_got_ref, down_piece, piece),
        ):
            span = pl.ds(pl.multiple_of(place * size, 16), size)
            total = keep_ref[:, span, :].astype(F32) + got_ref[:, span, :].astype(F32)
            ref[:, start : start + size, :] = total.astype(ref.dtype)


def pair_sum(count, conv, conv_got, down, down_got):
    shards, rows, lanes = conv.shape
    down_piece = down.shape[1] // count
    unit = 16 * count
    piece = 16 * round((2 * (rows + down.shape[1]) / 3 - down.shape[1]) / unit)
    outs = shapes_of(count, (shards, piece + down_piece, lanes))
    outs += shapes_of(shards, (rows - count * piece, lanes))
    outs = pl.pallas_call(
        functools.partial(pair_kernel, count),
        out_shape=outs,
        in_specs=[VMEM] * 4,
        out_specs=[VMEM] * len(outs),
        compiler_params=params(32),
        cost_estimate=cost(conv, conv_got, *outs),
        name="pair_sum",
    )(conv, conv_got, down, down_got)
    return outs[:count], outs[count:], (piece, down_piece)


def middle_kernel(count, shards, *refs):
    planes, slabs = refs[:count], refs[count : count + shards]
    to_slabs, mine_ref = refs[count + shards : -1], refs[-1]
    mine_ref[...] = tree([part[...].astype(F32) for part in slabs]).astype(BF16)
    for step, ref in enumerate(to_slabs):
        shard = relative(lax.axis_index("dp"), step, shards)
        ref[...] = tree([part[shard].astype(F32) for part in planes]).astype(ref.dtype)


def middle_sum(planes, slabs):
    count, shards = len(planes), len(slabs)
    _, piece, lanes = planes[0].shape
    outs = shapes_of(shards, (piece, lanes)) + [jax.ShapeDtypeStruct(slabs[0].shape, BF16)]
    parts = [*planes, *slabs]
    outs = pl.pallas_call(
        functools.partial(middle_kernel, count, shards),
        out_shape=outs,
        in_specs=[VMEM] * len(parts),
        out_specs=[VMEM] * len(outs),
        compiler_params=params(32),
        cost_estimate=cost(*parts, *outs),
        name="middle_sum",
    )(*parts)
    return outs[:shards], outs[shards]


def last_kernel(factor, shards, *refs):
    planes_ref, slabs_ref = refs[-2:]
    total = tree([part[...].astype(F32) for part in refs[:shards]])
    planes_ref[...] = (total * factor).astype(BF16)
    total = tree([part[...].astype(F32) for part in refs[shards:-2]])
    slabs_ref[...] = (total * factor).astype(BF16)


def last_sum(factor, slabs, planes):
    parts = [*slabs, *planes]
    return pl.pallas_call(
        functools.partial(last_kernel, factor, len(slabs)),
        out_shape=[
            jax.ShapeDtypeStruct(slabs[0].shape, BF16), jax.ShapeDtypeStruct(planes[0].shape, BF16)
        ],
        in_specs=[VMEM] * len(parts),
        out_specs=[VMEM] * 2,
        compiler_params=params(32),
        cost_estimate=cost(*parts),
        name="last_sum",
    )(*parts)


def gather_kernel(count, piece, down_piece, *refs):
    near, far = refs[:count], refs[count : 2 * count]
    rest_ref, rest_far_ref, conv_ref, down_ref, conv_whole, down_whole = refs[2 * count :]
    lanes = rest_ref.shape[1]
    cut = count * piece
    high = lax.axis_index("dom") // 2
    low = lax.rem(lax.axis_index("dom"), 2)
    for side, group, rest in ((low, near, rest_ref), (1 - low, far, rest_far_ref)):
        lane = pl.ds(pl.multiple_of(side * lanes, lanes), lanes)
        for step, ref in enumerate(group):
            place = source_of(high, step, count)
            row = pl.multiple_of(place * piece, 16)
            conv_whole[pl.ds(row, piece), lane] = ref[:piece, :].astype(F32)
            row = pl.multiple_of(place * down_piece, 16)
            down_whole[pl.ds(row, down_piece), lane] = ref[piece:, :].astype(F32)
        conv_whole[cut:, lane] = rest[...].astype(F32)
    conv_ref[...] = conv_whole[...]
    down_ref[...] = down_whole[: down_ref.shape[0]]


def gather_up(conv_rows, down_rows, pieces, near, far, rest, rest_far):
    count = len(near)
    lanes = rest.shape[1]
    outs = [jax.ShapeDtypeStruct((rows, 2 * lanes), F32) for rows in (conv_rows, down_rows)]
    return pl.pallas_call(
        functools.partial(gather_kernel, count, *pieces),
        out_shape=outs,
        in_specs=[VMEM] * (2 * count + 2),
        out_specs=[VMEM] * 2,
        scratch_shapes=[
            pltpu.VMEM((conv_rows, 2 * lanes), F32),
            pltpu.VMEM((count * pieces[1], 2 * lanes), F32),
        ],
        compiler_params=params(32),
        cost_estimate=cost(*near, *far, *outs),
        name="gather_up",
    )(*near, *far, rest, rest_far)


def body(grad_out, pre_act, conv_weight, down_weight, fine_act, neighbours, octant_routes):
    own = grad_out[0]
    pre = pre_act[0]
    links = neighbours[0]
    routes = octant_routes[0, 0]
    slots, voxels, channels = own.shape
    devices = lax.axis_size("dom")
    shards = lax.axis_size("dp")
    count = devices // 2
    factor = 1.0 / math.sqrt(shards * devices * slots * voxels)

    forward = [(i, i + 1) for i in range(devices - 1)]
    backward = [(i + 1, i) for i in range(devices - 1)]
    ring = [(i, (i + 1) % devices) for i in range(devices)]
    swap = [(i, i ^ 1) for i in range(devices)]

    def spread_out(parts, axis, stride):
        return [parts[0]] + [
            exchange(parts[step], axis, step, stride) for step in range(1, len(parts))
        ]

    low = lax.ppermute(own[:, voxels - PLANE :], "dom", forward)
    high = lax.ppermute(own[:, :PLANE], "dom", backward)
    to_lower, stay, to_upper = input_gradient(
        links, routes, own, low, high, pre, conv_weight
    )
    from_upper = lax.ppermute(to_lower, "dom", [(b, a) for a, b in ring])
    from_lower = lax.ppermute(to_upper, "dom", ring)
    conv_keep, conv_send = filter_gradient(shards, links, own, low, high, pre)
    fine_grad, down_keep, down_send = fine_gradient(
        shards, count, from_upper, stay, from_lower, down_weight, fine_act[0]
    )
    conv_got = lax.ppermute(conv_send, "dom", swap)
    down_got = lax.ppermute(down_send, "dom", swap)

    planes, slabs, pieces = pair_sum(count, conv_keep, conv_got, down_keep, down_got)
    slabs = spread_out(slabs, "dp", 1)
    planes = spread_out(planes, "dom", 2)
    to_slabs, rest = middle_sum(planes, slabs)
    to_slabs = spread_out(to_slabs, "dp", 1)
    mine, rest = last_sum(factor, to_slabs, spread_out([rest] * count, "dom", 2))
    near = spread_out([mine] * count, "dom", 2)
    far = [lax.ppermute(value, "dom", swap) for value in near]
    rest_far = lax.ppermute(rest, "dom", swap)
    conv_rows = 27 * channels // shards
    down_rows = down_weight.shape[0] * down_weight.shape[1] // shards
    conv_grad, down_grad = gather_up(conv_rows, down_rows, pieces, near, far, rest, rest_far)
    return (fine_grad[None], conv_grad, down_grad)


def solution(mesh):
    return jax.shard_map(
        body,
        mesh=mesh,
        in_specs=(
            P("dp", "dom", None, None),
            P("dp", "dom", None, None),
            P(),
            P(),
            P("dp", "dom", None, None),
            P("dp", "dom", None),
            P("dp", "dom", None, None),
        ),
        out_specs=(P("dp", "dom", None, None), P("dp", None), P("dp", None)),
        check_vma=False,
    )
```

```python
import functools
import math

import jax
import jax.numpy as jnp
from jax import lax
from jax.experimental import pallas as pl
from jax.experimental.pallas import tpu as pltpu
from jax.sharding import PartitionSpec as P

BE = 8
PLANE = BE * BE
HALF = BE // 2
F32 = jnp.float32
BF16 = jnp.bfloat16
MIB = 1 << 20

VMEM = pl.BlockSpec(memory_space=pltpu.VMEM)
SMEM = pl.BlockSpec(memory_space=pltpu.SMEM)
ANY = pl.BlockSpec(memory_space=pl.ANY)
HBM = pl.BlockSpec(memory_space=pltpu.HBM)


def params(mib):
    return pltpu.CompilerParams(vmem_limit_bytes=int(mib * MIB))


def relative(index, step, count):
    if count & (count - 1) == 0:
        return index ^ step
    return lax.rem(index + step, count)


def source_of(index, step, count):
    if count & (count - 1) == 0:
        return index ^ step
    return (index - step) % count if isinstance(index, int) else lax.rem(index + count - step, count)


def partner(index, step, count):
    return index ^ step if count & (count - 1) == 0 else (index + step) % count


def started(source, target, sem):
    copy = pltpu.make_async_copy(source, target, sem)
    copy.start()
    return copy


GROUPS = (0, -1, 1)


def column_of(tap):
    _, rest = divmod(tap, 9)
    tap_y, tap_z = rest // 3 - 1, rest % 3 - 1
    return 3 * GROUPS.index(-tap_z) + tap_y + 1


def extend(ref, wide_ref):
    slots = ref.shape[0]
    wide_ref[:slots] = ref[...]
    wide_ref[slots] = jnp.zeros(ref.shape[1:], ref.dtype)


def spread(links_ref, ref, start, step_x, slot, row, shift, win_ref):
    channels = ref.shape[-1]
    empty = ref.shape[0] - 1

    def fetch(step_y, step_z, first, rows):
        found = links_ref[slot, 9 * (step_x + 1) + 3 * (step_y + 1) + step_z + 1]
        place = jnp.where(found < 0, empty, found)
        return ref[place, start + first : start + first + rows, :].astype(F32)

    def column(step_z):
        below = fetch(-1, step_z, PLANE - 16, 16).reshape(2, BE, channels)[1:]
        middle = fetch(0, step_z, 0, PLANE).reshape(BE, BE, channels)
        above = fetch(1, step_z, 0, 16).reshape(2, BE, channels)[:1]
        return jnp.concatenate([below, middle, above], axis=0)

    value = column(0)
    if shift != 0:
        turn = 1 if shift < 0 else BE - 1
        edge = 0 if shift < 0 else BE - 1
        place_z = lax.broadcasted_iota(jnp.int32, value.shape, 1)
        value = jnp.where(
            place_z == edge,
            pltpu.roll(column(shift), turn, axis=1),
            pltpu.roll(value, turn, axis=1),
        )
    for tap_y in (-1, 0, 1):
        lane = (3 * GROUPS.index(shift) + tap_y + 1) * channels
        part = value[1 - tap_y : 1 - tap_y + BE].reshape(PLANE, channels)
        win_ref[row : row + PLANE, lane : lane + channels] = part.astype(BF16)


def builders(links_ref, own_ref, low_ref, high_ref, win_ref, shift):
    slots = own_ref.shape[0] - 1
    calls = []
    for plane in range(BE + 2):
        if plane == 0:
            ref, start, step_x = low_ref, 0, -1
        elif plane == BE + 1:
            ref, start, step_x = high_ref, 0, 1
        else:
            ref, start, step_x = own_ref, (plane - 1) * PLANE, 0
        for slot in range(slots):
            row = (plane * slots + slot) * PLANE
            calls.append(
                functools.partial(
                    spread, links_ref, ref, start, step_x, slot, row, shift, win_ref
                )
            )
    return calls


def interleave(first, second):
    done = 0
    for index, call in enumerate(first):
        call()
        until = len(second) * (index + 1) // len(first)
        for other in second[done:until]:
            other()
        done = until


def input_kernel(
    links_ref, routes_ref, own_ref, low_ref, high_ref, pre_ref, weight_ref,
    to_lower_ref, stay_ref, to_upper_ref,
    own_wide, low_wide, high_wide, win_ref, taps_ref, acc_ref, octants_ref, tap_sems, out_sems,
):
    slots, voxels, channels = own_ref.shape
    groups = routes_ref.shape[1] // 8
    copies = []
    for tap in range(27):
        column = column_of(tap)
        lanes = slice(column * channels, (column + 1) * channels)
        copies.append(
            started(weight_ref.at[tap], taps_ref.at[tap // 9, :, lanes], tap_sems.at[tap])
        )
    for ref, wide in ((own_ref, own_wide), (low_ref, low_wide), (high_ref, high_wide)):
        extend(ref, wide)
    slab = slots * PLANE
    rows = BE * slab
    part = rows // 2

    def product(group, start):
        lanes = slice(3 * group * channels, 3 * (group + 1) * channels)
        total = None
        for index_x in range(3):
            offset = start + (2 - index_x) * slab
            term = lax.dot_general(
                win_ref[offset : offset + part, lanes],
                taps_ref[index_x, :, lanes],
                (((1,), (1,)), ((), ())),
                preferred_element_type=F32,
            )
            total = term if total is None else total + term
        if group > 0:
            total = total + acc_ref[start : start + part, :]
        acc_ref[start : start + part, :] = total

    def products(group):
        return [functools.partial(product, group, start) for start in range(0, rows, part)]

    sources = (links_ref, own_wide, low_wide, high_wide, win_ref)
    for call in builders(*sources, GROUPS[0]):
        call()
    for copy in copies:
        copy.wait()
    interleave(products(0), builders(*sources, GROUPS[1]))
    interleave(products(1), builders(*sources, GROUPS[2]))
    for call in products(2):
        call()

    octants_ref[...] = jnp.zeros_like(octants_ref)
    place_z = lax.broadcasted_iota(jnp.int32, (BE // 2, BE, channels), 1)
    for slot in range(slots):
        group = jnp.int32(3 * groups)
        for row in range(3):
            for place in range(groups):
                group = jnp.where(
                    routes_ref[row, 8 * place] == 8 * slot, row * groups + place, group
                )

        def finish(x, carry):
            value = acc_ref[pl.ds(pl.multiple_of(x * slab + slot * PLANE, PLANE), PLANE), :]
            pre = pre_ref[slot, pl.ds(pl.multiple_of(x * PLANE, PLANE), PLANE), :].astype(F32)
            value = jnp.where(pre > 0, value, 0.0).reshape(BE // 2, 2, BE, channels)
            even, odd = value[:, 0], value[:, 1]
            near = jnp.where(place_z < HALF, even, pltpu.roll(odd, HALF, axis=1))
            far = jnp.where(place_z < HALF, pltpu.roll(even, HALF, axis=1), odd)
            side = x // HALF
            row = (x - side * HALF) * 16
            for side_y in range(2):
                for side_z, piece in enumerate((near, far)):
                    block = piece[2 * side_y : 2 * side_y + 2].reshape(16, channels).astype(BF16)
                    start = (4 * side + 2 * side_y + side_z) * PLANE + row
                    octants_ref[group, pl.ds(pl.multiple_of(start, 16), 16), :] = block
            return carry

        lax.fori_loop(0, BE, finish, 0)
    outs = []
    for row, ref in enumerate((to_lower_ref, stay_ref, to_upper_ref)):
        outs.append(started(octants_ref.at[pl.ds(row * groups, groups)], ref, out_sems.at[row]))
    for copy in outs:
        copy.wait()


def wide_scratch(own, low):
    slots, voxels, channels = own.shape
    return [
        pltpu.VMEM((slots + 1, voxels, channels), BF16),
        pltpu.VMEM((slots + 1, low.shape[1], channels), BF16),
        pltpu.VMEM((slots + 1, low.shape[1], channels), BF16),
        pltpu.VMEM((slots * PLANE * (BE + 2), 9 * channels), BF16),
    ]


def input_gradient(links, routes, own, low, high, pre, weight):
    slots, voxels, channels = own.shape
    groups = routes.shape[1] // 8
    rows = slots * voxels
    out = jax.ShapeDtypeStruct((groups, voxels, channels), BF16)
    return pl.pallas_call(
        input_kernel,
        out_shape=(out, out, out),
        in_specs=[SMEM, SMEM, VMEM, VMEM, VMEM, VMEM, ANY],
        out_specs=(ANY, ANY, ANY),
        scratch_shapes=wide_scratch(own, low)
        + [
            pltpu.VMEM((3, channels, 9 * channels), BF16),
            pltpu.VMEM((rows, channels), F32),
            pltpu.VMEM((3 * groups + 1, voxels, channels), BF16),
            pltpu.SemaphoreType.DMA((27,)),
            pltpu.SemaphoreType.DMA((3,)),
        ],
        compiler_params=params(40),
        cost_estimate=pl.CostEstimate(
            flops=2 * rows * 27 * channels * channels, bytes_accessed=8 * MIB, transcendentals=0
        ),
        name="input_gradient",
    )(links, routes, own, low, high, pre, weight)


def filter_kernel(
    shard_rows, links_ref, own_ref, low_ref, high_ref, pre_ref,
    early_ref, late_ref, own_wide, low_wide, high_wide, win_ref, act_ref,
):
    slots, voxels, channels = own_ref.shape
    slab = slots * PLANE
    rows = BE * slab
    for ref, wide in ((own_ref, own_wide), (low_ref, low_wide), (high_ref, high_wide)):
        extend(ref, wide)

    def transpose(pair):
        parts = []
        for x in (2 * pair, 2 * pair + 1):
            for slot in range(slots):
                parts.append(pre_ref[slot, x * PLANE : (x + 1) * PLANE, :])
        block = jnp.maximum(jnp.concatenate(parts, axis=0).astype(F32), 0.0)
        act_ref[:, pair * 2 * slab : (pair + 1) * 2 * slab] = block.T.astype(BF16)

    unit = math.gcd(channels, shard_rows)
    cut = early_ref.shape[1]

    def product(tap):
        offset = (2 - tap // 9) * slab
        column = column_of(tap) * channels
        total = jnp.dot(
            act_ref[...],
            win_ref[offset : offset + rows, column : column + channels],
            preferred_element_type=F32,
        )
        total = total.astype(BF16)
        for part in range(channels // unit):
            shard, start = divmod(tap * channels + part * unit, shard_rows)
            ref = early_ref
            if start >= cut:
                ref, start = late_ref, start - cut
            ref[shard, start : start + unit, :] = total[part * unit : (part + 1) * unit]

    def products(group):
        taps = [tap for tap in range(27) if column_of(tap) // 3 == group]
        return [functools.partial(product, tap) for tap in taps]

    sources = (links_ref, own_wide, low_wide, high_wide, win_ref)
    turns = [functools.partial(transpose, pair) for pair in range(BE // 2)]
    interleave(turns, builders(*sources, GROUPS[0]))
    interleave(products(0), builders(*sources, GROUPS[1]))
    interleave(products(1), builders(*sources, GROUPS[2]))
    for call in products(2):
        call()


def filter_gradient(shards, cut, links, own, low, high, pre):
    slots, voxels, channels = own.shape
    shard_rows = 27 * channels // shards
    rows = slots * voxels
    early = jax.ShapeDtypeStruct((shards, cut, channels), BF16)
    late = jax.ShapeDtypeStruct((shards, shard_rows - cut, channels), BF16)
    return pl.pallas_call(
        functools.partial(filter_kernel, shard_rows),
        out_shape=(early, late),
        in_specs=[SMEM, VMEM, VMEM, VMEM, VMEM],
        out_specs=(VMEM, VMEM),
        scratch_shapes=wide_scratch(own, low) + [pltpu.VMEM((channels, rows), BF16)],
        compiler_params=params(40),
        cost_estimate=pl.CostEstimate(
            flops=2 * rows * 27 * channels * channels, bytes_accessed=8 * MIB, transcendentals=0
        ),
        name="filter_gradient",
    )(links, own, low, high, pre)


def fine_kernel(
    groups, upper_ref, stay_ref, lower_ref, weight_ref, act_ref,
    grad_ref, down_ref, acc_ref,
):
    step = pl.program_id(0)
    fine, voxels, fine_channels = act_ref.shape
    channels = upper_ref.shape[-1]
    taps = weight_ref.shape[0]
    cells = voxels // taps

    @pl.when(step == 0)
    def _():
        acc_ref[...] = jnp.zeros_like(acc_ref)

    def work(ref):
        octants = ref[0]
        product = lax.dot_general(
            octants,
            weight_ref[...].reshape(taps * fine_channels, channels),
            (((1,), (1,)), ((), ())),
            preferred_element_type=F32,
        ).astype(BF16)
        wide = []
        for place in range(fine):
            for tap in range(taps):
                grad_ref[place, tap * cells : (tap + 1) * cells, :] = product[
                    place * cells : (place + 1) * cells,
                    tap * fine_channels : (tap + 1) * fine_channels,
                ]
            wide.append(
                jnp.concatenate(
                    [act_ref[place, tap * cells : (tap + 1) * cells, :] for tap in range(taps)],
                    axis=1,
                )
            )
        acc_ref[...] += jnp.dot(
            octants.T, jnp.concatenate(wide, axis=0), preferred_element_type=F32
        )

    for row, ref in enumerate((upper_ref, stay_ref, lower_ref)):
        pl.when(step // groups == row)(functools.partial(work, ref))

    @pl.when(step == pl.num_programs(0) - 1)
    def _():
        total = acc_ref[...].T.astype(BF16)
        shards = down_ref.shape[0]
        rows = total.shape[0] // shards
        down_ref[:, :rows, :] = total.reshape(shards, rows, channels)


def fine_gradient(shards, count, from_upper, stay, from_lower, weight, fine_act):
    fine, voxels, fine_channels = fine_act.shape
    groups, _, channels = stay.shape
    taps = weight.shape[0]
    whole = pl.BlockSpec((1, voxels, channels), lambda i: (i % groups, 0, 0))
    rows = count * piece_rows(taps * fine_channels // shards, count)
    down = jax.ShapeDtypeStruct((shards, rows, channels), BF16)
    same = pl.BlockSpec(down.shape, lambda i: (0, 0, 0))
    block = pl.BlockSpec((8, voxels, fine_channels), lambda i: (i, 0, 0))
    return pl.pallas_call(
        functools.partial(fine_kernel, groups),
        grid=(3 * groups,),
        out_shape=(jax.ShapeDtypeStruct(fine_act.shape, BF16), down),
        in_specs=[
            whole, whole, whole,
            pl.BlockSpec(weight.shape, lambda i: (0, 0, 0)),
            block,
        ],
        out_specs=(block, same),
        scratch_shapes=[pltpu.VMEM((channels, taps * fine_channels), F32)],
        compiler_params=params(40),
        cost_estimate=pl.CostEstimate(
            flops=64 * fine * voxels * fine_channels * channels, bytes_accessed=8 * MIB,
            transcendentals=0,
        ),
        name="fine_gradient",
    )(from_upper, stay, from_lower, weight, fine_act)


def piece_rows(rows, count):
    return -(-rows // (16 * count)) * 16


def tree(values):
    while len(values) > 1:
        values = [
            values[i] + values[i + 1] if i + 1 < len(values) else values[i]
            for i in range(0, len(values), 2)
        ]
    return values[0]


def cost(*arrays):
    moved = sum(math.prod(x.shape) * jnp.dtype(x.dtype).itemsize for x in arrays)
    return pl.CostEstimate(flops=moved, bytes_accessed=moved, transcendentals=0)


def shapes_of(count, shape):
    return [jax.ShapeDtypeStruct(shape, F32 if step == 0 else BF16) for step in range(count)]


def parity():
    return lax.rem(lax.axis_index("dom"), 2)


def pair_kernel(count, early, down, late, *outs):
    planes, slabs = outs[:count], outs[count:]
    shards, cut, _ = early[0].shape
    piece = cut // count
    down_piece = down[0].shape[1] // count

    @pl.when(parity() == 0)
    def _():
        high = lax.axis_index("dom") // 2
        for step, ref in enumerate(planes):
            place = relative(high, step, count)
            for refs, size, start in ((early, piece, 0), (down, down_piece, piece)):
                span = pl.ds(pl.multiple_of(place * size, 16), size)
                total = refs[0][:, span, :].astype(F32) + refs[1][:, span, :].astype(F32)
                ref[:, start : start + size, :] = total.astype(ref.dtype)

    @pl.when(parity() == 1)
    def _():
        for step, ref in enumerate(slabs):
            shard = relative(lax.axis_index("dp"), step, shards)
            total = late[0][shard].astype(F32) + late[1][shard].astype(F32)
            ref[...] = total.astype(ref.dtype)


def pair_sum(count, early, down, late):
    shards, cut, channels = early[0].shape
    outs = shapes_of(count, (shards, (cut + down[0].shape[1]) // count, channels))
    outs += shapes_of(shards, late[0].shape[1:])
    parts = [*early, *down, *late]

    def kernel(*refs):
        pair_kernel(count, refs[:2], refs[2:4], refs[4:6], *refs[6:])

    outs = pl.pallas_call(
        kernel,
        out_shape=outs,
        in_specs=[VMEM] * 6,
        out_specs=[VMEM] * len(outs),
        compiler_params=params(24),
        cost_estimate=cost(*parts, *outs),
        name="pair_sum",
    )(*parts)
    return outs[:count], outs[count:]


def middle_kernel(count, shards, *refs):
    planes, slabs = refs[:count], refs[count : count + shards]
    to_slabs, mine_ref = refs[count + shards : -1], refs[-1]

    @pl.when(parity() == 0)
    def _():
        for step, ref in enumerate(to_slabs):
            shard = relative(lax.axis_index("dp"), step, shards)
            ref[...] = tree([part[shard].astype(F32) for part in planes]).astype(ref.dtype)

    @pl.when(parity() == 1)
    def _():
        mine_ref[...] = tree([part[...].astype(F32) for part in slabs]).astype(BF16)


def middle_sum(planes, slabs):
    count, shards = len(planes), len(slabs)
    outs = shapes_of(shards, planes[0].shape[1:])
    outs += [jax.ShapeDtypeStruct(slabs[0].shape, BF16)]
    parts = [*planes, *slabs]
    outs = pl.pallas_call(
        functools.partial(middle_kernel, count, shards),
        out_shape=outs,
        in_specs=[VMEM] * len(parts),
        out_specs=[VMEM] * len(outs),
        compiler_params=params(24),
        cost_estimate=cost(*parts, *outs),
        name="middle_sum",
    )(*parts)
    return outs[:shards], outs[shards]


def last_kernel(factor, shards, *refs):
    slabs, planes = refs[:shards], refs[shards:-2]
    for side, group, ref in ((0, slabs, refs[-2]), (1, planes, refs[-1])):

        @pl.when(parity() == side)
        def _():
            total = tree([part[...].astype(F32) for part in group])
            ref[...] = (total * factor).astype(BF16)


def last_sum(factor, slabs, planes):
    parts = [*slabs, *planes]
    return pl.pallas_call(
        functools.partial(last_kernel, factor, len(slabs)),
        out_shape=[
            jax.ShapeDtypeStruct(slabs[0].shape, BF16), jax.ShapeDtypeStruct(planes[0].shape, BF16)
        ],
        in_specs=[VMEM] * len(parts),
        out_specs=[VMEM] * 2,
        compiler_params=params(24),
        cost_estimate=cost(*parts),
        name="last_sum",
    )(*parts)


def gather_kernel(count, piece, down_piece, *refs):
    near, far = refs[:count], refs[count : 2 * count]
    rest_ref, rest_far_ref, conv_ref, down_ref, down_whole = refs[2 * count :]
    high = lax.axis_index("dom") // 2
    for side, group, rest in ((0, near, rest_far_ref), (1, far, rest_ref)):

        @pl.when(parity() == side)
        def _():
            for step, ref in enumerate(group):
                place = source_of(high, step, count)
                row = pl.multiple_of(place * piece, 16)
                conv_ref[pl.ds(row, piece), :] = ref[:piece, :].astype(F32)
                row = pl.multiple_of(place * down_piece, 16)
                down_whole[pl.ds(row, down_piece), :] = ref[piece:, :].astype(F32)
            conv_ref[count * piece :, :] = rest[...].astype(F32)

    down_ref[...] = down_whole[: down_ref.shape[0]]


def gather_up(conv_rows, down_rows, piece, near, far, rest, rest_far):
    count = len(near)
    channels = rest.shape[1]
    down_piece = near[0].shape[0] - piece
    outs = [jax.ShapeDtypeStruct((rows, channels), F32) for rows in (conv_rows, down_rows)]
    return pl.pallas_call(
        functools.partial(gather_kernel, count, piece, down_piece),
        out_shape=outs,
        in_specs=[VMEM] * (2 * count + 2),
        out_specs=[VMEM] * 2,
        scratch_shapes=[pltpu.VMEM((count * down_piece, channels), F32)],
        compiler_params=params(24),
        cost_estimate=cost(*near, *far, *outs),
        name="gather_up",
    )(*near, *far, rest, rest_far)


def body(grad_out, pre_act, conv_weight, down_weight, fine_act, neighbours, octant_routes):
    own = grad_out[0]
    pre = pre_act[0]
    links = neighbours[0]
    routes = octant_routes[0, 0]
    slots, voxels, channels = own.shape
    devices = lax.axis_size("dom")
    shards = lax.axis_size("dp")
    count = devices // 2
    factor = 1.0 / math.sqrt(shards * devices * slots * voxels)

    forward = [(i, i + 1) for i in range(devices - 1)]
    backward = [(i + 1, i) for i in range(devices - 1)]
    ring = [(i, (i + 1) % devices) for i in range(devices)]

    to_even = [(i + 1, i) for i in range(0, devices, 2)]
    to_odd = [(i, i + 1) for i in range(0, devices, 2)]

    def over_plane(parts, side):
        moved = [parts[0]]
        for step in range(1, count):
            pairs = [
                (2 * high + side, 2 * partner(high, step, count) + side) for high in range(count)
            ]
            moved.append(lax.ppermute(parts[step], "dom", pairs))
        return moved

    def over_shards(parts, side):
        moved = [parts[0]]
        for step in range(1, shards):
            pairs = [
                (shard * devices + index, partner(shard, step, shards) * devices + index)
                for shard in range(shards)
                for index in range(side, devices, 2)
            ]
            moved.append(lax.ppermute(parts[step], ("dp", "dom"), pairs))
        return moved

    low = lax.ppermute(own[:, voxels - PLANE :], "dom", forward)
    high = lax.ppermute(own[:, :PLANE], "dom", backward)
    to_lower, stay, to_upper = input_gradient(
        links, routes, own, low, high, pre, conv_weight
    )
    from_upper = lax.ppermute(to_lower, "dom", [(b, a) for a, b in ring])
    from_lower = lax.ppermute(to_upper, "dom", ring)
    conv_rows = 27 * channels // shards
    down_rows = down_weight.shape[0] * down_weight.shape[1] // shards
    piece = 16 * round((2 * (conv_rows + down_rows) / 3 - down_rows) / (16 * count))
    early, late = filter_gradient(shards, count * piece, links, own, low, high, pre)
    fine_grad, down = fine_gradient(
        shards, count, from_upper, stay, from_lower, down_weight, fine_act[0]
    )
    early = (early, lax.ppermute(early, "dom", to_even))
    late = (late, lax.ppermute(late, "dom", to_odd))
    down = (down, lax.ppermute(down, "dom", to_even))

    planes, slabs = pair_sum(count, early, down, late)
    slabs = over_shards(slabs, 1)
    planes = over_plane(planes, 0)
    to_slabs, rest = middle_sum(planes, slabs)
    to_slabs = over_shards(to_slabs, 0)
    mine, rest = last_sum(factor, to_slabs, over_plane([rest] * count, 1))
    near = over_plane([mine] * count, 0)
    far = [lax.ppermute(value, "dom", to_odd) for value in near]
    rest_far = lax.ppermute(rest, "dom", to_even)
    conv_grad, down_grad = gather_up(conv_rows, down_rows, piece, near, far, rest, rest_far)
    return (fine_grad[None], conv_grad, down_grad)


def solution(mesh):
    return jax.shard_map(
        body,
        mesh=mesh,
        in_specs=(
            P("dp", "dom", None, None),
            P("dp", "dom", None, None),
            P(),
            P(),
            P("dp", "dom", None, None),
            P("dp", "dom", None),
            P("dp", "dom", None, None),
        ),
        out_specs=(P("dp", "dom", None, None), P("dp", None), P("dp", None)),
        check_vma=False,
    )
```

```python
import functools
import math

import jax
import jax.numpy as jnp
from jax import lax
from jax.experimental import pallas as pl
from jax.experimental.pallas import tpu as pltpu
from jax.sharding import PartitionSpec as P

BE = 8
PLANE = BE * BE
HALF = BE // 2
F32 = jnp.float32
BF16 = jnp.bfloat16
MIB = 1 << 20

VMEM = pl.BlockSpec(memory_space=pltpu.VMEM)
SMEM = pl.BlockSpec(memory_space=pltpu.SMEM)
ANY = pl.BlockSpec(memory_space=pl.ANY)
HBM = pl.BlockSpec(memory_space=pltpu.HBM)


def params(mib):
    return pltpu.CompilerParams(vmem_limit_bytes=int(mib * MIB))


def relative(index, step, count):
    if count & (count - 1) == 0:
        return index ^ step
    return lax.rem(index + step, count)


def source_of(index, step, count):
    if count & (count - 1) == 0:
        return index ^ step
    return (index - step) % count if isinstance(index, int) else lax.rem(index + count - step, count)


def exchange(value, axis, step, stride):
    count = lax.axis_size(axis) // stride
    pairs = []
    for index in range(lax.axis_size(axis)):
        high, low = divmod(index, stride)
        other = high ^ step if count & (count - 1) == 0 else (high + step) % count
        pairs.append((index, other * stride + low))
    return lax.ppermute(value, axis, pairs)


def in_hbm(value):
    return pltpu.with_memory_space_constraint(value, pltpu.HBM)


def started(source, target, sem):
    copy = pltpu.make_async_copy(source, target, sem)
    copy.start()
    return copy


GROUPS = (0, -1, 1)


def column_of(tap):
    _, rest = divmod(tap, 9)
    tap_y, tap_z = rest // 3 - 1, rest % 3 - 1
    return 3 * GROUPS.index(-tap_z) + tap_y + 1


def extend(ref, wide_ref):
    slots = ref.shape[0]
    wide_ref[:slots] = ref[...]
    wide_ref[slots] = jnp.zeros(ref.shape[1:], ref.dtype)


def spread(links_ref, ref, start, step_x, slot, row, shift, win_ref):
    channels = ref.shape[-1]
    empty = ref.shape[0] - 1

    def fetch(step_y, step_z, first, rows):
        found = links_ref[slot, 9 * (step_x + 1) + 3 * (step_y + 1) + step_z + 1]
        place = jnp.where(found < 0, empty, found)
        return ref[place, start + first : start + first + rows, :].astype(F32)

    def column(step_z):
        below = fetch(-1, step_z, PLANE - 16, 16).reshape(2, BE, channels)[1:]
        middle = fetch(0, step_z, 0, PLANE).reshape(BE, BE, channels)
        above = fetch(1, step_z, 0, 16).reshape(2, BE, channels)[:1]
        return jnp.concatenate([below, middle, above], axis=0)

    value = column(0)
    if shift != 0:
        turn = 1 if shift < 0 else BE - 1
        edge = 0 if shift < 0 else BE - 1
        place_z = lax.broadcasted_iota(jnp.int32, value.shape, 1)
        value = jnp.where(
            place_z == edge,
            pltpu.roll(column(shift), turn, axis=1),
            pltpu.roll(value, turn, axis=1),
        )
    for tap_y in (-1, 0, 1):
        lane = (3 * GROUPS.index(shift) + tap_y + 1) * channels
        part = value[1 - tap_y : 1 - tap_y + BE].reshape(PLANE, channels)
        win_ref[row : row + PLANE, lane : lane + channels] = part.astype(BF16)


def builders(links_ref, own_ref, low_ref, high_ref, win_ref, shift):
    slots = own_ref.shape[0] - 1
    calls = []
    for plane in range(BE + 2):
        if plane == 0:
            ref, start, step_x = low_ref, 0, -1
        elif plane == BE + 1:
            ref, start, step_x = high_ref, 0, 1
        else:
            ref, start, step_x = own_ref, (plane - 1) * PLANE, 0
        for slot in range(slots):
            row = (plane * slots + slot) * PLANE
            calls.append(
                functools.partial(
                    spread, links_ref, ref, start, step_x, slot, row, shift, win_ref
                )
            )
    return calls


def interleave(first, second):
    done = 0
    for index, call in enumerate(first):
        call()
        until = len(second) * (index + 1) // len(first)
        for other in second[done:until]:
            other()
        done = until


def input_kernel(
    links_ref, routes_ref, own_hbm, low_ref, high_ref, pre_hbm, weight_ref,
    to_lower_ref, stay_ref, to_upper_ref,
    own_wide, low_wide, high_wide, win_ref, taps_ref, acc_ref, octants_ref,
    pre_ref, tap_sems, out_sems, in_sems,
):
    slots, voxels, channels = pre_ref.shape
    groups = routes_ref.shape[1] // 8
    own_copies = [
        started(own_hbm.at[0, slot], own_wide.at[slot], in_sems.at[slot]) for slot in range(slots)
    ]
    copies = {}
    for tap in sorted(range(27), key=column_of):
        column = column_of(tap)
        lanes = slice(column * channels, (column + 1) * channels)
        copies[tap] = started(
            weight_ref.at[tap], taps_ref.at[tap // 9, :, lanes], tap_sems.at[tap]
        )
    pre_copy = started(pre_hbm.at[0], pre_ref, in_sems.at[slots])
    for ref, wide in ((low_ref, low_wide), (high_ref, high_wide)):
        extend(ref, wide)
    own_wide[slots] = jnp.zeros((voxels, channels), BF16)
    octants_ref[...] = jnp.zeros_like(octants_ref)
    slab = slots * PLANE
    rows = BE * slab
    part = rows // 2

    def product(group, start):
        lanes = slice(3 * group * channels, 3 * (group + 1) * channels)
        total = None
        for index_x in range(3):
            offset = start + (2 - index_x) * slab
            term = lax.dot_general(
                win_ref[offset : offset + part, lanes],
                taps_ref[index_x, :, lanes],
                (((1,), (1,)), ((), ())),
                preferred_element_type=F32,
            )
            total = term if total is None else total + term
        if group > 0:
            total = total + acc_ref[start : start + part, :]
        acc_ref[start : start + part, :] = total

    def products(group):
        return [functools.partial(product, group, start) for start in range(0, rows, part)]

    def arrive(group):
        for tap, copy in copies.items():
            if column_of(tap) // 3 == group:
                copy.wait()

    sources = (links_ref, own_wide, low_wide, high_wide, win_ref)
    for copy in own_copies:
        copy.wait()
    for call in builders(*sources, GROUPS[0]):
        call()
    arrive(0)
    interleave(products(0), builders(*sources, GROUPS[1]))
    arrive(1)
    interleave(products(1), builders(*sources, GROUPS[2]))
    arrive(2)
    for call in products(2):
        call()
    pre_copy.wait()

    place_z = lax.broadcasted_iota(jnp.int32, (BE // 2, BE, channels), 1)
    for slot in range(slots):
        group = jnp.int32(3 * groups)
        for row in range(3):
            for place in range(groups):
                group = jnp.where(
                    routes_ref[row, 8 * place] == 8 * slot, row * groups + place, group
                )

        def finish(x, carry):
            value = acc_ref[pl.ds(pl.multiple_of(x * slab + slot * PLANE, PLANE), PLANE), :]
            pre = pre_ref[slot, pl.ds(pl.multiple_of(x * PLANE, PLANE), PLANE), :].astype(F32)
            value = jnp.where(pre > 0, value, 0.0).reshape(BE // 2, 2, BE, channels)
            even, odd = value[:, 0], value[:, 1]
            near = jnp.where(place_z < HALF, even, pltpu.roll(odd, HALF, axis=1))
            far = jnp.where(place_z < HALF, pltpu.roll(even, HALF, axis=1), odd)
            side = x // HALF
            row = (x - side * HALF) * 16
            for side_y in range(2):
                for side_z, piece in enumerate((near, far)):
                    block = piece[2 * side_y : 2 * side_y + 2].reshape(16, channels).astype(BF16)
                    start = (4 * side + 2 * side_y + side_z) * PLANE + row
                    octants_ref[group, pl.ds(pl.multiple_of(start, 16), 16), :] = block
            return carry

        lax.fori_loop(0, BE, finish, 0)
    outs = []
    for row, ref in enumerate((to_lower_ref, stay_ref, to_upper_ref)):
        outs.append(started(octants_ref.at[pl.ds(row * groups, groups)], ref, out_sems.at[row]))
    for copy in outs:
        copy.wait()


def wide_scratch(own, low):
    *_, slots, voxels, channels = own.shape
    return [
        pltpu.VMEM((slots + 1, voxels, channels), BF16),
        pltpu.VMEM((slots + 1, low.shape[1], channels), BF16),
        pltpu.VMEM((slots + 1, low.shape[1], channels), BF16),
        pltpu.VMEM((slots * PLANE * (BE + 2), 9 * channels), BF16),
    ]


def input_gradient(links, routes, own, low, high, pre, weight):
    _, slots, voxels, channels = own.shape
    groups = routes.shape[-1] // 8
    rows = slots * voxels
    out = jax.ShapeDtypeStruct((groups, voxels, channels), BF16)
    return pl.pallas_call(
        input_kernel,
        out_shape=(out, out, out),
        in_specs=[SMEM, SMEM, HBM, VMEM, VMEM, HBM, HBM],
        out_specs=(ANY, ANY, ANY),
        scratch_shapes=wide_scratch(own, low)
        + [
            pltpu.VMEM((3, channels, 9 * channels), BF16),
            pltpu.VMEM((rows, channels), F32),
            pltpu.VMEM((3 * groups + 1, voxels, channels), BF16),
            pltpu.VMEM((slots, voxels, channels), BF16),
            pltpu.SemaphoreType.DMA((27,)),
            pltpu.SemaphoreType.DMA((3,)),
            pltpu.SemaphoreType.DMA((slots + 1,)),
        ],
        compiler_params=params(40),
        cost_estimate=pl.CostEstimate(
            flops=2 * rows * 27 * channels * channels, bytes_accessed=8 * MIB, transcendentals=0
        ),
        name="input_gradient",
    )(links, routes, in_hbm(own), low, high, in_hbm(pre), in_hbm(weight))


def filter_kernel(
    shard_rows, links_ref, own_ref, low_ref, high_ref, pre_ref,
    keep_ref, send_ref, own_wide, low_wide, high_wide, win_ref, act_ref,
):
    slots, voxels, channels = own_ref.shape
    slab = slots * PLANE
    rows = BE * slab
    lanes = channels // 2
    for ref, wide in ((own_ref, own_wide), (low_ref, low_wide), (high_ref, high_wide)):
        extend(ref, wide)

    def transpose(pair):
        parts = []
        for x in (2 * pair, 2 * pair + 1):
            for slot in range(slots):
                parts.append(pre_ref[slot, x * PLANE : (x + 1) * PLANE, :])
        block = jnp.maximum(jnp.concatenate(parts, axis=0).astype(F32), 0.0)
        act_ref[:, pair * 2 * slab : (pair + 1) * 2 * slab] = block.T.astype(BF16)

    first = lax.rem(lax.axis_index("dom"), 2) == 0
    unit = math.gcd(channels, shard_rows)

    def product(tap):
        offset = (2 - tap // 9) * slab
        column = column_of(tap) * channels
        total = jnp.dot(
            act_ref[...],
            win_ref[offset : offset + rows, column : column + channels],
            preferred_element_type=F32,
        )
        left, right = total[:, :lanes], total[:, lanes:]
        keep = jnp.where(first, left, right).astype(BF16)
        send = jnp.where(first, right, left).astype(BF16)
        for part in range(channels // unit):
            shard, start = divmod(tap * channels + part * unit, shard_rows)
            span = slice(part * unit, (part + 1) * unit)
            keep_ref[shard, start : start + unit, :] = keep[span]
            send_ref[shard, start : start + unit, :] = send[span]

    def products(group):
        taps = [tap for tap in range(27) if column_of(tap) // 3 == group]
        return [functools.partial(product, tap) for tap in taps]

    sources = (links_ref, own_wide, low_wide, high_wide, win_ref)
    turns = [functools.partial(transpose, pair) for pair in range(BE // 2)]
    interleave(turns, builders(*sources, GROUPS[0]))
    interleave(products(0), builders(*sources, GROUPS[1]))
    interleave(products(1), builders(*sources, GROUPS[2]))
    for call in products(2):
        call()


def filter_gradient(shards, links, own, low, high, pre):
    slots, voxels, channels = own.shape
    shard_rows = 27 * channels // shards
    rows = slots * voxels
    out = jax.ShapeDtypeStruct((shards, shard_rows, channels // 2), BF16)
    return pl.pallas_call(
        functools.partial(filter_kernel, shard_rows),
        out_shape=(out, out),
        in_specs=[SMEM, VMEM, VMEM, VMEM, VMEM],
        out_specs=(VMEM, VMEM),
        scratch_shapes=wide_scratch(own, low) + [pltpu.VMEM((channels, rows), BF16)],
        compiler_params=params(40),
        cost_estimate=pl.CostEstimate(
            flops=2 * rows * 27 * channels * channels, bytes_accessed=8 * MIB, transcendentals=0
        ),
        name="filter_gradient",
    )(links, own, low, high, pre)


def down_kernel(
    groups, upper_ref, stay_ref, lower_ref, act_ref, keep_ref, send_ref, acc_ref
):
    step = pl.program_id(0)
    fine = act_ref.shape[0]
    channels = upper_ref.shape[-1]
    cells = upper_ref.shape[1] // fine
    taps = act_ref.shape[1] // cells

    @pl.when(step == 0)
    def _():
        acc_ref[...] = jnp.zeros_like(acc_ref)

    def work(ref):
        wide = []
        for place in range(fine):
            wide.append(
                jnp.concatenate(
                    [act_ref[place, tap * cells : (tap + 1) * cells, :] for tap in range(taps)],
                    axis=1,
                )
            )
        acc_ref[...] += jnp.dot(
            ref[0].T, jnp.concatenate(wide, axis=0), preferred_element_type=F32
        )

    for row, ref in enumerate((upper_ref, stay_ref, lower_ref)):
        pl.when(step // groups == row)(functools.partial(work, ref))

    @pl.when(step == pl.num_programs(0) - 1)
    def _():
        total = acc_ref[...].T
        first = lax.rem(lax.axis_index("dom"), 2) == 0
        lanes = channels // 2
        shards = keep_ref.shape[0]
        rows = total.shape[0] // shards
        left = total[:, :lanes].reshape(shards, rows, lanes)
        right = total[:, lanes:].reshape(shards, rows, lanes)
        keep_ref[:, :rows, :] = jnp.where(first, left, right).astype(BF16)
        send_ref[:, :rows, :] = jnp.where(first, right, left).astype(BF16)


def down_gradient(shards, count, from_upper, stay, from_lower, taps, fine_act):
    fine, voxels, fine_channels = fine_act.shape
    groups, _, channels = stay.shape
    whole = pl.BlockSpec((1, voxels, channels), lambda i: (i % groups, 0, 0))
    rows = count * piece_rows(taps * fine_channels // shards, count)
    down = jax.ShapeDtypeStruct((shards, rows, channels // 2), BF16)
    same = pl.BlockSpec(down.shape, lambda i: (0, 0, 0))
    return pl.pallas_call(
        functools.partial(down_kernel, groups),
        grid=(3 * groups,),
        out_shape=(down, down),
        in_specs=[
            whole, whole, whole, pl.BlockSpec((8, voxels, fine_channels), lambda i: (i, 0, 0))
        ],
        out_specs=(same, same),
        scratch_shapes=[pltpu.VMEM((channels, taps * fine_channels), F32)],
        compiler_params=params(40),
        cost_estimate=pl.CostEstimate(
            flops=64 * fine * voxels * fine_channels * channels, bytes_accessed=8 * MIB,
            transcendentals=0,
        ),
        name="down_gradient",
    )(from_upper, stay, from_lower, fine_act)


def fine_kernel(groups, upper_ref, stay_ref, lower_ref, weight_ref, grad_ref):
    step = pl.program_id(0)
    taps, fine_channels, channels = weight_ref.shape
    fine, voxels, _ = grad_ref.shape
    cells = voxels // taps

    def work(ref):
        product = lax.dot_general(
            ref[0],
            weight_ref[...].reshape(taps * fine_channels, channels),
            (((1,), (1,)), ((), ())),
            preferred_element_type=F32,
        ).astype(BF16)
        for place in range(fine):
            for tap in range(taps):
                grad_ref[place, tap * cells : (tap + 1) * cells, :] = product[
                    place * cells : (place + 1) * cells,
                    tap * fine_channels : (tap + 1) * fine_channels,
                ]

    for row, ref in enumerate((upper_ref, stay_ref, lower_ref)):
        pl.when(step // groups == row)(functools.partial(work, ref))


def fine_gradient(from_upper, stay, from_lower, weight):
    groups, voxels, channels = stay.shape
    whole = pl.BlockSpec((1, voxels, channels), lambda i: (i % groups, 0, 0))
    return pl.pallas_call(
        functools.partial(fine_kernel, groups),
        grid=(3 * groups,),
        out_shape=jax.ShapeDtypeStruct((24 * groups, voxels, weight.shape[1]), BF16),
        in_specs=[whole, whole, whole, pl.BlockSpec(weight.shape, lambda i: (0, 0, 0))],
        out_specs=pl.BlockSpec((8, voxels, weight.shape[1]), lambda i: (i, 0, 0)),
        compiler_params=params(40),
        cost_estimate=pl.CostEstimate(
            flops=2 * 24 * groups * voxels * weight.shape[1] * channels, bytes_accessed=4 * MIB,
            transcendentals=0,
        ),
        name="fine_gradient",
    )(from_upper, stay, from_lower, weight)


def piece_rows(rows, count):
    return -(-rows // (16 * count)) * 16


def tree(values):
    while len(values) > 1:
        values = [
            values[i] + values[i + 1] if i + 1 < len(values) else values[i]
            for i in range(0, len(values), 2)
        ]
    return values[0]


def cost(*arrays):
    moved = sum(math.prod(x.shape) * jnp.dtype(x.dtype).itemsize for x in arrays)
    return pl.CostEstimate(flops=moved, bytes_accessed=moved, transcendentals=0)


def shapes_of(count, shape):
    return [jax.ShapeDtypeStruct(shape, F32 if step == 0 else BF16) for step in range(count)]


def pair_kernel(count, conv_ref, conv_got_ref, down_ref, down_got_ref, *outs):
    planes, slabs = outs[:count], outs[count:]
    shards, rows, _ = conv_ref.shape
    down_piece = down_ref.shape[1] // count
    piece = planes[0].shape[1] - down_piece
    cut = count * piece
    for step, ref in enumerate(slabs):
        shard = relative(lax.axis_index("dp"), step, shards)
        total = conv_ref[shard, cut:, :].astype(F32) + conv_got_ref[shard, cut:, :].astype(F32)
        ref[...] = total.astype(ref.dtype)
    high = lax.axis_index("dom") // 2
    for step, ref in enumerate(planes):
        place = relative(high, step, count)
        for keep_ref, got_ref, size, start in (
            (conv_ref, conv_got_ref, piece, 0),
            (down_ref, down_got_ref, down_piece, piece),
        ):
            span = pl.ds(pl.multiple_of(place * size, 16), size)
            total = keep_ref[:, span, :].astype(F32) + got_ref[:, span, :].astype(F32)
            ref[:, start : start + size, :] = total.astype(ref.dtype)


def pair_sum(count, conv, conv_got, down, down_got):
    shards, rows, lanes = conv.shape
    down_piece = down.shape[1] // count
    unit = 16 * count
    piece = 16 * round((2 * (rows + down.shape[1]) / 3 - down.shape[1]) / unit)
    outs = shapes_of(count, (shards, piece + down_piece, lanes))
    outs += shapes_of(shards, (rows - count * piece, lanes))
    outs = pl.pallas_call(
        functools.partial(pair_kernel, count),
        out_shape=outs,
        in_specs=[VMEM] * 4,
        out_specs=[VMEM] * len(outs),
        compiler_params=params(32),
        cost_estimate=cost(conv, conv_got, *outs),
        name="pair_sum",
    )(conv, conv_got, down, down_got)
    return outs[:count], outs[count:], (piece, down_piece)


def far_first(count):
    return [0, *range(count - 1, 0, -1)]


def middle_kernel(count, shards, *refs):
    planes, slabs = refs[:count], refs[count : count + shards]
    to_slabs, mine_ref = refs[count + shards : -1], refs[-1]
    mine_ref[...] = tree([part[...].astype(F32) for part in slabs]).astype(BF16)
    for step, ref in zip(far_first(shards), to_slabs):
        shard = relative(lax.axis_index("dp"), step, shards)
        ref[...] = tree([part[shard].astype(F32) for part in planes]).astype(ref.dtype)


def middle_sum(planes, slabs):
    count, shards = len(planes), len(slabs)
    _, piece, lanes = planes[0].shape
    outs = shapes_of(shards, (piece, lanes)) + [jax.ShapeDtypeStruct(slabs[0].shape, BF16)]
    parts = [*planes, *slabs]
    outs = pl.pallas_call(
        functools.partial(middle_kernel, count, shards),
        out_shape=outs,
        in_specs=[VMEM] * len(parts),
        out_specs=[VMEM] * len(outs),
        compiler_params=params(32),
        cost_estimate=cost(*parts, *outs),
        name="middle_sum",
    )(*parts)
    return outs[:shards], outs[shards]


def last_kernel(factor, shards, *refs):
    *refs, _, planes_ref, slabs_ref = refs
    total = tree([part[...].astype(F32) for part in refs[:shards]])
    planes_ref[...] = (total * factor).astype(BF16)
    total = tree([part[...].astype(F32) for part in refs[shards:]])
    slabs_ref[...] = (total * factor).astype(BF16)


def last_sum(factor, slabs, planes, after):
    parts = [*slabs, *planes]
    return pl.pallas_call(
        functools.partial(last_kernel, factor, len(slabs)),
        out_shape=[
            jax.ShapeDtypeStruct(slabs[0].shape, BF16), jax.ShapeDtypeStruct(planes[0].shape, BF16)
        ],
        in_specs=[VMEM] * len(parts) + [HBM],
        out_specs=[VMEM] * 2,
        compiler_params=params(32),
        cost_estimate=cost(*parts),
        name="last_sum",
    )(*parts, in_hbm(after))


def gather_kernel(count, piece, down_piece, *refs):
    near, far = refs[:count], refs[count : 2 * count]
    rest_ref, rest_far_ref, conv_ref, down_ref, conv_whole, down_whole = refs[2 * count :]
    lanes = rest_ref.shape[1]
    cut = count * piece
    high = lax.axis_index("dom") // 2
    low = lax.rem(lax.axis_index("dom"), 2)
    for side, group, rest in ((low, near, rest_ref), (1 - low, far, rest_far_ref)):
        lane = pl.ds(pl.multiple_of(side * lanes, lanes), lanes)
        for step, ref in enumerate(group):
            place = source_of(high, step, count)
            row = pl.multiple_of(place * piece, 16)
            conv_whole[pl.ds(row, piece), lane] = ref[:piece, :].astype(F32)
            row = pl.multiple_of(place * down_piece, 16)
            down_whole[pl.ds(row, down_piece), lane] = ref[piece:, :].astype(F32)
        conv_whole[cut:, lane] = rest[...].astype(F32)
    conv_ref[...] = conv_whole[...]
    down_ref[...] = down_whole[: down_ref.shape[0]]


def gather_up(conv_rows, down_rows, pieces, near, far, rest, rest_far):
    count = len(near)
    lanes = rest.shape[1]
    outs = [jax.ShapeDtypeStruct((rows, 2 * lanes), F32) for rows in (conv_rows, down_rows)]
    return pl.pallas_call(
        functools.partial(gather_kernel, count, *pieces),
        out_shape=outs,
        in_specs=[VMEM] * (2 * count + 2),
        out_specs=[VMEM] * 2,
        scratch_shapes=[
            pltpu.VMEM((conv_rows, 2 * lanes), F32),
            pltpu.VMEM((count * pieces[1], 2 * lanes), F32),
        ],
        compiler_params=params(32),
        cost_estimate=cost(*near, *far, *outs),
        name="gather_up",
    )(*near, *far, rest, rest_far)


def body(grad_out, pre_act, conv_weight, down_weight, fine_act, neighbours, octant_routes):
    own = grad_out[0]
    pre = pre_act[0]
    links = neighbours[0]
    routes = octant_routes[0, 0]
    slots, voxels, channels = own.shape
    devices = lax.axis_size("dom")
    shards = lax.axis_size("dp")
    count = devices // 2
    factor = 1.0 / math.sqrt(shards * devices * slots * voxels)

    forward = [(i, i + 1) for i in range(devices - 1)]
    backward = [(i + 1, i) for i in range(devices - 1)]
    ring = [(i, (i + 1) % devices) for i in range(devices)]
    swap = [(i, i ^ 1) for i in range(devices)]

    def spread_out(parts, axis, stride, steps=None):
        steps = steps or list(range(len(parts)))
        return [parts[0]] + [
            exchange(part, axis, step, stride) for step, part in zip(steps[1:], parts[1:])
        ]

    low = lax.ppermute(own[:, voxels - PLANE :], "dom", forward)
    high = lax.ppermute(own[:, :PLANE], "dom", backward)
    to_lower, stay, to_upper = input_gradient(
        links, routes, grad_out, low, high, pre_act, conv_weight
    )
    from_upper = lax.ppermute(to_lower, "dom", [(b, a) for a, b in ring])
    from_lower = lax.ppermute(to_upper, "dom", ring)
    conv_keep, conv_send = filter_gradient(shards, links, own, low, high, pre)
    down_keep, down_send = down_gradient(
        shards, count, from_upper, stay, from_lower, down_weight.shape[0], fine_act[0]
    )
    fine_grad = fine_gradient(from_upper, stay, from_lower, down_weight)
    conv_got = lax.ppermute(conv_send, "dom", swap)
    down_got = lax.ppermute(down_send, "dom", swap)

    planes, slabs, pieces = pair_sum(count, conv_keep, conv_got, down_keep, down_got)
    slabs = spread_out(slabs, "dp", 1)
    planes = spread_out(planes, "dom", 2)
    to_slabs, rest = middle_sum(planes, slabs)
    to_slabs = spread_out(to_slabs, "dp", 1, far_first(shards))
    mine, rest = last_sum(factor, to_slabs, spread_out([rest] * count, "dom", 2), fine_grad)
    near = spread_out([mine] * count, "dom", 2)
    far = [lax.ppermute(value, "dom", swap) for value in near]
    rest_far = lax.ppermute(rest, "dom", swap)
    conv_rows = 27 * channels // shards
    down_rows = down_weight.shape[0] * down_weight.shape[1] // shards
    conv_grad, down_grad = gather_up(conv_rows, down_rows, pieces, near, far, rest, rest_far)
    return (fine_grad[None], conv_grad, down_grad)


def solution(mesh):
    return jax.shard_map(
        body,
        mesh=mesh,
        in_specs=(
            P("dp", "dom", None, None),
            P("dp", "dom", None, None),
            P(),
            P(),
            P("dp", "dom", None, None),
            P("dp", "dom", None),
            P("dp", "dom", None, None),
        ),
        out_specs=(P("dp", "dom", None, None), P("dp", None), P("dp", None)),
        check_vma=False,
    )
```

```python
import functools
import math

import jax
import jax.numpy as jnp
from jax import lax
from jax.experimental import pallas as pl
from jax.experimental.pallas import tpu as pltpu
from jax.sharding import PartitionSpec as P

BE = 8
PLANE = BE * BE
HALF = BE // 2
F32 = jnp.float32
BF16 = jnp.bfloat16
MIB = 1 << 20

VMEM = pl.BlockSpec(memory_space=pltpu.VMEM)
SMEM = pl.BlockSpec(memory_space=pltpu.SMEM)
ANY = pl.BlockSpec(memory_space=pl.ANY)
HBM = pl.BlockSpec(memory_space=pltpu.HBM)


def params(mib):
    return pltpu.CompilerParams(vmem_limit_bytes=int(mib * MIB))


def relative(index, step, count):
    if count & (count - 1) == 0:
        return index ^ step
    return lax.rem(index + step, count)


def source_of(index, step, count):
    if count & (count - 1) == 0:
        return index ^ step
    return (index - step) % count if isinstance(index, int) else lax.rem(index + count - step, count)


def exchange(value, axis, step, stride):
    count = lax.axis_size(axis) // stride
    pairs = []
    for index in range(lax.axis_size(axis)):
        high, low = divmod(index, stride)
        other = high ^ step if count & (count - 1) == 0 else (high + step) % count
        pairs.append((index, other * stride + low))
    return lax.ppermute(value, axis, pairs)


def in_hbm(value):
    return pltpu.with_memory_space_constraint(value, pltpu.HBM)


def started(source, target, sem):
    copy = pltpu.make_async_copy(source, target, sem)
    copy.start()
    return copy


GROUPS = (0, -1, 1)


def column_of(tap):
    _, rest = divmod(tap, 9)
    tap_y, tap_z = rest // 3 - 1, rest % 3 - 1
    return 3 * GROUPS.index(-tap_z) + tap_y + 1


def extend(ref, wide_ref):
    slots = ref.shape[0]
    wide_ref[:slots] = ref[...]
    wide_ref[slots] = jnp.zeros(ref.shape[1:], ref.dtype)


def spread(links_ref, ref, start, step_x, slot, row, shift, win_ref):
    channels = ref.shape[-1]
    empty = ref.shape[0] - 1

    def fetch(step_y, step_z, first, rows):
        found = links_ref[slot, 9 * (step_x + 1) + 3 * (step_y + 1) + step_z + 1]
        place = jnp.where(found < 0, empty, found)
        return ref[place, start + first : start + first + rows, :].astype(F32)

    def column(step_z):
        below = fetch(-1, step_z, PLANE - 16, 16).reshape(2, BE, channels)[1:]
        middle = fetch(0, step_z, 0, PLANE).reshape(BE, BE, channels)
        above = fetch(1, step_z, 0, 16).reshape(2, BE, channels)[:1]
        return jnp.concatenate([below, middle, above], axis=0)

    value = column(0)
    if shift != 0:
        turn = 1 if shift < 0 else BE - 1
        edge = 0 if shift < 0 else BE - 1
        place_z = lax.broadcasted_iota(jnp.int32, value.shape, 1)
        value = jnp.where(
            place_z == edge,
            pltpu.roll(column(shift), turn, axis=1),
            pltpu.roll(value, turn, axis=1),
        )
    for tap_y in (-1, 0, 1):
        lane = (3 * GROUPS.index(shift) + tap_y + 1) * channels
        part = value[1 - tap_y : 1 - tap_y + BE].reshape(PLANE, channels)
        win_ref[row : row + PLANE, lane : lane + channels] = part.astype(BF16)


def builders(links_ref, own_ref, low_ref, high_ref, win_ref, shift):
    slots = own_ref.shape[0] - 1
    calls = []
    for plane in range(BE + 2):
        if plane == 0:
            ref, start, step_x = low_ref, 0, -1
        elif plane == BE + 1:
            ref, start, step_x = high_ref, 0, 1
        else:
            ref, start, step_x = own_ref, (plane - 1) * PLANE, 0
        for slot in range(slots):
            row = (plane * slots + slot) * PLANE
            calls.append(
                functools.partial(
                    spread, links_ref, ref, start, step_x, slot, row, shift, win_ref
                )
            )
    return calls


def interleave(first, second):
    done = 0
    for index, call in enumerate(first):
        call()
        until = len(second) * (index + 1) // len(first)
        for other in second[done:until]:
            other()
        done = until


def prepare_kernel(own_hbm, pre_hbm, weight_hbm, own_wide, act_ref, taps_ref, pre_ref, sems):
    _, slots, voxels, channels = own_hbm.shape
    slab = slots * PLANE
    pre_copy = started(pre_hbm.at[0], pre_ref, sems.at[27])
    copies = [started(own_hbm.at[0], own_wide.at[pl.ds(0, slots)], sems.at[28])]
    for tap in range(27):
        lanes = slice(column_of(tap) * channels, (column_of(tap) + 1) * channels)
        copies.append(started(weight_hbm.at[tap], taps_ref.at[tap // 9, :, lanes], sems.at[tap]))
    own_wide[slots] = jnp.zeros((voxels, channels), BF16)
    pre_copy.wait()
    for pair in range(BE // 2):
        parts = []
        for x in (2 * pair, 2 * pair + 1):
            for slot in range(slots):
                parts.append(pre_ref[slot, x * PLANE : (x + 1) * PLANE, :])
        block = jnp.maximum(jnp.concatenate(parts, axis=0).astype(F32), 0.0)
        act_ref[:, pair * 2 * slab : (pair + 1) * 2 * slab] = block.T.astype(BF16)
    for copy in copies:
        copy.wait()


def prepare(own, pre, weight):
    _, slots, voxels, channels = own.shape
    return pl.pallas_call(
        prepare_kernel,
        out_shape=(
            jax.ShapeDtypeStruct((slots + 1, voxels, channels), BF16),
            jax.ShapeDtypeStruct((channels, slots * voxels), BF16),
            jax.ShapeDtypeStruct((3, channels, 9 * channels), BF16),
        ),
        in_specs=[HBM] * 3,
        out_specs=[VMEM] * 3,
        scratch_shapes=[
            pltpu.VMEM((slots, voxels, channels), BF16),
            pltpu.SemaphoreType.DMA((29,)),
        ],
        compiler_params=params(24),
        cost_estimate=pl.CostEstimate(
            flops=4 * MIB, bytes_accessed=12 * MIB, transcendentals=0
        ),
        name="prepare",
    )(in_hbm(own), in_hbm(pre), in_hbm(weight))


def input_kernel(
    links_ref, routes_ref, own_wide, low_ref, high_ref, pre_hbm, taps_ref,
    to_lower_ref, stay_ref, to_upper_ref,
    low_wide, high_wide, win_ref, acc_ref, octants_ref, pre_ref, out_sems, pre_sem,
):
    slots, voxels, channels = pre_ref.shape
    groups = routes_ref.shape[1] // 8
    pre_copy = started(pre_hbm.at[0], pre_ref, pre_sem)
    for ref, wide in ((low_ref, low_wide), (high_ref, high_wide)):
        extend(ref, wide)
    octants_ref[...] = jnp.zeros_like(octants_ref)
    slab = slots * PLANE
    rows = BE * slab
    part = rows // 2

    def product(group, start):
        lanes = slice(3 * group * channels, 3 * (group + 1) * channels)
        total = None
        for index_x in range(3):
            offset = start + (2 - index_x) * slab
            term = lax.dot_general(
                win_ref[offset : offset + part, lanes],
                taps_ref[index_x, :, lanes],
                (((1,), (1,)), ((), ())),
                preferred_element_type=F32,
            )
            total = term if total is None else total + term
        if group > 0:
            total = total + acc_ref[start : start + part, :]
        acc_ref[start : start + part, :] = total

    def products(group):
        return [functools.partial(product, group, start) for start in range(0, rows, part)]

    sources = (links_ref, own_wide, low_wide, high_wide, win_ref)
    for call in builders(*sources, GROUPS[0]):
        call()
    interleave(products(0), builders(*sources, GROUPS[1]))
    interleave(products(1), builders(*sources, GROUPS[2]))
    for call in products(2):
        call()
    pre_copy.wait()

    place_z = lax.broadcasted_iota(jnp.int32, (BE // 2, BE, channels), 1)
    for slot in range(slots):
        group = jnp.int32(3 * groups)
        for row in range(3):
            for place in range(groups):
                group = jnp.where(
                    routes_ref[row, 8 * place] == 8 * slot, row * groups + place, group
                )

        def finish(x, carry):
            value = acc_ref[pl.ds(pl.multiple_of(x * slab + slot * PLANE, PLANE), PLANE), :]
            pre = pre_ref[slot, pl.ds(pl.multiple_of(x * PLANE, PLANE), PLANE), :].astype(F32)
            value = jnp.where(pre > 0, value, 0.0).reshape(BE // 2, 2, BE, channels)
            even, odd = value[:, 0], value[:, 1]
            near = jnp.where(place_z < HALF, even, pltpu.roll(odd, HALF, axis=1))
            far = jnp.where(place_z < HALF, pltpu.roll(even, HALF, axis=1), odd)
            side = x // HALF
            row = (x - side * HALF) * 16
            for side_y in range(2):
                for side_z, piece in enumerate((near, far)):
                    block = piece[2 * side_y : 2 * side_y + 2].reshape(16, channels).astype(BF16)
                    start = (4 * side + 2 * side_y + side_z) * PLANE + row
                    octants_ref[group, pl.ds(pl.multiple_of(start, 16), 16), :] = block
            return carry

        lax.fori_loop(0, BE, finish, 0)
    outs = []
    for row, ref in enumerate((to_lower_ref, stay_ref, to_upper_ref)):
        outs.append(started(octants_ref.at[pl.ds(row * groups, groups)], ref, out_sems.at[row]))
    for copy in outs:
        copy.wait()


def window_scratch(slots, low):
    _, rows, channels = low.shape
    return [
        pltpu.VMEM((slots + 1, rows, channels), BF16),
        pltpu.VMEM((slots + 1, rows, channels), BF16),
        pltpu.VMEM((slots * PLANE * (BE + 2), 9 * channels), BF16),
    ]


def input_gradient(links, routes, own_wide, low, high, pre, taps):
    _, slots, voxels, channels = pre.shape
    groups = routes.shape[-1] // 8
    rows = slots * voxels
    out = jax.ShapeDtypeStruct((groups, voxels, channels), BF16)
    return pl.pallas_call(
        input_kernel,
        out_shape=(out, out, out),
        in_specs=[SMEM, SMEM, VMEM, VMEM, VMEM, HBM, VMEM],
        out_specs=(ANY, ANY, ANY),
        scratch_shapes=window_scratch(slots, low)
        + [
            pltpu.VMEM((rows, channels), F32),
            pltpu.VMEM((3 * groups + 1, voxels, channels), BF16),
            pltpu.VMEM((slots, voxels, channels), BF16),
            pltpu.SemaphoreType.DMA((3,)),
            pltpu.SemaphoreType.DMA,
        ],
        compiler_params=params(36),
        cost_estimate=pl.CostEstimate(
            flops=2 * rows * 27 * channels * channels, bytes_accessed=8 * MIB, transcendentals=0
        ),
        name="input_gradient",
    )(links, routes, own_wide, low, high, in_hbm(pre), taps)


def filter_kernel(
    shard_rows, links_ref, own_wide, low_ref, high_ref, act_ref,
    keep_ref, send_ref, low_wide, high_wide, win_ref,
):
    slots = low_ref.shape[0]
    channels, rows = act_ref.shape
    slab = slots * PLANE
    lanes = channels // 2
    for ref, wide in ((low_ref, low_wide), (high_ref, high_wide)):
        extend(ref, wide)
    first = lax.rem(lax.axis_index("dom"), 2) == 0
    unit = math.gcd(channels, shard_rows)

    def product(tap):
        offset = (2 - tap // 9) * slab
        column = column_of(tap) * channels
        total = jnp.dot(
            act_ref[...],
            win_ref[offset : offset + rows, column : column + channels],
            preferred_element_type=F32,
        )
        left, right = total[:, :lanes], total[:, lanes:]
        keep = jnp.where(first, left, right).astype(BF16)
        send = jnp.where(first, right, left).astype(BF16)
        for part in range(channels // unit):
            shard, start = divmod(tap * channels + part * unit, shard_rows)
            span = slice(part * unit, (part + 1) * unit)
            keep_ref[shard, start : start + unit, :] = keep[span]
            send_ref[shard, start : start + unit, :] = send[span]

    def products(group):
        taps = [tap for tap in range(27) if column_of(tap) // 3 == group]
        return [functools.partial(product, tap) for tap in taps]

    sources = (links_ref, own_wide, low_wide, high_wide, win_ref)
    for call in builders(*sources, GROUPS[0]):
        call()
    interleave(products(0), builders(*sources, GROUPS[1]))
    interleave(products(1), builders(*sources, GROUPS[2]))
    for call in products(2):
        call()


def filter_gradient(shards, links, own_wide, low, high, act):
    channels, rows = act.shape
    shard_rows = 27 * channels // shards
    out = jax.ShapeDtypeStruct((shards, shard_rows, channels // 2), BF16)
    return pl.pallas_call(
        functools.partial(filter_kernel, shard_rows),
        out_shape=(out, out),
        in_specs=[SMEM, VMEM, VMEM, VMEM, VMEM],
        out_specs=(VMEM, VMEM),
        scratch_shapes=window_scratch(low.shape[0], low),
        compiler_params=params(36),
        cost_estimate=pl.CostEstimate(
            flops=2 * rows * 27 * channels * channels, bytes_accessed=8 * MIB, transcendentals=0
        ),
        name="filter_gradient",
    )(links, own_wide, low, high, act)


def down_kernel(
    groups, upper_ref, stay_ref, lower_ref, act_ref, keep_ref, send_ref, acc_ref
):
    step = pl.program_id(0)
    fine = act_ref.shape[0]
    channels = upper_ref.shape[-1]
    cells = upper_ref.shape[1] // fine
    taps = act_ref.shape[1] // cells

    @pl.when(step == 0)
    def _():
        acc_ref[...] = jnp.zeros_like(acc_ref)

    def work(ref):
        wide = []
        for place in range(fine):
            wide.append(
                jnp.concatenate(
                    [act_ref[place, tap * cells : (tap + 1) * cells, :] for tap in range(taps)],
                    axis=1,
                )
            )
        acc_ref[...] += jnp.dot(
            ref[0].T, jnp.concatenate(wide, axis=0), preferred_element_type=F32
        )

    for row, ref in enumerate((upper_ref, stay_ref, lower_ref)):
        pl.when(step // groups == row)(functools.partial(work, ref))

    @pl.when(step == pl.num_programs(0) - 1)
    def _():
        total = acc_ref[...].T
        first = lax.rem(lax.axis_index("dom"), 2) == 0
        lanes = channels // 2
        shards = keep_ref.shape[0]
        rows = total.shape[0] // shards
        left = total[:, :lanes].reshape(shards, rows, lanes)
        right = total[:, lanes:].reshape(shards, rows, lanes)
        keep_ref[:, :rows, :] = jnp.where(first, left, right).astype(BF16)
        send_ref[:, :rows, :] = jnp.where(first, right, left).astype(BF16)


def down_gradient(shards, count, from_upper, stay, from_lower, taps, fine_act):
    fine, voxels, fine_channels = fine_act.shape
    groups, _, channels = stay.shape
    whole = pl.BlockSpec((1, voxels, channels), lambda i: (i % groups, 0, 0))
    rows = count * piece_rows(taps * fine_channels // shards, count)
    down = jax.ShapeDtypeStruct((shards, rows, channels // 2), BF16)
    same = pl.BlockSpec(down.shape, lambda i: (0, 0, 0))
    return pl.pallas_call(
        functools.partial(down_kernel, groups),
        grid=(3 * groups,),
        out_shape=(down, down),
        in_specs=[
            whole, whole, whole, pl.BlockSpec((8, voxels, fine_channels), lambda i: (i, 0, 0))
        ],
        out_specs=(same, same),
        scratch_shapes=[pltpu.VMEM((channels, taps * fine_channels), F32)],
        compiler_params=params(40),
        cost_estimate=pl.CostEstimate(
            flops=64 * fine * voxels * fine_channels * channels, bytes_accessed=8 * MIB,
            transcendentals=0,
        ),
        name="down_gradient",
    )(from_upper, stay, from_lower, fine_act)


def fine_kernel(groups, upper_ref, stay_ref, lower_ref, weight_ref, grad_ref):
    step = pl.program_id(0)
    taps, fine_channels, channels = weight_ref.shape
    fine, voxels, _ = grad_ref.shape
    cells = voxels // taps

    def work(ref):
        product = lax.dot_general(
            ref[0],
            weight_ref[...].reshape(taps * fine_channels, channels),
            (((1,), (1,)), ((), ())),
            preferred_element_type=F32,
        ).astype(BF16)
        for place in range(fine):
            for tap in range(taps):
                grad_ref[place, tap * cells : (tap + 1) * cells, :] = product[
                    place * cells : (place + 1) * cells,
                    tap * fine_channels : (tap + 1) * fine_channels,
                ]

    for row, ref in enumerate((upper_ref, stay_ref, lower_ref)):
        pl.when(step // groups == row)(functools.partial(work, ref))


def fine_gradient(from_upper, stay, from_lower, weight):
    groups, voxels, channels = stay.shape
    whole = pl.BlockSpec((1, voxels, channels), lambda i: (i % groups, 0, 0))
    return pl.pallas_call(
        functools.partial(fine_kernel, groups),
        grid=(3 * groups,),
        out_shape=jax.ShapeDtypeStruct((24 * groups, voxels, weight.shape[1]), BF16),
        in_specs=[whole, whole, whole, pl.BlockSpec(weight.shape, lambda i: (0, 0, 0))],
        out_specs=pl.BlockSpec((8, voxels, weight.shape[1]), lambda i: (i, 0, 0)),
        compiler_params=params(40),
        cost_estimate=pl.CostEstimate(
            flops=2 * 24 * groups * voxels * weight.shape[1] * channels, bytes_accessed=4 * MIB,
            transcendentals=0,
        ),
        name="fine_gradient",
    )(from_upper, stay, from_lower, weight)


def piece_rows(rows, count):
    return -(-rows // (16 * count)) * 16


def tree(values):
    while len(values) > 1:
        values = [
            values[i] + values[i + 1] if i + 1 < len(values) else values[i]
            for i in range(0, len(values), 2)
        ]
    return values[0]


def cost(*arrays):
    moved = sum(math.prod(x.shape) * jnp.dtype(x.dtype).itemsize for x in arrays)
    return pl.CostEstimate(flops=moved, bytes_accessed=moved, transcendentals=0)


def shapes_of(count, shape):
    return [jax.ShapeDtypeStruct(shape, F32 if step == 0 else BF16) for step in range(count)]


def pair_kernel(count, conv_ref, conv_got_ref, down_ref, down_got_ref, *outs):
    planes, slabs = outs[:count], outs[count:]
    shards, rows, _ = conv_ref.shape
    down_piece = down_ref.shape[1] // count
    piece = planes[0].shape[1] - down_piece
    cut = count * piece
    for step, ref in enumerate(slabs):
        shard = relative(lax.axis_index("dp"), step, shards)
        total = conv_ref[shard, cut:, :].astype(F32) + conv_got_ref[shard, cut:, :].astype(F32)
        ref[...] = total.astype(ref.dtype)
    high = lax.axis_index("dom") // 2
    for step, ref in enumerate(planes):
        place = relative(high, step, count)
        for keep_ref, got_ref, size, start in (
            (conv_ref, conv_got_ref, piece, 0),
            (down_ref, down_got_ref, down_piece, piece),
        ):
            span = pl.ds(pl.multiple_of(place * size, 16), size)
            total = keep_ref[:, span, :].astype(F32) + got_ref[:, span, :].astype(F32)
            ref[:, start : start + size, :] = total.astype(ref.dtype)


def pair_sum(count, conv, conv_got, down, down_got):
    shards, rows, lanes = conv.shape
    down_piece = down.shape[1] // count
    unit = 16 * count
    piece = 16 * round((2 * (rows + down.shape[1]) / 3 - down.shape[1]) / unit)
    outs = shapes_of(count, (shards, piece + down_piece, lanes))
    outs += shapes_of(shards, (rows - count * piece, lanes))
    outs = pl.pallas_call(
        functools.partial(pair_kernel, count),
        out_shape=outs,
        in_specs=[VMEM] * 4,
        out_specs=[VMEM] * len(outs),
        compiler_params=params(32),
        cost_estimate=cost(conv, conv_got, *outs),
        name="pair_sum",
    )(conv, conv_got, down, down_got)
    return outs[:count], outs[count:], (piece, down_piece)


def far_first(count):
    return [0, *range(count - 1, 0, -1)]


def middle_kernel(count, shards, *refs):
    planes, slabs = refs[:count], refs[count : count + shards]
    to_slabs, mine_ref = refs[count + shards : -1], refs[-1]
    mine_ref[...] = tree([part[...].astype(F32) for part in slabs]).astype(BF16)
    for step, ref in zip(far_first(shards), to_slabs):
        shard = relative(lax.axis_index("dp"), step, shards)
        ref[...] = tree([part[shard].astype(F32) for part in planes]).astype(ref.dtype)


def middle_sum(planes, slabs):
    count, shards = len(planes), len(slabs)
    _, piece, lanes = planes[0].shape
    outs = shapes_of(shards, (piece, lanes)) + [jax.ShapeDtypeStruct(slabs[0].shape, BF16)]
    parts = [*planes, *slabs]
    outs = pl.pallas_call(
        functools.partial(middle_kernel, count, shards),
        out_shape=outs,
        in_specs=[VMEM] * len(parts),
        out_specs=[VMEM] * len(outs),
        compiler_params=params(32),
        cost_estimate=cost(*parts, *outs),
        name="middle_sum",
    )(*parts)
    return outs[:shards], outs[shards]


def last_kernel(factor, shards, *refs):
    *refs, _, planes_ref, slabs_ref = refs
    total = tree([part[...].astype(F32) for part in refs[:shards]])
    planes_ref[...] = (total * factor).astype(BF16)
    total = tree([part[...].astype(F32) for part in refs[shards:]])
    slabs_ref[...] = (total * factor).astype(BF16)


def last_sum(factor, slabs, planes, after):
    parts = [*slabs, *planes]
    return pl.pallas_call(
        functools.partial(last_kernel, factor, len(slabs)),
        out_shape=[
            jax.ShapeDtypeStruct(slabs[0].shape, BF16), jax.ShapeDtypeStruct(planes[0].shape, BF16)
        ],
        in_specs=[VMEM] * len(parts) + [HBM],
        out_specs=[VMEM] * 2,
        compiler_params=params(32),
        cost_estimate=cost(*parts),
        name="last_sum",
    )(*parts, in_hbm(after))


def gather_kernel(count, piece, down_piece, *refs):
    near, far = refs[:count], refs[count : 2 * count]
    rest_ref, rest_far_ref, conv_ref, down_ref, conv_whole, down_whole = refs[2 * count :]
    lanes = rest_ref.shape[1]
    cut = count * piece
    high = lax.axis_index("dom") // 2
    low = lax.rem(lax.axis_index("dom"), 2)
    for side, group, rest in ((low, near, rest_ref), (1 - low, far, rest_far_ref)):
        lane = pl.ds(pl.multiple_of(side * lanes, lanes), lanes)
        for step, ref in enumerate(group):
            place = source_of(high, step, count)
            row = pl.multiple_of(place * piece, 16)
            conv_whole[pl.ds(row, piece), lane] = ref[:piece, :].astype(F32)
            row = pl.multiple_of(place * down_piece, 16)
            down_whole[pl.ds(row, down_piece), lane] = ref[piece:, :].astype(F32)
        conv_whole[cut:, lane] = rest[...].astype(F32)
    conv_ref[...] = conv_whole[...]
    down_ref[...] = down_whole[: down_ref.shape[0]]


def gather_up(conv_rows, down_rows, pieces, near, far, rest, rest_far):
    count = len(near)
    lanes = rest.shape[1]
    outs = [jax.ShapeDtypeStruct((rows, 2 * lanes), F32) for rows in (conv_rows, down_rows)]
    return pl.pallas_call(
        functools.partial(gather_kernel, count, *pieces),
        out_shape=outs,
        in_specs=[VMEM] * (2 * count + 2),
        out_specs=[VMEM] * 2,
        scratch_shapes=[
            pltpu.VMEM((conv_rows, 2 * lanes), F32),
            pltpu.VMEM((count * pieces[1], 2 * lanes), F32),
        ],
        compiler_params=params(32),
        cost_estimate=cost(*near, *far, *outs),
        name="gather_up",
    )(*near, *far, rest, rest_far)


def body(grad_out, pre_act, conv_weight, down_weight, fine_act, neighbours, octant_routes):
    own = grad_out[0]
    links = neighbours[0]
    routes = octant_routes[0, 0]
    slots, voxels, channels = own.shape
    devices = lax.axis_size("dom")
    shards = lax.axis_size("dp")
    count = devices // 2
    factor = 1.0 / math.sqrt(shards * devices * slots * voxels)

    forward = [(i, i + 1) for i in range(devices - 1)]
    backward = [(i + 1, i) for i in range(devices - 1)]
    ring = [(i, (i + 1) % devices) for i in range(devices)]
    swap = [(i, i ^ 1) for i in range(devices)]

    def spread_out(parts, axis, stride, steps=None):
        steps = steps or list(range(len(parts)))
        return [parts[0]] + [
            exchange(part, axis, step, stride) for step, part in zip(steps[1:], parts[1:])
        ]

    low = lax.ppermute(own[:, voxels - PLANE :], "dom", forward)
    high = lax.ppermute(own[:, :PLANE], "dom", backward)
    own_wide, act, taps = prepare(grad_out, pre_act, conv_weight)
    to_lower, stay, to_upper = input_gradient(
        links, routes, own_wide, low, high, pre_act, taps
    )
    from_upper = lax.ppermute(to_lower, "dom", [(b, a) for a, b in ring])
    from_lower = lax.ppermute(to_upper, "dom", ring)
    conv_keep, conv_send = filter_gradient(shards, links, own_wide, low, high, act)
    down_keep, down_send = down_gradient(
        shards, count, from_upper, stay, from_lower, down_weight.shape[0], fine_act[0]
    )
    fine_grad = fine_gradient(from_upper, stay, from_lower, down_weight)
    conv_got = lax.ppermute(conv_send, "dom", swap)
    down_got = lax.ppermute(down_send, "dom", swap)

    planes, slabs, pieces = pair_sum(count, conv_keep, conv_got, down_keep, down_got)
    slabs = spread_out(slabs, "dp", 1)
    planes = spread_out(planes, "dom", 2)
    to_slabs, rest = middle_sum(planes, slabs)
    to_slabs = spread_out(to_slabs, "dp", 1, far_first(shards))
    mine, rest = last_sum(factor, to_slabs, spread_out([rest] * count, "dom", 2), fine_grad)
    near = spread_out([mine] * count, "dom", 2)
    far = [lax.ppermute(value, "dom", swap) for value in near]
    rest_far = lax.ppermute(rest, "dom", swap)
    conv_rows = 27 * channels // shards
    down_rows = down_weight.shape[0] * down_weight.shape[1] // shards
    conv_grad, down_grad = gather_up(conv_rows, down_rows, pieces, near, far, rest, rest_far)
    return (fine_grad[None], conv_grad, down_grad)


def solution(mesh):
    return jax.shard_map(
        body,
        mesh=mesh,
        in_specs=(
            P("dp", "dom", None, None),
            P("dp", "dom", None, None),
            P(),
            P(),
            P("dp", "dom", None, None),
            P("dp", "dom", None),
            P("dp", "dom", None, None),
        ),
        out_specs=(P("dp", "dom", None, None), P("dp", None), P("dp", None)),
        check_vma=False,
    )
```

```python
import functools
import math

import jax
import jax.numpy as jnp
from jax import lax
from jax.experimental import pallas as pl
from jax.experimental.pallas import tpu as pltpu
from jax.sharding import PartitionSpec as P

BE = 8
PLANE = BE * BE
HALF = BE // 2
F32 = jnp.float32
BF16 = jnp.bfloat16
MIB = 1 << 20
PLANE_FIRST = 0.74

VMEM = pl.BlockSpec(memory_space=pltpu.VMEM)
SMEM = pl.BlockSpec(memory_space=pltpu.SMEM)
ANY = pl.BlockSpec(memory_space=pl.ANY)
HBM = pl.BlockSpec(memory_space=pltpu.HBM)


def params(mib):
    return pltpu.CompilerParams(vmem_limit_bytes=int(mib * MIB))


def relative(index, step, count):
    if count & (count - 1) == 0:
        return index ^ step
    return lax.rem(index + step, count)


def source_of(index, step, count):
    if count & (count - 1) == 0:
        return index ^ step
    return (index - step) % count if isinstance(index, int) else lax.rem(index + count - step, count)


def exchange(value, axis, step, stride):
    count = lax.axis_size(axis) // stride
    pairs = []
    for index in range(lax.axis_size(axis)):
        high, low = divmod(index, stride)
        other = high ^ step if count & (count - 1) == 0 else (high + step) % count
        pairs.append((index, other * stride + low))
    return lax.ppermute(value, axis, pairs)


def in_hbm(value):
    return pltpu.with_memory_space_constraint(value, pltpu.HBM)


def started(source, target, sem):
    copy = pltpu.make_async_copy(source, target, sem)
    copy.start()
    return copy


GROUPS = (0, -1, 1)


def column_of(tap):
    _, rest = divmod(tap, 9)
    tap_y, tap_z = rest // 3 - 1, rest % 3 - 1
    return 3 * GROUPS.index(-tap_z) + tap_y + 1


def extend(ref, wide_ref):
    slots = ref.shape[0]
    wide_ref[:slots] = ref[...]
    wide_ref[slots] = jnp.zeros(ref.shape[1:], ref.dtype)


def spread(links_ref, ref, start, step_x, slot, row, shift, win_ref):
    channels = ref.shape[-1]
    empty = ref.shape[0] - 1

    def fetch(step_y, step_z, first, rows):
        found = links_ref[slot, 0, 9 * (step_x + 1) + 3 * (step_y + 1) + step_z + 1]
        place = jnp.where(found < 0, empty, found)
        return ref[place, start + first : start + first + rows, :].astype(F32)

    def column(step_z):
        below = fetch(-1, step_z, PLANE - 16, 16).reshape(2, BE, channels)[1:]
        middle = fetch(0, step_z, 0, PLANE).reshape(BE, BE, channels)
        above = fetch(1, step_z, 0, 16).reshape(2, BE, channels)[:1]
        return jnp.concatenate([below, middle, above], axis=0)

    value = column(0)
    if shift != 0:
        turn = 1 if shift < 0 else BE - 1
        edge = 0 if shift < 0 else BE - 1
        place_z = lax.broadcasted_iota(jnp.int32, value.shape, 1)
        value = jnp.where(
            place_z == edge,
            pltpu.roll(column(shift), turn, axis=1),
            pltpu.roll(value, turn, axis=1),
        )
    for tap_y in (-1, 0, 1):
        lane = (3 * GROUPS.index(shift) + tap_y + 1) * channels
        part = value[1 - tap_y : 1 - tap_y + BE].reshape(PLANE, channels)
        win_ref[row : row + PLANE, lane : lane + channels] = part.astype(BF16)


def builders(links_ref, own_ref, low_ref, high_ref, win_ref, shift):
    slots = own_ref.shape[0] - 1
    calls = []
    for plane in range(BE + 2):
        if plane == 0:
            ref, start, step_x = low_ref, 0, -1
        elif plane == BE + 1:
            ref, start, step_x = high_ref, 0, 1
        else:
            ref, start, step_x = own_ref, (plane - 1) * PLANE, 0
        for slot in range(slots):
            row = (plane * slots + slot) * PLANE
            calls.append(
                functools.partial(
                    spread, links_ref, ref, start, step_x, slot, row, shift, win_ref
                )
            )
    return calls


def interleave(first, second):
    done = 0
    for index, call in enumerate(first):
        call()
        until = len(second) * (index + 1) // len(first)
        for other in second[done:until]:
            other()
        done = until


def prepare_kernel(own_hbm, pre_hbm, weight_hbm, own_wide, act_ref, taps_ref, pre_ref, sems):
    _, slots, voxels, channels = own_hbm.shape
    slab = slots * PLANE
    pre_copy = started(pre_hbm.at[0], pre_ref, sems.at[27])
    copies = [started(own_hbm.at[0], own_wide.at[pl.ds(0, slots)], sems.at[28])]
    for tap in range(27):
        lanes = slice(column_of(tap) * channels, (column_of(tap) + 1) * channels)
        copies.append(started(weight_hbm.at[tap], taps_ref.at[tap // 9, :, lanes], sems.at[tap]))
    own_wide[slots] = jnp.zeros((voxels, channels), BF16)
    pre_copy.wait()
    for pair in range(BE // 2):
        parts = []
        for x in (2 * pair, 2 * pair + 1):
            for slot in range(slots):
                parts.append(pre_ref[slot, x * PLANE : (x + 1) * PLANE, :])
        block = jnp.maximum(jnp.concatenate(parts, axis=0).astype(F32), 0.0)
        act_ref[:, pair * 2 * slab : (pair + 1) * 2 * slab] = block.T.astype(BF16)
    for copy in copies:
        copy.wait()


def prepare(own, pre, weight):
    _, slots, voxels, channels = own.shape
    return pl.pallas_call(
        prepare_kernel,
        out_shape=(
            jax.ShapeDtypeStruct((slots + 1, voxels, channels), BF16),
            jax.ShapeDtypeStruct((channels, slots * voxels), BF16),
            jax.ShapeDtypeStruct((3, channels, 9 * channels), BF16),
        ),
        in_specs=[HBM] * 3,
        out_specs=[VMEM] * 3,
        scratch_shapes=[
            pltpu.VMEM((slots, voxels, channels), BF16),
            pltpu.SemaphoreType.DMA((29,)),
        ],
        compiler_params=params(24),
        cost_estimate=pl.CostEstimate(
            flops=4 * MIB, bytes_accessed=12 * MIB, transcendentals=0
        ),
        name="prepare",
    )(in_hbm(own), in_hbm(pre), in_hbm(weight))


def input_kernel(
    links_ref, routes_ref, own_wide, low_ref, high_ref, pre_hbm, taps_ref,
    to_lower_ref, stay_ref, to_upper_ref, win_ref,
    low_wide, high_wide, acc_ref, octants_ref, pre_ref, out_sems, pre_sem,
):
    slots, voxels, channels = pre_ref.shape
    groups = routes_ref.shape[-1] // 8
    pre_copy = started(pre_hbm.at[0], pre_ref, pre_sem)
    for ref, wide in ((low_ref, low_wide), (high_ref, high_wide)):
        extend(ref, wide)
    octants_ref[...] = jnp.zeros_like(octants_ref)
    slab = slots * PLANE
    rows = BE * slab
    part = rows // 2

    def product(group, start):
        lanes = slice(3 * group * channels, 3 * (group + 1) * channels)
        total = None
        for index_x in range(3):
            offset = start + (2 - index_x) * slab
            term = lax.dot_general(
                win_ref[offset : offset + part, lanes],
                taps_ref[index_x, :, lanes],
                (((1,), (1,)), ((), ())),
                preferred_element_type=F32,
            )
            total = term if total is None else total + term
        if group > 0:
            total = total + acc_ref[start : start + part, :]
        acc_ref[start : start + part, :] = total

    def products(group):
        return [functools.partial(product, group, start) for start in range(0, rows, part)]

    sources = (links_ref, own_wide, low_wide, high_wide, win_ref)
    place_z = lax.broadcasted_iota(jnp.int32, (BE // 2, BE, channels), 1)
    targets = []
    for slot in range(slots):
        group = jnp.int32(3 * groups)
        for row in range(3):
            for place in range(groups):
                group = jnp.where(
                    routes_ref[row, 0, 8 * place] == 8 * slot, row * groups + place, group
                )
        targets.append(group)

    def finish(x, slot):
        start = x * slab + slot * PLANE
        value = acc_ref[start : start + PLANE, :]
        pre = pre_ref[slot, x * PLANE : (x + 1) * PLANE, :].astype(F32)
        value = jnp.where(pre > 0, value, 0.0).reshape(BE // 2, 2, BE, channels)
        even, odd = value[:, 0], value[:, 1]
        near = jnp.where(place_z < HALF, even, pltpu.roll(odd, HALF, axis=1))
        far = jnp.where(place_z < HALF, pltpu.roll(even, HALF, axis=1), odd)
        side, row = x // HALF, x % HALF * 16
        for side_y in range(2):
            for side_z, piece in enumerate((near, far)):
                block = piece[2 * side_y : 2 * side_y + 2].reshape(16, channels).astype(BF16)
                start = (4 * side + 2 * side_y + side_z) * PLANE + row
                octants_ref[targets[slot], start : start + 16, :] = block

    def finishes(planes):
        return [functools.partial(finish, x, slot) for x in planes for slot in range(slots)]

    for call in builders(*sources, GROUPS[0]):
        call()
    pre_copy.wait()
    interleave(products(0), builders(*sources, GROUPS[1]))
    interleave(products(1), builders(*sources, GROUPS[2]))
    last = products(2)
    last[0]()
    interleave(last[1:], finishes(range(HALF)))
    for call in finishes(range(HALF, BE)):
        call()
    outs = []
    for row, ref in enumerate((to_lower_ref, stay_ref, to_upper_ref)):
        outs.append(started(octants_ref.at[pl.ds(row * groups, groups)], ref, out_sems.at[row]))
    for copy in outs:
        copy.wait()


def input_gradient(links, routes, own_wide, low, high, pre, taps):
    _, slots, voxels, channels = pre.shape
    groups = routes.shape[-1] // 8
    rows = slots * voxels
    out = jax.ShapeDtypeStruct((groups, voxels, channels), BF16)
    windows = jax.ShapeDtypeStruct((slots * PLANE * (BE + 2), 9 * channels), BF16)
    return pl.pallas_call(
        input_kernel,
        out_shape=(out, out, out, windows),
        in_specs=[SMEM, SMEM, VMEM, VMEM, VMEM, HBM, VMEM],
        out_specs=(ANY, ANY, ANY, VMEM),
        scratch_shapes=[
            pltpu.VMEM((slots + 1, *low.shape[1:]), BF16),
            pltpu.VMEM((slots + 1, *low.shape[1:]), BF16),
            pltpu.VMEM((rows, channels), F32),
            pltpu.VMEM((3 * groups + 1, voxels, channels), BF16),
            pltpu.VMEM((slots, voxels, channels), BF16),
            pltpu.SemaphoreType.DMA((3,)),
            pltpu.SemaphoreType.DMA,
        ],
        compiler_params=params(20),
        cost_estimate=pl.CostEstimate(
            flops=2 * rows * 27 * channels * channels, bytes_accessed=8 * MIB, transcendentals=0
        ),
        name="input_gradient",
    )(links, routes, own_wide, low, high, in_hbm(pre), taps)


def filter_kernel(
    shard_rows, win_ref, act_ref, keep_ref, send_ref
):
    channels, rows = act_ref.shape
    slab = rows // BE
    lanes = channels // 2
    first = lax.rem(lax.axis_index("dom"), 2) == 0
    unit = math.gcd(channels, shard_rows)

    def product(tap):
        offset = (2 - tap // 9) * slab
        column = column_of(tap) * channels
        total = jnp.dot(
            act_ref[...],
            win_ref[offset : offset + rows, column : column + channels],
            preferred_element_type=F32,
        )
        left, right = total[:, :lanes], total[:, lanes:]
        keep = jnp.where(first, left, right).astype(BF16)
        send = jnp.where(first, right, left).astype(BF16)
        for part in range(channels // unit):
            shard, start = divmod(tap * channels + part * unit, shard_rows)
            span = slice(part * unit, (part + 1) * unit)
            keep_ref[shard, start : start + unit, :] = keep[span]
            send_ref[shard, start : start + unit, :] = send[span]

    for tap in sorted(range(27), key=column_of):
        product(tap)


def filter_gradient(shards, windows, act):
    channels, rows = act.shape
    shard_rows = 27 * channels // shards
    out = jax.ShapeDtypeStruct((shards, shard_rows, channels // 2), BF16)
    return pl.pallas_call(
        functools.partial(filter_kernel, shard_rows),
        out_shape=(out, out),
        in_specs=[VMEM, VMEM],
        out_specs=(VMEM, VMEM),
        compiler_params=params(12),
        cost_estimate=pl.CostEstimate(
            flops=2 * rows * 27 * channels * channels, bytes_accessed=8 * MIB, transcendentals=0
        ),
        name="filter_gradient",
    )(windows, act)


def down_kernel(
    groups, upper_ref, stay_ref, lower_ref, act_ref, keep_ref, send_ref, acc_ref
):
    step = pl.program_id(0)
    fine = act_ref.shape[0]
    channels = upper_ref.shape[-1]
    cells = upper_ref.shape[1] // fine
    taps = act_ref.shape[1] // cells

    @pl.when(step == 0)
    def _():
        acc_ref[...] = jnp.zeros_like(acc_ref)

    def work(ref):
        wide = []
        for place in range(fine):
            wide.append(
                jnp.concatenate(
                    [act_ref[place, tap * cells : (tap + 1) * cells, :] for tap in range(taps)],
                    axis=1,
                )
            )
        acc_ref[...] += jnp.dot(
            ref[0].T, jnp.concatenate(wide, axis=0), preferred_element_type=F32
        )

    for row, ref in enumerate((upper_ref, stay_ref, lower_ref)):
        pl.when(step // groups == row)(functools.partial(work, ref))

    @pl.when(step == pl.num_programs(0) - 1)
    def _():
        total = acc_ref[...].T
        first = lax.rem(lax.axis_index("dom"), 2) == 0
        lanes = channels // 2
        shards = keep_ref.shape[0]
        rows = total.shape[0] // shards
        left = total[:, :lanes].reshape(shards, rows, lanes)
        right = total[:, lanes:].reshape(shards, rows, lanes)
        keep_ref[:, :rows, :] = jnp.where(first, left, right).astype(BF16)
        send_ref[:, :rows, :] = jnp.where(first, right, left).astype(BF16)


def down_gradient(shards, count, from_upper, stay, from_lower, taps, fine_act):
    fine, voxels, fine_channels = fine_act.shape
    groups, _, channels = stay.shape
    whole = pl.BlockSpec((1, voxels, channels), lambda i: (i % groups, 0, 0))
    rows = count * piece_rows(taps * fine_channels // shards, count)
    down = jax.ShapeDtypeStruct((shards, rows, channels // 2), BF16)
    same = pl.BlockSpec(down.shape, lambda i: (0, 0, 0))
    return pl.pallas_call(
        functools.partial(down_kernel, groups),
        grid=(3 * groups,),
        out_shape=(down, down),
        in_specs=[
            whole, whole, whole, pl.BlockSpec((8, voxels, fine_channels), lambda i: (i, 0, 0))
        ],
        out_specs=(same, same),
        scratch_shapes=[pltpu.VMEM((channels, taps * fine_channels), F32)],
        compiler_params=params(40),
        cost_estimate=pl.CostEstimate(
            flops=64 * fine * voxels * fine_channels * channels, bytes_accessed=8 * MIB,
            transcendentals=0,
        ),
        name="down_gradient",
    )(from_upper, stay, from_lower, fine_act)


def fine_kernel(groups, upper_ref, stay_ref, lower_ref, weight_ref, grad_ref):
    step = pl.program_id(0)
    taps, fine_channels, channels = weight_ref.shape
    fine, voxels, _ = grad_ref.shape
    cells = voxels // taps

    def work(ref):
        product = lax.dot_general(
            ref[0],
            weight_ref[...].reshape(taps * fine_channels, channels),
            (((1,), (1,)), ((), ())),
            preferred_element_type=F32,
        ).astype(BF16)
        for place in range(fine):
            for tap in range(taps):
                grad_ref[place, tap * cells : (tap + 1) * cells, :] = product[
                    place * cells : (place + 1) * cells,
                    tap * fine_channels : (tap + 1) * fine_channels,
                ]

    for row, ref in enumerate((upper_ref, stay_ref, lower_ref)):
        pl.when(step // groups == row)(functools.partial(work, ref))


def fine_gradient(from_upper, stay, from_lower, weight):
    groups, voxels, channels = stay.shape
    whole = pl.BlockSpec((1, voxels, channels), lambda i: (i % groups, 0, 0))
    return pl.pallas_call(
        functools.partial(fine_kernel, groups),
        grid=(3 * groups,),
        out_shape=jax.ShapeDtypeStruct((24 * groups, voxels, weight.shape[1]), BF16),
        in_specs=[whole, whole, whole, pl.BlockSpec(weight.shape, lambda i: (0, 0, 0))],
        out_specs=pl.BlockSpec((8, voxels, weight.shape[1]), lambda i: (i, 0, 0)),
        compiler_params=params(40),
        cost_estimate=pl.CostEstimate(
            flops=2 * 24 * groups * voxels * weight.shape[1] * channels, bytes_accessed=4 * MIB,
            transcendentals=0,
        ),
        name="fine_gradient",
    )(from_upper, stay, from_lower, weight)


def piece_rows(rows, count):
    return -(-rows // (16 * count)) * 16


def tree(values):
    while len(values) > 1:
        values = [
            values[i] + values[i + 1] if i + 1 < len(values) else values[i]
            for i in range(0, len(values), 2)
        ]
    return values[0]


def cost(*arrays):
    moved = sum(math.prod(x.shape) * jnp.dtype(x.dtype).itemsize for x in arrays)
    return pl.CostEstimate(flops=moved, bytes_accessed=moved, transcendentals=0)


def shapes_of(count, shape):
    return [jax.ShapeDtypeStruct(shape, F32 if step == 0 else BF16) for step in range(count)]


def farthest_then_nearest(count):
    return [0, count - 1, *range(1, count - 1)]


def far_first(count):
    return [0, *range(count - 1, 0, -1)]


def pair_kernel(count, conv_ref, conv_got_ref, down_ref, down_got_ref, *outs):
    planes, slabs = outs[:count], outs[count:]
    shards, rows, _ = conv_ref.shape
    down_piece = down_ref.shape[1] // count
    piece = planes[0].shape[1] - down_piece
    cut = count * piece
    for step, ref in zip(farthest_then_nearest(shards), slabs):
        shard = relative(lax.axis_index("dp"), step, shards)
        total = conv_ref[shard, cut:, :].astype(F32) + conv_got_ref[shard, cut:, :].astype(F32)
        ref[...] = total.astype(ref.dtype)
    high = lax.axis_index("dom") // 2
    for step, ref in enumerate(planes):
        place = relative(high, step, count)
        for keep_ref, got_ref, size, start in (
            (conv_ref, conv_got_ref, piece, 0),
            (down_ref, down_got_ref, down_piece, piece),
        ):
            span = pl.ds(pl.multiple_of(place * size, 16), size)
            total = keep_ref[:, span, :].astype(F32) + got_ref[:, span, :].astype(F32)
            ref[:, start : start + size, :] = total.astype(ref.dtype)


def pair_sum(count, conv, conv_got, down, down_got):
    shards, rows, lanes = conv.shape
    down_piece = down.shape[1] // count
    unit = 16 * count
    piece = 16 * round((PLANE_FIRST * (rows + down.shape[1]) - down.shape[1]) / unit)
    outs = shapes_of(count, (shards, piece + down_piece, lanes))
    outs += shapes_of(shards, (rows - count * piece, lanes))
    outs = pl.pallas_call(
        functools.partial(pair_kernel, count),
        out_shape=outs,
        in_specs=[VMEM] * 4,
        out_specs=[VMEM] * len(outs),
        compiler_params=params(32),
        cost_estimate=cost(conv, conv_got, *outs),
        name="pair_sum",
    )(conv, conv_got, down, down_got)
    return outs[:count], outs[count:], (piece, down_piece)


def middle_kernel(count, shards, *refs):
    planes, slabs = refs[:count], refs[count : count + shards]
    to_slabs, mine_ref = refs[count + shards : -1], refs[-1]
    mine_ref[...] = tree([part[...].astype(F32) for part in slabs]).astype(BF16)
    for step, ref in zip(far_first(shards), to_slabs):
        shard = relative(lax.axis_index("dp"), step, shards)
        ref[...] = tree([part[shard].astype(F32) for part in planes]).astype(ref.dtype)


def middle_sum(planes, slabs):
    count, shards = len(planes), len(slabs)
    _, piece, lanes = planes[0].shape
    outs = shapes_of(shards, (piece, lanes)) + [jax.ShapeDtypeStruct(slabs[0].shape, BF16)]
    parts = [*planes, *slabs]
    outs = pl.pallas_call(
        functools.partial(middle_kernel, count, shards),
        out_shape=outs,
        in_specs=[VMEM] * len(parts),
        out_specs=[VMEM] * len(outs),
        compiler_params=params(32),
        cost_estimate=cost(*parts, *outs),
        name="middle_sum",
    )(*parts)
    return outs[:shards], outs[shards]


def last_kernel(factor, shards, *refs):
    *refs, _, planes_ref, slabs_ref = refs
    total = tree([part[...].astype(F32) for part in refs[:shards]])
    planes_ref[...] = (total * factor).astype(BF16)
    total = tree([part[...].astype(F32) for part in refs[shards:]])
    slabs_ref[...] = (total * factor).astype(BF16)


def last_sum(factor, slabs, planes, after):
    parts = [*slabs, *planes]
    return pl.pallas_call(
        functools.partial(last_kernel, factor, len(slabs)),
        out_shape=[
            jax.ShapeDtypeStruct(slabs[0].shape, BF16), jax.ShapeDtypeStruct(planes[0].shape, BF16)
        ],
        in_specs=[VMEM] * len(parts) + [HBM],
        out_specs=[VMEM] * 2,
        compiler_params=params(32),
        cost_estimate=cost(*parts),
        name="last_sum",
    )(*parts, in_hbm(after))


def gather_kernel(count, piece, down_piece, *refs):
    near, far = refs[:count], refs[count : 2 * count]
    rest_ref, rest_far_ref, conv_ref, down_ref, conv_whole, down_whole = refs[2 * count :]
    lanes = rest_ref.shape[1]
    cut = count * piece
    high = lax.axis_index("dom") // 2
    low = lax.rem(lax.axis_index("dom"), 2)
    for side, group, rest in ((low, near, rest_ref), (1 - low, far, rest_far_ref)):
        lane = pl.ds(pl.multiple_of(side * lanes, lanes), lanes)
        for step, ref in zip(far_first(count), group):
            place = source_of(high, step, count)
            row = pl.multiple_of(place * piece, 16)
            conv_whole[pl.ds(row, piece), lane] = ref[:piece, :].astype(F32)
            row = pl.multiple_of(place * down_piece, 16)
            down_whole[pl.ds(row, down_piece), lane] = ref[piece:, :].astype(F32)
        conv_whole[cut:, lane] = rest[...].astype(F32)
    conv_ref[...] = conv_whole[...]
    down_ref[...] = down_whole[: down_ref.shape[0]]


def gather_up(conv_rows, down_rows, pieces, near, far, rest, rest_far):
    count = len(near)
    lanes = rest.shape[1]
    outs = [jax.ShapeDtypeStruct((rows, 2 * lanes), F32) for rows in (conv_rows, down_rows)]
    return pl.pallas_call(
        functools.partial(gather_kernel, count, *pieces),
        out_shape=outs,
        in_specs=[VMEM] * (2 * count + 2),
        out_specs=[VMEM] * 2,
        scratch_shapes=[
            pltpu.VMEM((conv_rows, 2 * lanes), F32),
            pltpu.VMEM((count * pieces[1], 2 * lanes), F32),
        ],
        compiler_params=params(32),
        cost_estimate=cost(*near, *far, *outs),
        name="gather_up",
    )(*near, *far, rest, rest_far)


def body(grad_out, pre_act, conv_weight, down_weight, fine_act, neighbours, octant_routes):
    own = grad_out[0]
    links = neighbours.transpose(1, 0, 2)
    routes = octant_routes.transpose(0, 2, 1, 3)[0]
    slots, voxels, channels = own.shape
    devices = lax.axis_size("dom")
    shards = lax.axis_size("dp")
    count = devices // 2
    factor = 1.0 / math.sqrt(shards * devices * slots * voxels)

    forward = [(i, i + 1) for i in range(devices - 1)]
    backward = [(i + 1, i) for i in range(devices - 1)]
    ring = [(i, (i + 1) % devices) for i in range(devices)]
    swap = [(i, i ^ 1) for i in range(devices)]

    def spread_out(parts, axis, stride, steps=None):
        steps = steps or list(range(len(parts)))
        return [parts[0]] + [
            exchange(part, axis, step, stride) for step, part in zip(steps[1:], parts[1:])
        ]

    low = lax.ppermute(own[:, voxels - PLANE :], "dom", forward)
    high = lax.ppermute(own[:, :PLANE], "dom", backward)
    own_wide, act, taps = prepare(grad_out, pre_act, conv_weight)
    to_lower, stay, to_upper, windows = input_gradient(
        links, routes, own_wide, low, high, pre_act, taps
    )
    from_upper = lax.ppermute(to_lower, "dom", [(b, a) for a, b in ring])
    from_lower = lax.ppermute(to_upper, "dom", ring)
    conv_keep, conv_send = filter_gradient(shards, windows, act)
    down_keep, down_send = down_gradient(
        shards, count, from_upper, stay, from_lower, down_weight.shape[0], fine_act[0]
    )
    fine_grad = fine_gradient(from_upper, stay, from_lower, down_weight)
    conv_got = lax.ppermute(conv_send, "dom", swap)
    down_got = lax.ppermute(down_send, "dom", swap)

    planes, slabs, pieces = pair_sum(count, conv_keep, conv_got, down_keep, down_got)
    slabs = spread_out(slabs, "dp", 1, farthest_then_nearest(shards))
    planes = spread_out(planes, "dom", 2)
    to_slabs, rest = middle_sum(planes, slabs)
    to_slabs = spread_out(to_slabs, "dp", 1, far_first(shards))
    mine, rest = last_sum(factor, to_slabs, spread_out([rest] * count, "dom", 2), fine_grad)
    near = spread_out([mine] * count, "dom", 2, far_first(count))
    far = [lax.ppermute(value, "dom", swap) for value in near]
    rest_far = lax.ppermute(rest, "dom", swap)
    conv_rows = 27 * channels // shards
    down_rows = down_weight.shape[0] * down_weight.shape[1] // shards
    conv_grad, down_grad = gather_up(conv_rows, down_rows, pieces, near, far, rest, rest_far)
    return (fine_grad[None], conv_grad, down_grad)


def solution(mesh):
    return jax.shard_map(
        body,
        mesh=mesh,
        in_specs=(
            P("dp", "dom", None, None),
            P("dp", "dom", None, None),
            P(),
            P(),
            P("dp", "dom", None, None),
            P("dp", "dom", None),
            P("dp", "dom", None, None),
        ),
        out_specs=(P("dp", "dom", None, None), P("dp", None), P("dp", None)),
        check_vma=False,
    )
```

```python
import functools
import math

import jax
import jax.numpy as jnp
from jax import lax
from jax.experimental import pallas as pl
from jax.experimental.pallas import tpu as pltpu
from jax.sharding import PartitionSpec as P

BE = 8
PLANE = BE * BE
HALF = BE // 2
F32 = jnp.float32
BF16 = jnp.bfloat16
MIB = 1 << 20
PLANE_FIRST = 0.7

VMEM = pl.BlockSpec(memory_space=pltpu.VMEM)
SMEM = pl.BlockSpec(memory_space=pltpu.SMEM)
ANY = pl.BlockSpec(memory_space=pl.ANY)
HBM = pl.BlockSpec(memory_space=pltpu.HBM)


def params(mib):
    return pltpu.CompilerParams(vmem_limit_bytes=int(mib * MIB))


def relative(index, step, count):
    if count & (count - 1) == 0:
        return index ^ step
    return lax.rem(index + step, count)


def source_of(index, step, count):
    if count & (count - 1) == 0:
        return index ^ step
    return (index - step) % count if isinstance(index, int) else lax.rem(index + count - step, count)


def exchange(value, axis, step, stride):
    count = lax.axis_size(axis) // stride
    pairs = []
    for index in range(lax.axis_size(axis)):
        high, low = divmod(index, stride)
        other = high ^ step if count & (count - 1) == 0 else (high + step) % count
        pairs.append((index, other * stride + low))
    return lax.ppermute(value, axis, pairs)


def in_hbm(value):
    return pltpu.with_memory_space_constraint(value, pltpu.HBM)


def started(source, target, sem):
    copy = pltpu.make_async_copy(source, target, sem)
    copy.start()
    return copy


GROUPS = (0, -1, 1)


def column_of(tap):
    _, rest = divmod(tap, 9)
    tap_y, tap_z = rest // 3 - 1, rest % 3 - 1
    return 3 * GROUPS.index(-tap_z) + tap_y + 1


def extend(ref, wide_ref):
    slots = ref.shape[0]
    wide_ref[:slots] = ref[...]
    wide_ref[slots] = jnp.zeros(ref.shape[1:], ref.dtype)


def spread(links_ref, ref, start, step_x, slot, row, shift, win_ref):
    channels = ref.shape[-1]
    empty = ref.shape[0] - 1

    def fetch(step_y, step_z, first, rows):
        found = links_ref[slot, 0, 9 * (step_x + 1) + 3 * (step_y + 1) + step_z + 1]
        place = jnp.where(found < 0, empty, found)
        return ref[place, start + first : start + first + rows, :].astype(F32)

    def column(step_z):
        below = fetch(-1, step_z, PLANE - 16, 16).reshape(2, BE, channels)[1:]
        middle = fetch(0, step_z, 0, PLANE).reshape(BE, BE, channels)
        above = fetch(1, step_z, 0, 16).reshape(2, BE, channels)[:1]
        return jnp.concatenate([below, middle, above], axis=0)

    value = column(0)
    if shift != 0:
        turn = 1 if shift < 0 else BE - 1
        edge = 0 if shift < 0 else BE - 1
        place_z = lax.broadcasted_iota(jnp.int32, value.shape, 1)
        value = jnp.where(
            place_z == edge,
            pltpu.roll(column(shift), turn, axis=1),
            pltpu.roll(value, turn, axis=1),
        )
    for tap_y in (-1, 0, 1):
        lane = (3 * GROUPS.index(shift) + tap_y + 1) * channels
        part = value[1 - tap_y : 1 - tap_y + BE].reshape(PLANE, channels)
        win_ref[row : row + PLANE, lane : lane + channels] = part.astype(BF16)


def builders(links_ref, own_ref, low_ref, high_ref, win_ref, shift):
    slots = own_ref.shape[0] - 1
    calls = []
    for plane in range(BE + 2):
        if plane == 0:
            ref, start, step_x = low_ref, 0, -1
        elif plane == BE + 1:
            ref, start, step_x = high_ref, 0, 1
        else:
            ref, start, step_x = own_ref, (plane - 1) * PLANE, 0
        for slot in range(slots):
            row = (plane * slots + slot) * PLANE
            calls.append(
                functools.partial(
                    spread, links_ref, ref, start, step_x, slot, row, shift, win_ref
                )
            )
    return calls


def interleave(first, second):
    done = 0
    for index, call in enumerate(first):
        call()
        until = len(second) * (index + 1) // len(first)
        for other in second[done:until]:
            other()
        done = until


def prepare_kernel(own_hbm, pre_hbm, weight_hbm, own_wide, act_ref, taps_ref, pre_ref, sems):
    _, slots, voxels, channels = own_hbm.shape
    slab = slots * PLANE
    pre_copy = started(pre_hbm.at[0], pre_ref, sems.at[27])
    copies = [started(own_hbm.at[0], own_wide.at[pl.ds(0, slots)], sems.at[28])]
    for tap in range(27):
        lanes = slice(column_of(tap) * channels, (column_of(tap) + 1) * channels)
        copies.append(started(weight_hbm.at[tap], taps_ref.at[tap // 9, :, lanes], sems.at[tap]))
    own_wide[slots] = jnp.zeros((voxels, channels), BF16)
    pre_copy.wait()
    for pair in range(BE // 2):
        parts = []
        for x in (2 * pair, 2 * pair + 1):
            for slot in range(slots):
                parts.append(pre_ref[slot, x * PLANE : (x + 1) * PLANE, :])
        block = jnp.maximum(jnp.concatenate(parts, axis=0).astype(F32), 0.0)
        act_ref[:, pair * 2 * slab : (pair + 1) * 2 * slab] = block.T.astype(BF16)
    for copy in copies:
        copy.wait()


def prepare(own, pre, weight):
    _, slots, voxels, channels = own.shape
    return pl.pallas_call(
        prepare_kernel,
        out_shape=(
            jax.ShapeDtypeStruct((slots + 1, voxels, channels), BF16),
            jax.ShapeDtypeStruct((channels, slots * voxels), BF16),
            jax.ShapeDtypeStruct((3, channels, 9 * channels), BF16),
        ),
        in_specs=[HBM] * 3,
        out_specs=[VMEM] * 3,
        scratch_shapes=[
            pltpu.VMEM((slots, voxels, channels), BF16),
            pltpu.SemaphoreType.DMA((29,)),
        ],
        compiler_params=params(24),
        cost_estimate=pl.CostEstimate(
            flops=4 * MIB, bytes_accessed=12 * MIB, transcendentals=0
        ),
        name="prepare",
    )(in_hbm(own), in_hbm(pre), in_hbm(weight))


def input_kernel(
    links_ref, routes_ref, own_wide, low_ref, high_ref, pre_hbm, taps_ref,
    to_lower_ref, stay_ref, to_upper_ref, win_ref,
    low_wide, high_wide, acc_ref, octants_ref, pre_ref, out_sems, pre_sem,
):
    slots, voxels, channels = pre_ref.shape
    groups = routes_ref.shape[-1] // 8
    pre_copy = started(pre_hbm.at[0], pre_ref, pre_sem)
    for ref, wide in ((low_ref, low_wide), (high_ref, high_wide)):
        extend(ref, wide)
    octants_ref[...] = jnp.zeros_like(octants_ref)
    slab = slots * PLANE
    rows = BE * slab
    part = rows // 2

    def product(group, start):
        lanes = slice(3 * group * channels, 3 * (group + 1) * channels)
        total = None
        for index_x in range(3):
            offset = start + (2 - index_x) * slab
            term = lax.dot_general(
                win_ref[offset : offset + part, lanes],
                taps_ref[index_x, :, lanes],
                (((1,), (1,)), ((), ())),
                preferred_element_type=F32,
            )
            total = term if total is None else total + term
        if group > 0:
            total = total + acc_ref[start : start + part, :]
        acc_ref[start : start + part, :] = total

    def products(group):
        return [functools.partial(product, group, start) for start in range(0, rows, part)]

    sources = (links_ref, own_wide, low_wide, high_wide, win_ref)
    place_z = lax.broadcasted_iota(jnp.int32, (BE // 2, BE, channels), 1)
    targets = []
    for slot in range(slots):
        group = jnp.int32(3 * groups)
        for row in range(3):
            for place in range(groups):
                group = jnp.where(
                    routes_ref[row, 0, 8 * place] == 8 * slot, row * groups + place, group
                )
        targets.append(group)

    def finish(x, slot):
        start = x * slab + slot * PLANE
        value = acc_ref[start : start + PLANE, :]
        pre = pre_ref[slot, x * PLANE : (x + 1) * PLANE, :].astype(F32)
        value = jnp.where(pre > 0, value, 0.0).reshape(BE // 2, 2, BE, channels)
        even, odd = value[:, 0], value[:, 1]
        near = jnp.where(place_z < HALF, even, pltpu.roll(odd, HALF, axis=1))
        far = jnp.where(place_z < HALF, pltpu.roll(even, HALF, axis=1), odd)
        side, row = x // HALF, x % HALF * 16
        for side_y in range(2):
            for side_z, piece in enumerate((near, far)):
                block = piece[2 * side_y : 2 * side_y + 2].reshape(16, channels).astype(BF16)
                start = (4 * side + 2 * side_y + side_z) * PLANE + row
                octants_ref[targets[slot], start : start + 16, :] = block

    def finishes(planes):
        return [functools.partial(finish, x, slot) for x in planes for slot in range(slots)]

    for call in builders(*sources, GROUPS[0]):
        call()
    pre_copy.wait()
    interleave(products(0), builders(*sources, GROUPS[1]))
    interleave(products(1), builders(*sources, GROUPS[2]))
    last = products(2)
    last[0]()
    interleave(last[1:], finishes(range(HALF)))
    outs = []

    def leave(side):
        rows = pl.ds(side * 4 * PLANE, 4 * PLANE)
        for row, ref in enumerate((to_lower_ref, stay_ref, to_upper_ref)):
            outs.append(
                started(
                    octants_ref.at[pl.ds(row * groups, groups), rows],
                    ref.at[:, rows],
                    out_sems.at[3 * side + row],
                )
            )

    leave(0)
    for call in finishes(range(HALF, BE)):
        call()
    leave(1)
    for copy in outs:
        copy.wait()


def input_gradient(links, routes, own_wide, low, high, pre, taps):
    _, slots, voxels, channels = pre.shape
    groups = routes.shape[-1] // 8
    rows = slots * voxels
    out = jax.ShapeDtypeStruct((groups, voxels, channels), BF16)
    windows = jax.ShapeDtypeStruct((slots * PLANE * (BE + 2), 9 * channels), BF16)
    return pl.pallas_call(
        input_kernel,
        out_shape=(out, out, out, windows),
        in_specs=[SMEM, SMEM, VMEM, VMEM, VMEM, HBM, VMEM],
        out_specs=(ANY, ANY, ANY, VMEM),
        scratch_shapes=[
            pltpu.VMEM((slots + 1, *low.shape[1:]), BF16),
            pltpu.VMEM((slots + 1, *low.shape[1:]), BF16),
            pltpu.VMEM((rows, channels), F32),
            pltpu.VMEM((3 * groups + 1, voxels, channels), BF16),
            pltpu.VMEM((slots, voxels, channels), BF16),
            pltpu.SemaphoreType.DMA((6,)),
            pltpu.SemaphoreType.DMA,
        ],
        compiler_params=params(20),
        cost_estimate=pl.CostEstimate(
            flops=2 * rows * 27 * channels * channels, bytes_accessed=8 * MIB, transcendentals=0
        ),
        name="input_gradient",
    )(links, routes, own_wide, low, high, in_hbm(pre), taps)


def filter_kernel(
    shard_rows, win_ref, act_ref, keep_ref, send_ref
):
    channels, rows = act_ref.shape
    slab = rows // BE
    lanes = channels // 2
    first = lax.rem(lax.axis_index("dom"), 2) == 0
    unit = math.gcd(channels, shard_rows)

    def product(tap):
        offset = (2 - tap // 9) * slab
        column = column_of(tap) * channels
        total = jnp.dot(
            act_ref[...],
            win_ref[offset : offset + rows, column : column + channels],
            preferred_element_type=F32,
        )
        left, right = total[:, :lanes], total[:, lanes:]
        keep = jnp.where(first, left, right).astype(BF16)
        send = jnp.where(first, right, left).astype(BF16)
        for part in range(channels // unit):
            shard, start = divmod(tap * channels + part * unit, shard_rows)
            span = slice(part * unit, (part + 1) * unit)
            keep_ref[shard, start : start + unit, :] = keep[span]
            send_ref[shard, start : start + unit, :] = send[span]

    for tap in sorted(range(27), key=column_of):
        product(tap)


def filter_gradient(shards, windows, act):
    channels, rows = act.shape
    shard_rows = 27 * channels // shards
    out = jax.ShapeDtypeStruct((shards, shard_rows, channels // 2), BF16)
    return pl.pallas_call(
        functools.partial(filter_kernel, shard_rows),
        out_shape=(out, out),
        in_specs=[VMEM, VMEM],
        out_specs=(VMEM, VMEM),
        compiler_params=params(12),
        cost_estimate=pl.CostEstimate(
            flops=2 * rows * 27 * channels * channels, bytes_accessed=8 * MIB, transcendentals=0
        ),
        name="filter_gradient",
    )(windows, act)


def down_kernel(
    groups, upper_ref, stay_ref, lower_ref, act_ref, keep_ref, send_ref, acc_ref
):
    step = pl.program_id(0)
    fine = act_ref.shape[0]
    channels = upper_ref.shape[-1]
    cells = upper_ref.shape[1] // fine
    taps = act_ref.shape[1] // cells

    @pl.when(step == 0)
    def _():
        acc_ref[...] = jnp.zeros_like(acc_ref)

    def work(ref):
        wide = []
        for place in range(fine):
            wide.append(
                jnp.concatenate(
                    [act_ref[place, tap * cells : (tap + 1) * cells, :] for tap in range(taps)],
                    axis=1,
                )
            )
        acc_ref[...] += jnp.dot(
            ref[0].T, jnp.concatenate(wide, axis=0), preferred_element_type=F32
        )

    for row, ref in enumerate((upper_ref, stay_ref, lower_ref)):
        pl.when(step // groups == row)(functools.partial(work, ref))

    @pl.when(step == pl.num_programs(0) - 1)
    def _():
        total = acc_ref[...].T
        first = lax.rem(lax.axis_index("dom"), 2) == 0
        lanes = channels // 2
        shards = keep_ref.shape[0]
        rows = total.shape[0] // shards
        left = total[:, :lanes].reshape(shards, rows, lanes)
        right = total[:, lanes:].reshape(shards, rows, lanes)
        keep_ref[:, :rows, :] = jnp.where(first, left, right).astype(BF16)
        send_ref[:, :rows, :] = jnp.where(first, right, left).astype(BF16)


def down_gradient(shards, count, from_upper, stay, from_lower, taps, fine_act):
    fine, voxels, fine_channels = fine_act.shape
    groups, _, channels = stay.shape
    whole = pl.BlockSpec((1, voxels, channels), lambda i: (i % groups, 0, 0))
    rows = count * piece_rows(taps * fine_channels // shards, count)
    down = jax.ShapeDtypeStruct((shards, rows, channels // 2), BF16)
    same = pl.BlockSpec(down.shape, lambda i: (0, 0, 0))
    return pl.pallas_call(
        functools.partial(down_kernel, groups),
        grid=(3 * groups,),
        out_shape=(down, down),
        in_specs=[
            whole, whole, whole, pl.BlockSpec((8, voxels, fine_channels), lambda i: (i, 0, 0))
        ],
        out_specs=(same, same),
        scratch_shapes=[pltpu.VMEM((channels, taps * fine_channels), F32)],
        compiler_params=params(40),
        cost_estimate=pl.CostEstimate(
            flops=64 * fine * voxels * fine_channels * channels, bytes_accessed=8 * MIB,
            transcendentals=0,
        ),
        name="down_gradient",
    )(from_upper, stay, from_lower, fine_act)


def fine_kernel(groups, upper_ref, stay_ref, lower_ref, weight_ref, grad_ref):
    step = pl.program_id(0)
    taps, fine_channels, channels = weight_ref.shape
    fine, voxels, _ = grad_ref.shape
    cells = voxels // taps

    def work(ref):
        product = lax.dot_general(
            ref[0],
            weight_ref[...].reshape(taps * fine_channels, channels),
            (((1,), (1,)), ((), ())),
            preferred_element_type=F32,
        ).astype(BF16)
        for place in range(fine):
            for tap in range(taps):
                grad_ref[place, tap * cells : (tap + 1) * cells, :] = product[
                    place * cells : (place + 1) * cells,
                    tap * fine_channels : (tap + 1) * fine_channels,
                ]

    for row, ref in enumerate((upper_ref, stay_ref, lower_ref)):
        pl.when(step // groups == row)(functools.partial(work, ref))


def fine_gradient(from_upper, stay, from_lower, weight):
    groups, voxels, channels = stay.shape
    whole = pl.BlockSpec((1, voxels, channels), lambda i: (i % groups, 0, 0))
    return pl.pallas_call(
        functools.partial(fine_kernel, groups),
        grid=(3 * groups,),
        out_shape=jax.ShapeDtypeStruct((24 * groups, voxels, weight.shape[1]), BF16),
        in_specs=[whole, whole, whole, pl.BlockSpec(weight.shape, lambda i: (0, 0, 0))],
        out_specs=pl.BlockSpec((8, voxels, weight.shape[1]), lambda i: (i, 0, 0)),
        compiler_params=params(40),
        cost_estimate=pl.CostEstimate(
            flops=2 * 24 * groups * voxels * weight.shape[1] * channels, bytes_accessed=4 * MIB,
            transcendentals=0,
        ),
        name="fine_gradient",
    )(from_upper, stay, from_lower, weight)


def piece_rows(rows, count):
    return -(-rows // (16 * count)) * 16


def tree(values):
    while len(values) > 1:
        values = [
            values[i] + values[i + 1] if i + 1 < len(values) else values[i]
            for i in range(0, len(values), 2)
        ]
    return values[0]


def cost(*arrays):
    moved = sum(math.prod(x.shape) * jnp.dtype(x.dtype).itemsize for x in arrays)
    return pl.CostEstimate(flops=moved, bytes_accessed=moved, transcendentals=0)


def shapes_of(count, shape):
    return [jax.ShapeDtypeStruct(shape, F32 if step == 0 else BF16) for step in range(count)]


def farthest_then_nearest(count):
    return [0, count - 1, *range(1, count - 1)]


def far_first(count):
    return [0, *range(count - 1, 0, -1)]


def pair_kernel(count, conv_ref, conv_got_ref, down_ref, down_got_ref, *outs):
    planes, slabs = outs[:count], outs[count:]
    shards, rows, _ = conv_ref.shape
    down_piece = down_ref.shape[1] // count
    piece = planes[0].shape[1] - down_piece
    cut = count * piece
    for step, ref in zip(farthest_then_nearest(shards), slabs):
        shard = relative(lax.axis_index("dp"), step, shards)
        total = conv_ref[shard, cut:, :].astype(F32) + conv_got_ref[shard, cut:, :].astype(F32)
        ref[...] = total.astype(ref.dtype)
    high = lax.axis_index("dom") // 2
    for step, ref in zip(far_first(count), planes):
        place = relative(high, step, count)
        for keep_ref, got_ref, size, start in (
            (conv_ref, conv_got_ref, piece, 0),
            (down_ref, down_got_ref, down_piece, piece),
        ):
            span = pl.ds(pl.multiple_of(place * size, 16), size)
            total = keep_ref[:, span, :].astype(F32) + got_ref[:, span, :].astype(F32)
            ref[:, start : start + size, :] = total.astype(ref.dtype)


def pair_sum(count, conv, conv_got, down, down_got):
    shards, rows, lanes = conv.shape
    down_piece = down.shape[1] // count
    unit = 16 * count
    piece = 16 * round((PLANE_FIRST * (rows + down.shape[1]) - down.shape[1]) / unit)
    outs = shapes_of(count, (shards, piece + down_piece, lanes))
    outs += shapes_of(shards, (rows - count * piece, lanes))
    outs = pl.pallas_call(
        functools.partial(pair_kernel, count),
        out_shape=outs,
        in_specs=[VMEM] * 4,
        out_specs=[VMEM] * len(outs),
        compiler_params=params(32),
        cost_estimate=cost(conv, conv_got, *outs),
        name="pair_sum",
    )(conv, conv_got, down, down_got)
    return outs[:count], outs[count:], (piece, down_piece)


def middle_kernel(count, shards, *refs):
    planes, slabs = refs[:count], refs[count : count + shards]
    to_slabs, mine_ref = refs[count + shards : -1], refs[-1]
    mine_ref[...] = tree([part[...].astype(F32) for part in slabs]).astype(BF16)
    for step, ref in zip(far_first(shards), to_slabs):
        shard = relative(lax.axis_index("dp"), step, shards)
        ref[...] = tree([part[shard].astype(F32) for part in planes]).astype(ref.dtype)


def middle_sum(planes, slabs):
    count, shards = len(planes), len(slabs)
    _, piece, lanes = planes[0].shape
    outs = shapes_of(shards, (piece, lanes)) + [jax.ShapeDtypeStruct(slabs[0].shape, BF16)]
    parts = [*planes, *slabs]
    outs = pl.pallas_call(
        functools.partial(middle_kernel, count, shards),
        out_shape=outs,
        in_specs=[VMEM] * len(parts),
        out_specs=[VMEM] * len(outs),
        compiler_params=params(32),
        cost_estimate=cost(*parts, *outs),
        name="middle_sum",
    )(*parts)
    return outs[:shards], outs[shards]


def last_kernel(factor, shards, *refs):
    *refs, _, planes_ref, slabs_ref = refs
    total = tree([part[...].astype(F32) for part in refs[:shards]])
    planes_ref[...] = (total * factor).astype(BF16)
    total = tree([part[...].astype(F32) for part in refs[shards:]])
    slabs_ref[...] = (total * factor).astype(BF16)


def last_sum(factor, slabs, planes, after):
    parts = [*slabs, *planes]
    return pl.pallas_call(
        functools.partial(last_kernel, factor, len(slabs)),
        out_shape=[
            jax.ShapeDtypeStruct(slabs[0].shape, BF16), jax.ShapeDtypeStruct(planes[0].shape, BF16)
        ],
        in_specs=[VMEM] * len(parts) + [HBM],
        out_specs=[VMEM] * 2,
        compiler_params=params(32),
        cost_estimate=cost(*parts),
        name="last_sum",
    )(*parts, in_hbm(after))


def gather_kernel(count, piece, down_piece, *refs):
    near, far = refs[:count], refs[count : 2 * count]
    rest_ref, rest_far_ref, conv_ref, down_ref, conv_whole, down_whole, sems = refs[2 * count :]
    lanes = rest_ref.shape[1]
    cut = count * piece
    high = lax.axis_index("dom") // 2
    low = lax.rem(lax.axis_index("dom"), 2)
    own = pl.ds(pl.multiple_of(low * lanes, lanes), lanes)
    other = pl.ds(pl.multiple_of((1 - low) * lanes, lanes), lanes)
    conv_whole[cut:, own] = rest_ref[...].astype(F32)
    conv_whole[cut:, other] = rest_far_ref[...].astype(F32)
    tail = pl.ds(cut, conv_ref.shape[0] - cut)
    copies = [started(conv_whole.at[tail], conv_ref.at[tail], sems.at[0])]
    for index, step in enumerate(far_first(count)):
        place = source_of(high, step, count)
        rows = pl.ds(pl.multiple_of(place * piece, 16), piece)
        down_rows = pl.ds(pl.multiple_of(place * down_piece, 16), down_piece)
        for lane, ref in ((own, near[index]), (other, far[index])):
            conv_whole[rows, lane] = ref[:piece, :].astype(F32)
            down_whole[down_rows, lane] = ref[piece:, :].astype(F32)
        copies.append(started(conv_whole.at[rows], conv_ref.at[rows], sems.at[index + 1]))
    copies.append(
        started(down_whole.at[pl.ds(0, down_ref.shape[0])], down_ref, sems.at[count + 1])
    )
    for copy in copies:
        copy.wait()


def gather_up(conv_rows, down_rows, pieces, near, far, rest, rest_far):
    count = len(near)
    lanes = rest.shape[1]
    outs = [jax.ShapeDtypeStruct((rows, 2 * lanes), F32) for rows in (conv_rows, down_rows)]
    return pl.pallas_call(
        functools.partial(gather_kernel, count, *pieces),
        out_shape=outs,
        in_specs=[VMEM] * (2 * count + 2),
        out_specs=[ANY] * 2,
        scratch_shapes=[
            pltpu.VMEM((conv_rows, 2 * lanes), F32),
            pltpu.VMEM((count * pieces[1], 2 * lanes), F32),
            pltpu.SemaphoreType.DMA((count + 2,)),
        ],
        compiler_params=params(32),
        cost_estimate=cost(*near, *far, *outs),
        name="gather_up",
    )(*near, *far, rest, rest_far)


def body(grad_out, pre_act, conv_weight, down_weight, fine_act, neighbours, octant_routes):
    own = grad_out[0]
    links = neighbours.transpose(1, 0, 2)
    routes = octant_routes.transpose(0, 2, 1, 3)[0]
    slots, voxels, channels = own.shape
    devices = lax.axis_size("dom")
    shards = lax.axis_size("dp")
    count = devices // 2
    factor = 1.0 / math.sqrt(shards * devices * slots * voxels)

    forward = [(i, i + 1) for i in range(devices - 1)]
    backward = [(i + 1, i) for i in range(devices - 1)]
    ring = [(i, (i + 1) % devices) for i in range(devices)]
    swap = [(i, i ^ 1) for i in range(devices)]

    def spread_out(parts, axis, stride, steps=None):
        steps = steps or list(range(len(parts)))
        return [parts[0]] + [
            exchange(part, axis, step, stride) for step, part in zip(steps[1:], parts[1:])
        ]

    low = lax.ppermute(own[:, voxels - PLANE :], "dom", forward)
    high = lax.ppermute(own[:, :PLANE], "dom", backward)
    own_wide, act, taps = prepare(grad_out, pre_act, conv_weight)
    to_lower, stay, to_upper, windows = input_gradient(
        links, routes, own_wide, low, high, pre_act, taps
    )
    from_upper = lax.ppermute(to_lower, "dom", [(b, a) for a, b in ring])
    from_lower = lax.ppermute(to_upper, "dom", ring)
    conv_keep, conv_send = filter_gradient(shards, windows, act)
    down_keep, down_send = down_gradient(
        shards, count, from_upper, stay, from_lower, down_weight.shape[0], fine_act[0]
    )
    fine_grad = fine_gradient(from_upper, stay, from_lower, down_weight)
    conv_got = lax.ppermute(conv_send, "dom", swap)
    down_got = lax.ppermute(down_send, "dom", swap)

    planes, slabs, pieces = pair_sum(count, conv_keep, conv_got, down_keep, down_got)
    slabs = spread_out(slabs, "dp", 1, farthest_then_nearest(shards))
    planes = spread_out(planes, "dom", 2, far_first(count))
    to_slabs, rest = middle_sum(planes, slabs)
    to_slabs = spread_out(to_slabs, "dp", 1, far_first(shards))
    mine, rest = last_sum(factor, to_slabs, spread_out([rest] * count, "dom", 2), fine_grad)
    near = spread_out([mine] * count, "dom", 2, far_first(count))
    far = [lax.ppermute(value, "dom", swap) for value in near]
    rest_far = lax.ppermute(rest, "dom", swap)
    conv_rows = 27 * channels // shards
    down_rows = down_weight.shape[0] * down_weight.shape[1] // shards
    conv_grad, down_grad = gather_up(conv_rows, down_rows, pieces, near, far, rest, rest_far)
    return (fine_grad[None], conv_grad, down_grad)


def solution(mesh):
    return jax.shard_map(
        body,
        mesh=mesh,
        in_specs=(
            P("dp", "dom", None, None),
            P("dp", "dom", None, None),
            P(),
            P(),
            P("dp", "dom", None, None),
            P("dp", "dom", None),
            P("dp", "dom", None, None),
        ),
        out_specs=(P("dp", "dom", None, None), P("dp", None), P("dp", None)),
        check_vma=False,
    )
```

```python
import functools
import math

import jax
import jax.numpy as jnp
from jax import lax
from jax.experimental import pallas as pl
from jax.experimental.pallas import tpu as pltpu
from jax.sharding import PartitionSpec as P

BE = 8
PLANE = BE * BE
HALF = BE // 2
F32 = jnp.float32
BF16 = jnp.bfloat16
MIB = 1 << 20
PLANE_FIRST = 0.7

VMEM = pl.BlockSpec(memory_space=pltpu.VMEM)
SMEM = pl.BlockSpec(memory_space=pltpu.SMEM)
ANY = pl.BlockSpec(memory_space=pl.ANY)
HBM = pl.BlockSpec(memory_space=pltpu.HBM)


def params(mib):
    return pltpu.CompilerParams(vmem_limit_bytes=int(mib * MIB))


def relative(index, step, count):
    if count & (count - 1) == 0:
        return index ^ step
    return lax.rem(index + step, count)


def source_of(index, step, count):
    if count & (count - 1) == 0:
        return index ^ step
    return (index - step) % count if isinstance(index, int) else lax.rem(index + count - step, count)


def exchange(value, axis, step, stride):
    count = lax.axis_size(axis) // stride
    pairs = []
    for index in range(lax.axis_size(axis)):
        high, low = divmod(index, stride)
        other = high ^ step if count & (count - 1) == 0 else (high + step) % count
        pairs.append((index, other * stride + low))
    return lax.ppermute(value, axis, pairs)


def in_hbm(value):
    return pltpu.with_memory_space_constraint(value, pltpu.HBM)


def started(source, target, sem):
    copy = pltpu.make_async_copy(source, target, sem)
    copy.start()
    return copy


GROUPS = (0, -1, 1)


def column_of(tap):
    _, rest = divmod(tap, 9)
    tap_y, tap_z = rest // 3 - 1, rest % 3 - 1
    return 3 * GROUPS.index(-tap_z) + tap_y + 1


def extend(ref, wide_ref):
    slots = ref.shape[0]
    wide_ref[:slots] = ref[...]
    wide_ref[slots] = jnp.zeros(ref.shape[1:], ref.dtype)


def spread(links_ref, ref, start, step_x, slot, row, shift, win_ref):
    channels = ref.shape[-1]
    empty = ref.shape[0] - 1

    def fetch(step_y, step_z, first, rows):
        found = links_ref[slot, 0, 9 * (step_x + 1) + 3 * (step_y + 1) + step_z + 1]
        place = jnp.where(found < 0, empty, found)
        return ref[place, start + first : start + first + rows, :].astype(F32)

    def column(step_z):
        below = fetch(-1, step_z, PLANE - 16, 16).reshape(2, BE, channels)[1:]
        middle = fetch(0, step_z, 0, PLANE).reshape(BE, BE, channels)
        above = fetch(1, step_z, 0, 16).reshape(2, BE, channels)[:1]
        return jnp.concatenate([below, middle, above], axis=0)

    value = column(0)
    if shift != 0:
        turn = 1 if shift < 0 else BE - 1
        edge = 0 if shift < 0 else BE - 1
        place_z = lax.broadcasted_iota(jnp.int32, value.shape, 1)
        value = jnp.where(
            place_z == edge,
            pltpu.roll(column(shift), turn, axis=1),
            pltpu.roll(value, turn, axis=1),
        )
    for tap_y in (-1, 0, 1):
        lane = (3 * GROUPS.index(shift) + tap_y + 1) * channels
        part = value[1 - tap_y : 1 - tap_y + BE].reshape(PLANE, channels)
        win_ref[row : row + PLANE, lane : lane + channels] = part.astype(BF16)


def builders(links_ref, own_ref, low_ref, high_ref, win_ref, shift):
    slots = own_ref.shape[0] - 1
    calls = []
    for plane in range(BE + 2):
        if plane == 0:
            ref, start, step_x = low_ref, 0, -1
        elif plane == BE + 1:
            ref, start, step_x = high_ref, 0, 1
        else:
            ref, start, step_x = own_ref, (plane - 1) * PLANE, 0
        for slot in range(slots):
            row = (plane * slots + slot) * PLANE
            calls.append(
                functools.partial(
                    spread, links_ref, ref, start, step_x, slot, row, shift, win_ref
                )
            )
    return calls


def interleave(first, second):
    done = 0
    for index, call in enumerate(first):
        call()
        until = len(second) * (index + 1) // len(first)
        for other in second[done:until]:
            other()
        done = until


def prepare_kernel(own_hbm, pre_hbm, weight_hbm, own_wide, act_ref, taps_ref, pre_ref, sems):
    _, slots, voxels, channels = own_hbm.shape
    slab = slots * PLANE
    pre_copy = started(pre_hbm.at[0], pre_ref, sems.at[27])
    copies = [started(own_hbm.at[0], own_wide.at[pl.ds(0, slots)], sems.at[28])]
    for tap in range(27):
        lanes = slice(column_of(tap) * channels, (column_of(tap) + 1) * channels)
        copies.append(started(weight_hbm.at[tap], taps_ref.at[tap // 9, :, lanes], sems.at[tap]))
    own_wide[slots] = jnp.zeros((voxels, channels), BF16)
    pre_copy.wait()
    for pair in range(BE // 2):
        parts = []
        for x in (2 * pair, 2 * pair + 1):
            for slot in range(slots):
                parts.append(pre_ref[slot, x * PLANE : (x + 1) * PLANE, :])
        block = jnp.maximum(jnp.concatenate(parts, axis=0).astype(F32), 0.0)
        act_ref[:, pair * 2 * slab : (pair + 1) * 2 * slab] = block.T.astype(BF16)
    for copy in copies:
        copy.wait()


def prepare(own, pre, weight):
    _, slots, voxels, channels = own.shape
    return pl.pallas_call(
        prepare_kernel,
        out_shape=(
            jax.ShapeDtypeStruct((slots + 1, voxels, channels), BF16),
            jax.ShapeDtypeStruct((channels, slots * voxels), BF16),
            jax.ShapeDtypeStruct((3, channels, 9 * channels), BF16),
        ),
        in_specs=[HBM] * 3,
        out_specs=[VMEM] * 3,
        scratch_shapes=[
            pltpu.VMEM((slots, voxels, channels), BF16),
            pltpu.SemaphoreType.DMA((29,)),
        ],
        compiler_params=params(24),
        cost_estimate=pl.CostEstimate(
            flops=4 * MIB, bytes_accessed=12 * MIB, transcendentals=0
        ),
        name="prepare",
    )(in_hbm(own), in_hbm(pre), in_hbm(weight))


def input_kernel(
    links_ref, routes_ref, own_wide, low_ref, high_ref, pre_hbm, taps_ref,
    to_lower_ref, stay_ref, to_upper_ref, win_ref,
    low_wide, high_wide, acc_ref, octants_ref, pre_ref, out_sems, pre_sem,
):
    slots, voxels, channels = pre_ref.shape
    groups = routes_ref.shape[-1] // 8
    pre_copy = started(pre_hbm.at[0], pre_ref, pre_sem)
    for ref, wide in ((low_ref, low_wide), (high_ref, high_wide)):
        extend(ref, wide)
    octants_ref[...] = jnp.zeros_like(octants_ref)
    slab = slots * PLANE
    rows = BE * slab
    part = rows // 2

    def product(group, start):
        lanes = slice(3 * group * channels, 3 * (group + 1) * channels)
        total = None
        for index_x in range(3):
            offset = start + (2 - index_x) * slab
            term = lax.dot_general(
                win_ref[offset : offset + part, lanes],
                taps_ref[index_x, :, lanes],
                (((1,), (1,)), ((), ())),
                preferred_element_type=F32,
            )
            total = term if total is None else total + term
        if group > 0:
            total = total + acc_ref[start : start + part, :]
        acc_ref[start : start + part, :] = total

    def products(group):
        return [functools.partial(product, group, start) for start in range(0, rows, part)]

    sources = (links_ref, own_wide, low_wide, high_wide, win_ref)
    for call in builders(*sources, GROUPS[0]):
        call()
    interleave(products(0), builders(*sources, GROUPS[1]))
    interleave(products(1), builders(*sources, GROUPS[2]))
    for call in products(2):
        call()
    pre_copy.wait()

    place_z = lax.broadcasted_iota(jnp.int32, (BE // 2, BE, channels), 1)
    for slot in range(slots):
        group = jnp.int32(3 * groups)
        for row in range(3):
            for place in range(groups):
                group = jnp.where(
                    routes_ref[row, 0, 8 * place] == 8 * slot, row * groups + place, group
                )

        def finish(x, carry):
            value = acc_ref[pl.ds(pl.multiple_of(x * slab + slot * PLANE, PLANE), PLANE), :]
            pre = pre_ref[slot, pl.ds(pl.multiple_of(x * PLANE, PLANE), PLANE), :].astype(F32)
            value = jnp.where(pre > 0, value, 0.0).reshape(BE // 2, 2, BE, channels)
            even, odd = value[:, 0], value[:, 1]
            near = jnp.where(place_z < HALF, even, pltpu.roll(odd, HALF, axis=1))
            far = jnp.where(place_z < HALF, pltpu.roll(even, HALF, axis=1), odd)
            side = x // HALF
            row = (x - side * HALF) * 16
            for side_y in range(2):
                for side_z, piece in enumerate((near, far)):
                    block = piece[2 * side_y : 2 * side_y + 2].reshape(16, channels).astype(BF16)
                    start = (4 * side + 2 * side_y + side_z) * PLANE + row
                    octants_ref[group, pl.ds(pl.multiple_of(start, 16), 16), :] = block
            return carry

        lax.fori_loop(0, BE, finish, 0)
    outs = []
    for row, ref in enumerate((to_lower_ref, stay_ref, to_upper_ref)):
        outs.append(started(octants_ref.at[pl.ds(row * groups, groups)], ref, out_sems.at[row]))
    for copy in outs:
        copy.wait()


def input_gradient(links, routes, own_wide, low, high, pre, taps):
    _, slots, voxels, channels = pre.shape
    groups = routes.shape[-1] // 8
    rows = slots * voxels
    out = jax.ShapeDtypeStruct((groups, voxels, channels), BF16)
    windows = jax.ShapeDtypeStruct((slots * PLANE * (BE + 2), 9 * channels), BF16)
    return pl.pallas_call(
        input_kernel,
        out_shape=(out, out, out, windows),
        in_specs=[SMEM, SMEM, VMEM, VMEM, VMEM, HBM, VMEM],
        out_specs=(ANY, ANY, ANY, VMEM),
        scratch_shapes=[
            pltpu.VMEM((slots + 1, *low.shape[1:]), BF16),
            pltpu.VMEM((slots + 1, *low.shape[1:]), BF16),
            pltpu.VMEM((rows, channels), F32),
            pltpu.VMEM((3 * groups + 1, voxels, channels), BF16),
            pltpu.VMEM((slots, voxels, channels), BF16),
            pltpu.SemaphoreType.DMA((3,)),
            pltpu.SemaphoreType.DMA,
        ],
        compiler_params=params(20),
        cost_estimate=pl.CostEstimate(
            flops=2 * rows * 27 * channels * channels, bytes_accessed=8 * MIB, transcendentals=0
        ),
        name="input_gradient",
    )(links, routes, own_wide, low, high, in_hbm(pre), taps)


def filter_kernel(
    shard_rows, win_ref, act_ref, keep_ref, send_ref
):
    channels, rows = act_ref.shape
    slab = rows // BE
    lanes = channels // 2
    first = lax.rem(lax.axis_index("dom"), 2) == 0
    unit = math.gcd(channels, shard_rows)

    def product(tap):
        offset = (2 - tap // 9) * slab
        column = column_of(tap) * channels
        total = jnp.dot(
            act_ref[...],
            win_ref[offset : offset + rows, column : column + channels],
            preferred_element_type=F32,
        )
        left, right = total[:, :lanes], total[:, lanes:]
        keep = jnp.where(first, left, right).astype(BF16)
        send = jnp.where(first, right, left).astype(BF16)
        for part in range(channels // unit):
            shard, start = divmod(tap * channels + part * unit, shard_rows)
            span = slice(part * unit, (part + 1) * unit)
            keep_ref[shard, start : start + unit, :] = keep[span]
            send_ref[shard, start : start + unit, :] = send[span]

    for tap in sorted(range(27), key=column_of):
        product(tap)


def filter_gradient(shards, windows, act):
    channels, rows = act.shape
    shard_rows = 27 * channels // shards
    out = jax.ShapeDtypeStruct((shards, shard_rows, channels // 2), BF16)
    return pl.pallas_call(
        functools.partial(filter_kernel, shard_rows),
        out_shape=(out, out),
        in_specs=[VMEM, VMEM],
        out_specs=(VMEM, VMEM),
        compiler_params=params(12),
        cost_estimate=pl.CostEstimate(
            flops=2 * rows * 27 * channels * channels, bytes_accessed=8 * MIB, transcendentals=0
        ),
        name="filter_gradient",
    )(windows, act)


def down_kernel(
    groups, upper_ref, stay_ref, lower_ref, act_ref, keep_ref, send_ref, acc_ref
):
    step = pl.program_id(0)
    fine = act_ref.shape[0]
    channels = upper_ref.shape[-1]
    cells = upper_ref.shape[1] // fine
    taps = act_ref.shape[1] // cells

    @pl.when(step == 0)
    def _():
        acc_ref[...] = jnp.zeros_like(acc_ref)

    def work(ref):
        wide = []
        for place in range(fine):
            wide.append(
                jnp.concatenate(
                    [act_ref[place, tap * cells : (tap + 1) * cells, :] for tap in range(taps)],
                    axis=1,
                )
            )
        acc_ref[...] += jnp.dot(
            ref[0].T, jnp.concatenate(wide, axis=0), preferred_element_type=F32
        )

    for row, ref in enumerate((upper_ref, stay_ref, lower_ref)):
        pl.when(step // groups == row)(functools.partial(work, ref))

    @pl.when(step == pl.num_programs(0) - 1)
    def _():
        total = acc_ref[...].T
        first = lax.rem(lax.axis_index("dom"), 2) == 0
        lanes = channels // 2
        shards = keep_ref.shape[0]
        rows = total.shape[0] // shards
        left = total[:, :lanes].reshape(shards, rows, lanes)
        right = total[:, lanes:].reshape(shards, rows, lanes)
        keep_ref[:, :rows, :] = jnp.where(first, left, right).astype(BF16)
        send_ref[:, :rows, :] = jnp.where(first, right, left).astype(BF16)


def down_gradient(shards, count, from_upper, stay, from_lower, taps, fine_act):
    fine, voxels, fine_channels = fine_act.shape
    groups, _, channels = stay.shape
    whole = pl.BlockSpec((1, voxels, channels), lambda i: (i % groups, 0, 0))
    rows = count * piece_rows(taps * fine_channels // shards, count)
    down = jax.ShapeDtypeStruct((shards, rows, channels // 2), BF16)
    same = pl.BlockSpec(down.shape, lambda i: (0, 0, 0))
    return pl.pallas_call(
        functools.partial(down_kernel, groups),
        grid=(3 * groups,),
        out_shape=(down, down),
        in_specs=[
            whole, whole, whole, pl.BlockSpec((8, voxels, fine_channels), lambda i: (i, 0, 0))
        ],
        out_specs=(same, same),
        scratch_shapes=[pltpu.VMEM((channels, taps * fine_channels), F32)],
        compiler_params=params(40),
        cost_estimate=pl.CostEstimate(
            flops=64 * fine * voxels * fine_channels * channels, bytes_accessed=8 * MIB,
            transcendentals=0,
        ),
        name="down_gradient",
    )(from_upper, stay, from_lower, fine_act)


def fine_kernel(groups, upper_ref, stay_ref, lower_ref, weight_ref, grad_ref):
    step = pl.program_id(0)
    taps, fine_channels, channels = weight_ref.shape
    fine, voxels, _ = grad_ref.shape
    cells = voxels // taps

    def work(ref):
        product = lax.dot_general(
            ref[0],
            weight_ref[...].reshape(taps * fine_channels, channels),
            (((1,), (1,)), ((), ())),
            preferred_element_type=F32,
        ).astype(BF16)
        for place in range(fine):
            for tap in range(taps):
                grad_ref[place, tap * cells : (tap + 1) * cells, :] = product[
                    place * cells : (place + 1) * cells,
                    tap * fine_channels : (tap + 1) * fine_channels,
                ]

    for row, ref in enumerate((upper_ref, stay_ref, lower_ref)):
        pl.when(step // groups == row)(functools.partial(work, ref))


def fine_gradient(from_upper, stay, from_lower, weight):
    groups, voxels, channels = stay.shape
    whole = pl.BlockSpec((1, voxels, channels), lambda i: (i % groups, 0, 0))
    return pl.pallas_call(
        functools.partial(fine_kernel, groups),
        grid=(3 * groups,),
        out_shape=jax.ShapeDtypeStruct((24 * groups, voxels, weight.shape[1]), BF16),
        in_specs=[whole, whole, whole, pl.BlockSpec(weight.shape, lambda i: (0, 0, 0))],
        out_specs=pl.BlockSpec((8, voxels, weight.shape[1]), lambda i: (i, 0, 0)),
        compiler_params=params(40),
        cost_estimate=pl.CostEstimate(
            flops=2 * 24 * groups * voxels * weight.shape[1] * channels, bytes_accessed=4 * MIB,
            transcendentals=0,
        ),
        name="fine_gradient",
    )(from_upper, stay, from_lower, weight)


def piece_rows(rows, count):
    return -(-rows // (16 * count)) * 16


def tree(values):
    while len(values) > 1:
        values = [
            values[i] + values[i + 1] if i + 1 < len(values) else values[i]
            for i in range(0, len(values), 2)
        ]
    return values[0]


def cost(*arrays):
    moved = sum(math.prod(x.shape) * jnp.dtype(x.dtype).itemsize for x in arrays)
    return pl.CostEstimate(flops=moved, bytes_accessed=moved, transcendentals=0)


def shapes_of(count, shape):
    return [jax.ShapeDtypeStruct(shape, F32 if step == 0 else BF16) for step in range(count)]


def farthest_then_nearest(count):
    return [0, count - 1, *range(1, count - 1)]


def far_first(count):
    return [0, *range(count - 1, 0, -1)]


def pair_kernel(count, conv_ref, conv_got_ref, down_ref, down_got_ref, *outs):
    planes, slabs = outs[:count], outs[count:]
    shards, rows, _ = conv_ref.shape
    down_piece = down_ref.shape[1] // count
    piece = planes[0].shape[1] - down_piece
    cut = count * piece
    for step, ref in zip(farthest_then_nearest(shards), slabs):
        shard = relative(lax.axis_index("dp"), step, shards)
        total = conv_ref[shard, cut:, :].astype(F32) + conv_got_ref[shard, cut:, :].astype(F32)
        ref[...] = total.astype(ref.dtype)
    high = lax.axis_index("dom") // 2
    for step, ref in zip(far_first(count), planes):
        place = relative(high, step, count)
        for keep_ref, got_ref, size, start in (
            (conv_ref, conv_got_ref, piece, 0),
            (down_ref, down_got_ref, down_piece, piece),
        ):
            span = pl.ds(pl.multiple_of(place * size, 16), size)
            total = keep_ref[:, span, :].astype(F32) + got_ref[:, span, :].astype(F32)
            ref[:, start : start + size, :] = total.astype(ref.dtype)


def pair_sum(count, conv, conv_got, down, down_got):
    shards, rows, lanes = conv.shape
    down_piece = down.shape[1] // count
    unit = 16 * count
    piece = 16 * round((PLANE_FIRST * (rows + down.shape[1]) - down.shape[1]) / unit)
    outs = shapes_of(count, (shards, piece + down_piece, lanes))
    outs += shapes_of(shards, (rows - count * piece, lanes))
    outs = pl.pallas_call(
        functools.partial(pair_kernel, count),
        out_shape=outs,
        in_specs=[VMEM] * 4,
        out_specs=[VMEM] * len(outs),
        compiler_params=params(32),
        cost_estimate=cost(conv, conv_got, *outs),
        name="pair_sum",
    )(conv, conv_got, down, down_got)
    return outs[:count], outs[count:], (piece, down_piece)


def middle_kernel(count, shards, *refs):
    planes, slabs = refs[:count], refs[count : count + shards]
    to_slabs, mine_ref = refs[count + shards : -1], refs[-1]
    mine_ref[...] = tree([part[...].astype(F32) for part in slabs]).astype(BF16)
    for step, ref in zip(far_first(shards), to_slabs):
        shard = relative(lax.axis_index("dp"), step, shards)
        ref[...] = tree([part[shard].astype(F32) for part in planes]).astype(ref.dtype)


def middle_sum(planes, slabs):
    count, shards = len(planes), len(slabs)
    _, piece, lanes = planes[0].shape
    outs = shapes_of(shards, (piece, lanes)) + [jax.ShapeDtypeStruct(slabs[0].shape, BF16)]
    parts = [*planes, *slabs]
    outs = pl.pallas_call(
        functools.partial(middle_kernel, count, shards),
        out_shape=outs,
        in_specs=[VMEM] * len(parts),
        out_specs=[VMEM] * len(outs),
        compiler_params=params(32),
        cost_estimate=cost(*parts, *outs),
        name="middle_sum",
    )(*parts)
    return outs[:shards], outs[shards]


def last_kernel(factor, count, *refs):
    *refs, _, planes_ref, slabs_ref = refs
    total = tree([part[...].astype(F32) for part in refs[count:]])
    planes_ref[...] = (total * factor).astype(BF16)
    steps = far_first(count)
    total = tree([refs[steps.index(step)][...].astype(F32) for step in range(count)])
    slabs_ref[...] = (total * factor).astype(BF16)


def last_sum(factor, slabs, planes, after):
    parts = [*planes, *slabs]
    return pl.pallas_call(
        functools.partial(last_kernel, factor, len(planes)),
        out_shape=[
            jax.ShapeDtypeStruct(slabs[0].shape, BF16), jax.ShapeDtypeStruct(planes[0].shape, BF16)
        ],
        in_specs=[VMEM] * len(parts) + [HBM],
        out_specs=[VMEM] * 2,
        compiler_params=params(32),
        cost_estimate=cost(*parts),
        name="last_sum",
    )(*parts, in_hbm(after))


def gather_kernel(count, piece, down_piece, *refs):
    near, far = refs[:count], refs[count : 2 * count]
    rest_ref, rest_far_ref, conv_ref, down_ref, conv_whole, down_whole, sems = refs[2 * count :]
    lanes = rest_ref.shape[1]
    cut = count * piece
    high = lax.axis_index("dom") // 2
    low = lax.rem(lax.axis_index("dom"), 2)
    own = pl.ds(pl.multiple_of(low * lanes, lanes), lanes)
    other = pl.ds(pl.multiple_of((1 - low) * lanes, lanes), lanes)
    conv_whole[cut:, own] = rest_ref[...].astype(F32)
    conv_whole[cut:, other] = rest_far_ref[...].astype(F32)
    tail = pl.ds(cut, conv_ref.shape[0] - cut)
    copies = [started(conv_whole.at[tail], conv_ref.at[tail], sems.at[0])]
    for index, step in enumerate(far_first(count)):
        place = source_of(high, step, count)
        rows = pl.ds(pl.multiple_of(place * piece, 16), piece)
        down_rows = pl.ds(pl.multiple_of(place * down_piece, 16), down_piece)
        for lane, ref in ((own, near[index]), (other, far[index])):
            conv_whole[rows, lane] = ref[:piece, :].astype(F32)
            down_whole[down_rows, lane] = ref[piece:, :].astype(F32)
        copies.append(started(conv_whole.at[rows], conv_ref.at[rows], sems.at[index + 1]))
    copies.append(
        started(down_whole.at[pl.ds(0, down_ref.shape[0])], down_ref, sems.at[count + 1])
    )
    for copy in copies:
        copy.wait()


def gather_up(conv_rows, down_rows, pieces, near, far, rest, rest_far):
    count = len(near)
    lanes = rest.shape[1]
    outs = [jax.ShapeDtypeStruct((rows, 2 * lanes), F32) for rows in (conv_rows, down_rows)]
    return pl.pallas_call(
        functools.partial(gather_kernel, count, *pieces),
        out_shape=outs,
        in_specs=[VMEM] * (2 * count + 2),
        out_specs=[ANY] * 2,
        scratch_shapes=[
            pltpu.VMEM((conv_rows, 2 * lanes), F32),
            pltpu.VMEM((count * pieces[1], 2 * lanes), F32),
            pltpu.SemaphoreType.DMA((count + 2,)),
        ],
        compiler_params=params(32),
        cost_estimate=cost(*near, *far, *outs),
        name="gather_up",
    )(*near, *far, rest, rest_far)


def body(grad_out, pre_act, conv_weight, down_weight, fine_act, neighbours, octant_routes):
    own = grad_out[0]
    links = neighbours.transpose(1, 0, 2)
    routes = octant_routes.transpose(0, 2, 1, 3)[0]
    slots, voxels, channels = own.shape
    devices = lax.axis_size("dom")
    shards = lax.axis_size("dp")
    count = devices // 2
    factor = 1.0 / math.sqrt(shards * devices * slots * voxels)

    forward = [(i, i + 1) for i in range(devices - 1)]
    backward = [(i + 1, i) for i in range(devices - 1)]
    ring = [(i, (i + 1) % devices) for i in range(devices)]
    swap = [(i, i ^ 1) for i in range(devices)]

    def spread_out(parts, axis, stride, steps=None):
        steps = steps or list(range(len(parts)))
        return [parts[0]] + [
            exchange(part, axis, step, stride) for step, part in zip(steps[1:], parts[1:])
        ]

    low = lax.ppermute(own[:, voxels - PLANE :], "dom", forward)
    high = lax.ppermute(own[:, :PLANE], "dom", backward)
    own_wide, act, taps = prepare(grad_out, pre_act, conv_weight)
    to_lower, stay, to_upper, windows = input_gradient(
        links, routes, own_wide, low, high, pre_act, taps
    )
    from_upper = lax.ppermute(to_lower, "dom", [(b, a) for a, b in ring])
    from_lower = lax.ppermute(to_upper, "dom", ring)
    conv_keep, conv_send = filter_gradient(shards, windows, act)
    down_keep, down_send = down_gradient(
        shards, count, from_upper, stay, from_lower, down_weight.shape[0], fine_act[0]
    )
    fine_grad = fine_gradient(from_upper, stay, from_lower, down_weight)
    conv_got = lax.ppermute(conv_send, "dom", swap)
    down_got = lax.ppermute(down_send, "dom", swap)

    planes, slabs, pieces = pair_sum(count, conv_keep, conv_got, down_keep, down_got)
    slabs = spread_out(slabs, "dp", 1, farthest_then_nearest(shards))
    planes = spread_out(planes, "dom", 2, far_first(count))
    to_slabs, rest = middle_sum(planes, slabs)
    to_slabs = spread_out(to_slabs, "dp", 1, far_first(shards))
    mine, rest = last_sum(factor, to_slabs, spread_out([rest] * count, "dom", 2, far_first(count)), fine_grad)
    near = spread_out([mine] * count, "dom", 2, far_first(count))
    far = [lax.ppermute(value, "dom", swap) for value in near]
    rest_far = lax.ppermute(rest, "dom", swap)
    conv_rows = 27 * channels // shards
    down_rows = down_weight.shape[0] * down_weight.shape[1] // shards
    conv_grad, down_grad = gather_up(conv_rows, down_rows, pieces, near, far, rest, rest_far)
    return (fine_grad[None], conv_grad, down_grad)


def solution(mesh):
    return jax.shard_map(
        body,
        mesh=mesh,
        in_specs=(
            P("dp", "dom", None, None),
            P("dp", "dom", None, None),
            P(),
            P(),
            P("dp", "dom", None, None),
            P("dp", "dom", None),
            P("dp", "dom", None, None),
        ),
        out_specs=(P("dp", "dom", None, None), P("dp", None), P("dp", None)),
        check_vma=False,
    )
```

```python
import functools
import math

import jax
import jax.numpy as jnp
from jax import lax
from jax.experimental import pallas as pl
from jax.experimental.pallas import tpu as pltpu
from jax.sharding import PartitionSpec as P

BE = 8
PLANE = BE * BE
HALF = BE // 2
F32 = jnp.float32
BF16 = jnp.bfloat16
MIB = 1 << 20
PLANE_FIRST = 0.7

VMEM = pl.BlockSpec(memory_space=pltpu.VMEM)
SMEM = pl.BlockSpec(memory_space=pltpu.SMEM)
ANY = pl.BlockSpec(memory_space=pl.ANY)
HBM = pl.BlockSpec(memory_space=pltpu.HBM)


def params(mib):
    return pltpu.CompilerParams(vmem_limit_bytes=int(mib * MIB))


def relative(index, step, count):
    if count & (count - 1) == 0:
        return index ^ step
    return lax.rem(index + step, count)


def source_of(index, step, count):
    if count & (count - 1) == 0:
        return index ^ step
    return (index - step) % count if isinstance(index, int) else lax.rem(index + count - step, count)


def exchange(value, axis, step, stride):
    count = lax.axis_size(axis) // stride
    pairs = []
    for index in range(lax.axis_size(axis)):
        high, low = divmod(index, stride)
        other = high ^ step if count & (count - 1) == 0 else (high + step) % count
        pairs.append((index, other * stride + low))
    return lax.ppermute(value, axis, pairs)


def in_hbm(value):
    return pltpu.with_memory_space_constraint(value, pltpu.HBM)


def started(source, target, sem):
    copy = pltpu.make_async_copy(source, target, sem)
    copy.start()
    return copy


GROUPS = (0, -1, 1)


def column_of(tap):
    _, rest = divmod(tap, 9)
    tap_y, tap_z = rest // 3 - 1, rest % 3 - 1
    return 3 * GROUPS.index(-tap_z) + tap_y + 1


def extend(ref, wide_ref):
    slots = ref.shape[0]
    wide_ref[:slots] = ref[...]
    wide_ref[slots] = jnp.zeros(ref.shape[1:], ref.dtype)


def spread(links_ref, ref, start, step_x, slot, row, shift, win_ref):
    channels = ref.shape[-1]
    empty = ref.shape[0] - 1

    def fetch(step_y, step_z, first, rows):
        found = links_ref[slot, 0, 9 * (step_x + 1) + 3 * (step_y + 1) + step_z + 1]
        place = jnp.where(found < 0, empty, found)
        return ref[place, start + first : start + first + rows, :].astype(F32)

    def column(step_z):
        below = fetch(-1, step_z, PLANE - 16, 16).reshape(2, BE, channels)[1:]
        middle = fetch(0, step_z, 0, PLANE).reshape(BE, BE, channels)
        above = fetch(1, step_z, 0, 16).reshape(2, BE, channels)[:1]
        return jnp.concatenate([below, middle, above], axis=0)

    value = column(0)
    if shift != 0:
        turn = 1 if shift < 0 else BE - 1
        edge = 0 if shift < 0 else BE - 1
        place_z = lax.broadcasted_iota(jnp.int32, value.shape, 1)
        value = jnp.where(
            place_z == edge,
            pltpu.roll(column(shift), turn, axis=1),
            pltpu.roll(value, turn, axis=1),
        )
    for tap_y in (-1, 0, 1):
        lane = (3 * GROUPS.index(shift) + tap_y + 1) * channels
        part = value[1 - tap_y : 1 - tap_y + BE].reshape(PLANE, channels)
        win_ref[row : row + PLANE, lane : lane + channels] = part.astype(BF16)


def builders(links_ref, own_ref, low_ref, high_ref, win_ref, shift):
    slots = own_ref.shape[0] - 1
    calls = []
    for plane in range(BE + 2):
        if plane == 0:
            ref, start, step_x = low_ref, 0, -1
        elif plane == BE + 1:
            ref, start, step_x = high_ref, 0, 1
        else:
            ref, start, step_x = own_ref, (plane - 1) * PLANE, 0
        for slot in range(slots):
            row = (plane * slots + slot) * PLANE
            calls.append(
                functools.partial(
                    spread, links_ref, ref, start, step_x, slot, row, shift, win_ref
                )
            )
    return calls


def interleave(first, second):
    done = 0
    for index, call in enumerate(first):
        call()
        until = len(second) * (index + 1) // len(first)
        for other in second[done:until]:
            other()
        done = until


def prepare_kernel(own_hbm, pre_hbm, weight_hbm, own_wide, act_ref, taps_ref, pre_ref, sems):
    _, slots, voxels, channels = own_hbm.shape
    slab = slots * PLANE
    pre_copy = started(pre_hbm.at[0], pre_ref, sems.at[27])
    copies = [started(own_hbm.at[0], own_wide.at[pl.ds(0, slots)], sems.at[28])]
    for tap in range(27):
        lanes = slice(column_of(tap) * channels, (column_of(tap) + 1) * channels)
        copies.append(started(weight_hbm.at[tap], taps_ref.at[tap // 9, :, lanes], sems.at[tap]))
    own_wide[slots] = jnp.zeros((voxels, channels), BF16)
    pre_copy.wait()
    for pair in range(BE // 2):
        parts = []
        for x in (2 * pair, 2 * pair + 1):
            for slot in range(slots):
                parts.append(pre_ref[slot, x * PLANE : (x + 1) * PLANE, :])
        block = jnp.maximum(jnp.concatenate(parts, axis=0).astype(F32), 0.0)
        act_ref[:, pair * 2 * slab : (pair + 1) * 2 * slab] = block.T.astype(BF16)
    for copy in copies:
        copy.wait()


def prepare(own, pre, weight):
    _, slots, voxels, channels = own.shape
    return pl.pallas_call(
        prepare_kernel,
        out_shape=(
            jax.ShapeDtypeStruct((slots + 1, voxels, channels), BF16),
            jax.ShapeDtypeStruct((channels, slots * voxels), BF16),
            jax.ShapeDtypeStruct((3, channels, 9 * channels), BF16),
        ),
        in_specs=[HBM] * 3,
        out_specs=[VMEM] * 3,
        scratch_shapes=[
            pltpu.VMEM((slots, voxels, channels), BF16),
            pltpu.SemaphoreType.DMA((29,)),
        ],
        compiler_params=params(24),
        cost_estimate=pl.CostEstimate(
            flops=4 * MIB, bytes_accessed=12 * MIB, transcendentals=0
        ),
        name="prepare",
    )(in_hbm(own), in_hbm(pre), in_hbm(weight))


def input_kernel(
    links_ref, routes_ref, own_wide, low_ref, high_ref, pre_hbm, taps_ref,
    to_lower_ref, stay_ref, to_upper_ref, win_ref,
    low_wide, high_wide, acc_ref, octants_ref, pre_ref, out_sems, pre_sem,
):
    slots, voxels, channels = pre_ref.shape
    groups = routes_ref.shape[-1] // 8
    pre_copy = started(pre_hbm.at[0], pre_ref, pre_sem)
    for ref, wide in ((low_ref, low_wide), (high_ref, high_wide)):
        extend(ref, wide)
    octants_ref[...] = jnp.zeros_like(octants_ref)
    slab = slots * PLANE
    rows = BE * slab
    part = rows // 2

    def product(group, start):
        lanes = slice(3 * group * channels, 3 * (group + 1) * channels)
        total = None
        for index_x in range(3):
            offset = start + (2 - index_x) * slab
            term = lax.dot_general(
                win_ref[offset : offset + part, lanes],
                taps_ref[index_x, :, lanes],
                (((1,), (1,)), ((), ())),
                preferred_element_type=F32,
            )
            total = term if total is None else total + term
        if group > 0:
            total = total + acc_ref[start : start + part, :]
        acc_ref[start : start + part, :] = total

    def products(group):
        return [functools.partial(product, group, start) for start in range(0, rows, part)]

    sources = (links_ref, own_wide, low_wide, high_wide, win_ref)
    place_z = lax.broadcasted_iota(jnp.int32, (BE // 2, BE, channels), 1)
    targets = []
    for slot in range(slots):
        group = jnp.int32(3 * groups)
        for row in range(3):
            for place in range(groups):
                group = jnp.where(
                    routes_ref[row, 0, 8 * place] == 8 * slot, row * groups + place, group
                )
        targets.append(group)

    def finish(x, slot):
        start = x * slab + slot * PLANE
        value = acc_ref[start : start + PLANE, :]
        pre = pre_ref[slot, x * PLANE : (x + 1) * PLANE, :].astype(F32)
        value = jnp.where(pre > 0, value, 0.0).reshape(BE // 2, 2, BE, channels)
        even, odd = value[:, 0], value[:, 1]
        near = jnp.where(place_z < HALF, even, pltpu.roll(odd, HALF, axis=1))
        far = jnp.where(place_z < HALF, pltpu.roll(even, HALF, axis=1), odd)
        side, row = x // HALF, x % HALF * 16
        for side_y in range(2):
            for side_z, piece in enumerate((near, far)):
                block = piece[2 * side_y : 2 * side_y + 2].reshape(16, channels).astype(BF16)
                start = (4 * side + 2 * side_y + side_z) * PLANE + row
                octants_ref[targets[slot], start : start + 16, :] = block

    def finishes(planes):
        return [functools.partial(finish, x, slot) for x in planes for slot in range(slots)]

    for call in builders(*sources, GROUPS[0]):
        call()
    pre_copy.wait()
    interleave(products(0), builders(*sources, GROUPS[1]))
    interleave(products(1), builders(*sources, GROUPS[2]))
    last = products(2)
    last[0]()
    interleave(last[1:], finishes(range(HALF)))
    for call in finishes(range(HALF, BE)):
        call()
    outs = []
    for row, ref in enumerate((to_lower_ref, stay_ref, to_upper_ref)):
        outs.append(started(octants_ref.at[pl.ds(row * groups, groups)], ref, out_sems.at[row]))
    for copy in outs:
        copy.wait()


def input_gradient(links, routes, own_wide, low, high, pre, taps):
    _, slots, voxels, channels = pre.shape
    groups = routes.shape[-1] // 8
    rows = slots * voxels
    out = jax.ShapeDtypeStruct((groups, voxels, channels), BF16)
    windows = jax.ShapeDtypeStruct((slots * PLANE * (BE + 2), 9 * channels), BF16)
    return pl.pallas_call(
        input_kernel,
        out_shape=(out, out, out, windows),
        in_specs=[SMEM, SMEM, VMEM, VMEM, VMEM, HBM, VMEM],
        out_specs=(ANY, ANY, ANY, VMEM),
        scratch_shapes=[
            pltpu.VMEM((slots + 1, *low.shape[1:]), BF16),
            pltpu.VMEM((slots + 1, *low.shape[1:]), BF16),
            pltpu.VMEM((rows, channels), F32),
            pltpu.VMEM((3 * groups + 1, voxels, channels), BF16),
            pltpu.VMEM((slots, voxels, channels), BF16),
            pltpu.SemaphoreType.DMA((3,)),
            pltpu.SemaphoreType.DMA,
        ],
        compiler_params=params(20),
        cost_estimate=pl.CostEstimate(
            flops=2 * rows * 27 * channels * channels, bytes_accessed=8 * MIB, transcendentals=0
        ),
        name="input_gradient",
    )(links, routes, own_wide, low, high, in_hbm(pre), taps)


def filter_kernel(
    shard_rows, win_ref, act_ref, keep_ref, send_ref
):
    channels, rows = act_ref.shape
    slab = rows // BE
    lanes = channels // 2
    first = lax.rem(lax.axis_index("dom"), 2) == 0
    unit = math.gcd(channels, shard_rows)

    def product(tap):
        offset = (2 - tap // 9) * slab
        column = column_of(tap) * channels
        total = jnp.dot(
            act_ref[...],
            win_ref[offset : offset + rows, column : column + channels],
            preferred_element_type=F32,
        )
        left, right = total[:, :lanes], total[:, lanes:]
        keep = jnp.where(first, left, right).astype(BF16)
        send = jnp.where(first, right, left).astype(BF16)
        for part in range(channels // unit):
            shard, start = divmod(tap * channels + part * unit, shard_rows)
            span = slice(part * unit, (part + 1) * unit)
            keep_ref[shard, start : start + unit, :] = keep[span]
            send_ref[shard, start : start + unit, :] = send[span]

    for tap in sorted(range(27), key=column_of):
        product(tap)


def filter_gradient(shards, windows, act):
    channels, rows = act.shape
    shard_rows = 27 * channels // shards
    out = jax.ShapeDtypeStruct((shards, shard_rows, channels // 2), BF16)
    return pl.pallas_call(
        functools.partial(filter_kernel, shard_rows),
        out_shape=(out, out),
        in_specs=[VMEM, VMEM],
        out_specs=(VMEM, VMEM),
        compiler_params=params(12),
        cost_estimate=pl.CostEstimate(
            flops=2 * rows * 27 * channels * channels, bytes_accessed=8 * MIB, transcendentals=0
        ),
        name="filter_gradient",
    )(windows, act)


def down_kernel(
    groups, upper_ref, stay_ref, lower_ref, act_ref, keep_ref, send_ref, acc_ref
):
    step = pl.program_id(0)
    fine = act_ref.shape[0]
    channels = upper_ref.shape[-1]
    cells = upper_ref.shape[1] // fine
    taps = act_ref.shape[1] // cells

    @pl.when(step == 0)
    def _():
        acc_ref[...] = jnp.zeros_like(acc_ref)

    def work(ref):
        wide = []
        for place in range(fine):
            wide.append(
                jnp.concatenate(
                    [act_ref[place, tap * cells : (tap + 1) * cells, :] for tap in range(taps)],
                    axis=1,
                )
            )
        acc_ref[...] += jnp.dot(
            ref[0].T, jnp.concatenate(wide, axis=0), preferred_element_type=F32
        )

    for row, ref in enumerate((upper_ref, stay_ref, lower_ref)):
        pl.when(step // groups == row)(functools.partial(work, ref))

    @pl.when(step == pl.num_programs(0) - 1)
    def _():
        total = acc_ref[...].T
        first = lax.rem(lax.axis_index("dom"), 2) == 0
        lanes = channels // 2
        shards = keep_ref.shape[0]
        rows = total.shape[0] // shards
        left = total[:, :lanes].reshape(shards, rows, lanes)
        right = total[:, lanes:].reshape(shards, rows, lanes)
        keep_ref[:, :rows, :] = jnp.where(first, left, right).astype(BF16)
        send_ref[:, :rows, :] = jnp.where(first, right, left).astype(BF16)


def down_gradient(shards, count, from_upper, stay, from_lower, taps, fine_act):
    fine, voxels, fine_channels = fine_act.shape
    groups, _, channels = stay.shape
    whole = pl.BlockSpec((1, voxels, channels), lambda i: (i % groups, 0, 0))
    rows = count * piece_rows(taps * fine_channels // shards, count)
    down = jax.ShapeDtypeStruct((shards, rows, channels // 2), BF16)
    same = pl.BlockSpec(down.shape, lambda i: (0, 0, 0))
    return pl.pallas_call(
        functools.partial(down_kernel, groups),
        grid=(3 * groups,),
        out_shape=(down, down),
        in_specs=[
            whole, whole, whole, pl.BlockSpec((8, voxels, fine_channels), lambda i: (i, 0, 0))
        ],
        out_specs=(same, same),
        scratch_shapes=[pltpu.VMEM((channels, taps * fine_channels), F32)],
        compiler_params=params(40),
        cost_estimate=pl.CostEstimate(
            flops=64 * fine * voxels * fine_channels * channels, bytes_accessed=8 * MIB,
            transcendentals=0,
        ),
        name="down_gradient",
    )(from_upper, stay, from_lower, fine_act)


def fine_kernel(groups, upper_ref, stay_ref, lower_ref, weight_ref, grad_ref):
    step = pl.program_id(0)
    taps, fine_channels, channels = weight_ref.shape
    fine, voxels, _ = grad_ref.shape
    cells = voxels // taps

    def work(ref):
        product = lax.dot_general(
            ref[0],
            weight_ref[...].reshape(taps * fine_channels, channels),
            (((1,), (1,)), ((), ())),
            preferred_element_type=F32,
        ).astype(BF16)
        for place in range(fine):
            for tap in range(taps):
                grad_ref[place, tap * cells : (tap + 1) * cells, :] = product[
                    place * cells : (place + 1) * cells,
                    tap * fine_channels : (tap + 1) * fine_channels,
                ]

    for row, ref in enumerate((upper_ref, stay_ref, lower_ref)):
        pl.when(step // groups == row)(functools.partial(work, ref))


def fine_gradient(from_upper, stay, from_lower, weight):
    groups, voxels, channels = stay.shape
    whole = pl.BlockSpec((1, voxels, channels), lambda i: (i % groups, 0, 0))
    return pl.pallas_call(
        functools.partial(fine_kernel, groups),
        grid=(3 * groups,),
        out_shape=jax.ShapeDtypeStruct((24 * groups, voxels, weight.shape[1]), BF16),
        in_specs=[whole, whole, whole, pl.BlockSpec(weight.shape, lambda i: (0, 0, 0))],
        out_specs=pl.BlockSpec((8, voxels, weight.shape[1]), lambda i: (i, 0, 0)),
        compiler_params=params(40),
        cost_estimate=pl.CostEstimate(
            flops=2 * 24 * groups * voxels * weight.shape[1] * channels, bytes_accessed=4 * MIB,
            transcendentals=0,
        ),
        name="fine_gradient",
    )(from_upper, stay, from_lower, weight)


def piece_rows(rows, count):
    return -(-rows // (16 * count)) * 16


def tree(values):
    while len(values) > 1:
        values = [
            values[i] + values[i + 1] if i + 1 < len(values) else values[i]
            for i in range(0, len(values), 2)
        ]
    return values[0]


def cost(*arrays):
    moved = sum(math.prod(x.shape) * jnp.dtype(x.dtype).itemsize for x in arrays)
    return pl.CostEstimate(flops=moved, bytes_accessed=moved, transcendentals=0)


def shapes_of(count, shape):
    return [jax.ShapeDtypeStruct(shape, F32 if step == 0 else BF16) for step in range(count)]


def farthest_then_nearest(count):
    return [0, count - 1, *range(1, count - 1)]


def far_first(count):
    return [0, *range(count - 1, 0, -1)]


def pair_kernel(count, conv_ref, conv_got_ref, down_ref, down_got_ref, *outs):
    planes, slabs = outs[:count], outs[count:]
    shards, rows, _ = conv_ref.shape
    down_piece = down_ref.shape[1] // count
    piece = planes[0].shape[1] - down_piece
    cut = count * piece
    for step, ref in zip(farthest_then_nearest(shards), slabs):
        shard = relative(lax.axis_index("dp"), step, shards)
        total = conv_ref[shard, cut:, :].astype(F32) + conv_got_ref[shard, cut:, :].astype(F32)
        ref[...] = total.astype(ref.dtype)
    high = lax.axis_index("dom") // 2
    for step, ref in zip(far_first(count), planes):
        place = relative(high, step, count)
        for keep_ref, got_ref, size, start in (
            (conv_ref, conv_got_ref, piece, 0),
            (down_ref, down_got_ref, down_piece, piece),
        ):
            span = pl.ds(pl.multiple_of(place * size, 16), size)
            total = keep_ref[:, span, :].astype(F32) + got_ref[:, span, :].astype(F32)
            ref[:, start : start + size, :] = total.astype(ref.dtype)


def pair_sum(count, conv, conv_got, down, down_got):
    shards, rows, lanes = conv.shape
    down_piece = down.shape[1] // count
    unit = 16 * count
    piece = 16 * round((PLANE_FIRST * (rows + down.shape[1]) - down.shape[1]) / unit)
    outs = shapes_of(count, (shards, piece + down_piece, lanes))
    outs += shapes_of(shards, (rows - count * piece, lanes))
    outs = pl.pallas_call(
        functools.partial(pair_kernel, count),
        out_shape=outs,
        in_specs=[VMEM] * 4,
        out_specs=[VMEM] * len(outs),
        compiler_params=params(32),
        cost_estimate=cost(conv, conv_got, *outs),
        name="pair_sum",
    )(conv, conv_got, down, down_got)
    return outs[:count], outs[count:], (piece, down_piece)


def middle_kernel(count, shards, *refs):
    planes, slabs = refs[:count], refs[count : count + shards]
    to_slabs, mine_ref = refs[count + shards : -1], refs[-1]
    mine_ref[...] = tree([part[...].astype(F32) for part in slabs]).astype(BF16)
    for step, ref in zip(far_first(shards), to_slabs):
        shard = relative(lax.axis_index("dp"), step, shards)
        ref[...] = tree([part[shard].astype(F32) for part in planes]).astype(ref.dtype)


def middle_sum(planes, slabs):
    count, shards = len(planes), len(slabs)
    _, piece, lanes = planes[0].shape
    outs = shapes_of(shards, (piece, lanes)) + [jax.ShapeDtypeStruct(slabs[0].shape, BF16)]
    parts = [*planes, *slabs]
    outs = pl.pallas_call(
        functools.partial(middle_kernel, count, shards),
        out_shape=outs,
        in_specs=[VMEM] * len(parts),
        out_specs=[VMEM] * len(outs),
        compiler_params=params(32),
        cost_estimate=cost(*parts, *outs),
        name="middle_sum",
    )(*parts)
    return outs[:shards], outs[shards]


def last_kernel(factor, count, *refs):
    *refs, _, planes_ref, slabs_ref = refs
    total = tree([part[...].astype(F32) for part in refs[count:]])
    planes_ref[...] = (total * factor).astype(BF16)
    steps = far_first(count)
    total = tree([refs[steps.index(step)][...].astype(F32) for step in range(count)])
    slabs_ref[...] = (total * factor).astype(BF16)


def last_sum(factor, slabs, planes, after):
    parts = [*planes, *slabs]
    return pl.pallas_call(
        functools.partial(last_kernel, factor, len(planes)),
        out_shape=[
            jax.ShapeDtypeStruct(slabs[0].shape, BF16), jax.ShapeDtypeStruct(planes[0].shape, BF16)
        ],
        in_specs=[VMEM] * len(parts) + [HBM],
        out_specs=[VMEM] * 2,
        compiler_params=params(32),
        cost_estimate=cost(*parts),
        name="last_sum",
    )(*parts, in_hbm(after))


def gather_kernel(count, piece, down_piece, *refs):
    near, far = refs[:count], refs[count : 2 * count]
    rest_ref, rest_far_ref, conv_ref, down_ref, conv_whole, down_whole, sems = refs[2 * count :]
    lanes = rest_ref.shape[1]
    cut = count * piece
    high = lax.axis_index("dom") // 2
    low = lax.rem(lax.axis_index("dom"), 2)
    own = pl.ds(pl.multiple_of(low * lanes, lanes), lanes)
    other = pl.ds(pl.multiple_of((1 - low) * lanes, lanes), lanes)
    conv_whole[cut:, own] = rest_ref[...].astype(F32)
    conv_whole[cut:, other] = rest_far_ref[...].astype(F32)
    tail = pl.ds(cut, conv_ref.shape[0] - cut)
    copies = [started(conv_whole.at[tail], conv_ref.at[tail], sems.at[0])]
    for index, step in enumerate(far_first(count)):
        place = source_of(high, step, count)
        rows = pl.ds(pl.multiple_of(place * piece, 16), piece)
        down_rows = pl.ds(pl.multiple_of(place * down_piece, 16), down_piece)
        for lane, ref in ((own, near[index]), (other, far[index])):
            conv_whole[rows, lane] = ref[:piece, :].astype(F32)
            down_whole[down_rows, lane] = ref[piece:, :].astype(F32)
        copies.append(started(conv_whole.at[rows], conv_ref.at[rows], sems.at[index + 1]))
    copies.append(
        started(down_whole.at[pl.ds(0, down_ref.shape[0])], down_ref, sems.at[count + 1])
    )
    for copy in copies:
        copy.wait()


def gather_up(conv_rows, down_rows, pieces, near, far, rest, rest_far):
    count = len(near)
    lanes = rest.shape[1]
    outs = [jax.ShapeDtypeStruct((rows, 2 * lanes), F32) for rows in (conv_rows, down_rows)]
    return pl.pallas_call(
        functools.partial(gather_kernel, count, *pieces),
        out_shape=outs,
        in_specs=[VMEM] * (2 * count + 2),
        out_specs=[ANY] * 2,
        scratch_shapes=[
            pltpu.VMEM((conv_rows, 2 * lanes), F32),
            pltpu.VMEM((count * pieces[1], 2 * lanes), F32),
            pltpu.SemaphoreType.DMA((count + 2,)),
        ],
        compiler_params=params(32),
        cost_estimate=cost(*near, *far, *outs),
        name="gather_up",
    )(*near, *far, rest, rest_far)


def body(grad_out, pre_act, conv_weight, down_weight, fine_act, neighbours, octant_routes):
    own = grad_out[0]
    links = neighbours.transpose(1, 0, 2)
    routes = octant_routes.transpose(0, 2, 1, 3)[0]
    slots, voxels, channels = own.shape
    devices = lax.axis_size("dom")
    shards = lax.axis_size("dp")
    count = devices // 2
    factor = 1.0 / math.sqrt(shards * devices * slots * voxels)

    forward = [(i, i + 1) for i in range(devices - 1)]
    backward = [(i + 1, i) for i in range(devices - 1)]
    ring = [(i, (i + 1) % devices) for i in range(devices)]
    swap = [(i, i ^ 1) for i in range(devices)]

    def spread_out(parts, axis, stride, steps=None):
        steps = steps or list(range(len(parts)))
        return [parts[0]] + [
            exchange(part, axis, step, stride) for step, part in zip(steps[1:], parts[1:])
        ]

    low = lax.ppermute(own[:, voxels - PLANE :], "dom", forward)
    high = lax.ppermute(own[:, :PLANE], "dom", backward)
    own_wide, act, taps = prepare(grad_out, pre_act, conv_weight)
    to_lower, stay, to_upper, windows = input_gradient(
        links, routes, own_wide, low, high, pre_act, taps
    )
    from_upper = lax.ppermute(to_lower, "dom", [(b, a) for a, b in ring])
    from_lower = lax.ppermute(to_upper, "dom", ring)
    conv_keep, conv_send = filter_gradient(shards, windows, act)
    down_keep, down_send = down_gradient(
        shards, count, from_upper, stay, from_lower, down_weight.shape[0], fine_act[0]
    )
    fine_grad = fine_gradient(from_upper, stay, from_lower, down_weight)
    conv_got = lax.ppermute(conv_send, "dom", swap)
    down_got = lax.ppermute(down_send, "dom", swap)

    planes, slabs, pieces = pair_sum(count, conv_keep, conv_got, down_keep, down_got)
    slabs = spread_out(slabs, "dp", 1, farthest_then_nearest(shards))
    planes = spread_out(planes, "dom", 2, far_first(count))
    to_slabs, rest = middle_sum(planes, slabs)
    to_slabs = spread_out(to_slabs, "dp", 1, far_first(shards))
    mine, rest = last_sum(factor, to_slabs, spread_out([rest] * count, "dom", 2, far_first(count)), fine_grad)
    near = spread_out([mine] * count, "dom", 2, far_first(count))
    far = [lax.ppermute(value, "dom", swap) for value in near]
    rest_far = lax.ppermute(rest, "dom", swap)
    conv_rows = 27 * channels // shards
    down_rows = down_weight.shape[0] * down_weight.shape[1] // shards
    conv_grad, down_grad = gather_up(conv_rows, down_rows, pieces, near, far, rest, rest_far)
    return (fine_grad[None], conv_grad, down_grad)


def solution(mesh):
    return jax.shard_map(
        body,
        mesh=mesh,
        in_specs=(
            P("dp", "dom", None, None),
            P("dp", "dom", None, None),
            P(),
            P(),
            P("dp", "dom", None, None),
            P("dp", "dom", None),
            P("dp", "dom", None, None),
        ),
        out_specs=(P("dp", "dom", None, None), P("dp", None), P("dp", None)),
        check_vma=False,
    )
```

```python
import functools
import math

import jax
import jax.numpy as jnp
from jax import lax
from jax.experimental import pallas as pl
from jax.experimental.pallas import tpu as pltpu
from jax.sharding import PartitionSpec as P

BE = 8
PLANE = BE * BE
HALF = BE // 2
F32 = jnp.float32
BF16 = jnp.bfloat16
MIB = 1 << 20
PLANE_FIRST = 0.74

VMEM = pl.BlockSpec(memory_space=pltpu.VMEM)
SMEM = pl.BlockSpec(memory_space=pltpu.SMEM)
ANY = pl.BlockSpec(memory_space=pl.ANY)
HBM = pl.BlockSpec(memory_space=pltpu.HBM)


def params(mib):
    return pltpu.CompilerParams(vmem_limit_bytes=int(mib * MIB))


def relative(index, step, count):
    if count & (count - 1) == 0:
        return index ^ step
    return lax.rem(index + step, count)


def source_of(index, step, count):
    if count & (count - 1) == 0:
        return index ^ step
    return (index - step) % count if isinstance(index, int) else lax.rem(index + count - step, count)


def exchange(value, axis, step, stride):
    count = lax.axis_size(axis) // stride
    pairs = []
    for index in range(lax.axis_size(axis)):
        high, low = divmod(index, stride)
        other = high ^ step if count & (count - 1) == 0 else (high + step) % count
        pairs.append((index, other * stride + low))
    return lax.ppermute(value, axis, pairs)


def in_hbm(value):
    return pltpu.with_memory_space_constraint(value, pltpu.HBM)


def started(source, target, sem):
    copy = pltpu.make_async_copy(source, target, sem)
    copy.start()
    return copy


GROUPS = (0, -1, 1)


def column_of(tap):
    _, rest = divmod(tap, 9)
    tap_y, tap_z = rest // 3 - 1, rest % 3 - 1
    return 3 * GROUPS.index(-tap_z) + tap_y + 1


def extend(ref, wide_ref):
    slots = ref.shape[0]
    wide_ref[:slots] = ref[...]
    wide_ref[slots] = jnp.zeros(ref.shape[1:], ref.dtype)


def spread(links_ref, ref, start, step_x, slot, row, shift, win_ref):
    channels = ref.shape[-1]
    empty = ref.shape[0] - 1

    def fetch(step_y, step_z, first, rows):
        found = links_ref[slot, 0, 9 * (step_x + 1) + 3 * (step_y + 1) + step_z + 1]
        place = jnp.where(found < 0, empty, found)
        return ref[place, start + first : start + first + rows, :].astype(F32)

    def column(step_z):
        below = fetch(-1, step_z, PLANE - 16, 16).reshape(2, BE, channels)[1:]
        middle = fetch(0, step_z, 0, PLANE).reshape(BE, BE, channels)
        above = fetch(1, step_z, 0, 16).reshape(2, BE, channels)[:1]
        return jnp.concatenate([below, middle, above], axis=0)

    value = column(0)
    if shift != 0:
        turn = 1 if shift < 0 else BE - 1
        edge = 0 if shift < 0 else BE - 1
        place_z = lax.broadcasted_iota(jnp.int32, value.shape, 1)
        value = jnp.where(
            place_z == edge,
            pltpu.roll(column(shift), turn, axis=1),
            pltpu.roll(value, turn, axis=1),
        )
    for tap_y in (-1, 0, 1):
        lane = (3 * GROUPS.index(shift) + tap_y + 1) * channels
        part = value[1 - tap_y : 1 - tap_y + BE].reshape(PLANE, channels)
        win_ref[row : row + PLANE, lane : lane + channels] = part.astype(BF16)


def builders(links_ref, own_ref, low_ref, high_ref, win_ref, shift):
    slots = own_ref.shape[0] - 1
    calls = []
    for plane in range(BE + 2):
        if plane == 0:
            ref, start, step_x = low_ref, 0, -1
        elif plane == BE + 1:
            ref, start, step_x = high_ref, 0, 1
        else:
            ref, start, step_x = own_ref, (plane - 1) * PLANE, 0
        for slot in range(slots):
            row = (plane * slots + slot) * PLANE
            calls.append(
                functools.partial(
                    spread, links_ref, ref, start, step_x, slot, row, shift, win_ref
                )
            )
    return calls


def interleave(first, second):
    done = 0
    for index, call in enumerate(first):
        call()
        until = len(second) * (index + 1) // len(first)
        for other in second[done:until]:
            other()
        done = until


def prepare_kernel(own_hbm, pre_hbm, weight_hbm, own_wide, act_ref, taps_ref, pre_ref, sems):
    _, slots, voxels, channels = own_hbm.shape
    slab = slots * PLANE
    pre_copy = started(pre_hbm.at[0], pre_ref, sems.at[27])
    copies = [started(own_hbm.at[0], own_wide.at[pl.ds(0, slots)], sems.at[28])]
    for tap in range(27):
        lanes = slice(column_of(tap) * channels, (column_of(tap) + 1) * channels)
        copies.append(started(weight_hbm.at[tap], taps_ref.at[tap // 9, :, lanes], sems.at[tap]))
    own_wide[slots] = jnp.zeros((voxels, channels), BF16)
    pre_copy.wait()
    for pair in range(BE // 2):
        parts = []
        for x in (2 * pair, 2 * pair + 1):
            for slot in range(slots):
                parts.append(pre_ref[slot, x * PLANE : (x + 1) * PLANE, :])
        block = jnp.maximum(jnp.concatenate(parts, axis=0).astype(F32), 0.0)
        act_ref[:, pair * 2 * slab : (pair + 1) * 2 * slab] = block.T.astype(BF16)
    for copy in copies:
        copy.wait()


def prepare(own, pre, weight):
    _, slots, voxels, channels = own.shape
    return pl.pallas_call(
        prepare_kernel,
        out_shape=(
            jax.ShapeDtypeStruct((slots + 1, voxels, channels), BF16),
            jax.ShapeDtypeStruct((channels, slots * voxels), BF16),
            jax.ShapeDtypeStruct((3, channels, 9 * channels), BF16),
        ),
        in_specs=[HBM] * 3,
        out_specs=[VMEM] * 3,
        scratch_shapes=[
            pltpu.VMEM((slots, voxels, channels), BF16),
            pltpu.SemaphoreType.DMA((29,)),
        ],
        compiler_params=params(24),
        cost_estimate=pl.CostEstimate(
            flops=4 * MIB, bytes_accessed=12 * MIB, transcendentals=0
        ),
        name="prepare",
    )(in_hbm(own), in_hbm(pre), in_hbm(weight))


def input_kernel(
    links_ref, routes_ref, own_wide, low_ref, high_ref, pre_hbm, taps_ref,
    to_lower_ref, stay_ref, to_upper_ref, win_ref,
    low_wide, high_wide, acc_ref, octants_ref, pre_ref, out_sems, pre_sem,
):
    slots, voxels, channels = pre_ref.shape
    groups = routes_ref.shape[-1] // 8
    pre_copy = started(pre_hbm.at[0], pre_ref, pre_sem)
    for ref, wide in ((low_ref, low_wide), (high_ref, high_wide)):
        extend(ref, wide)
    octants_ref[...] = jnp.zeros_like(octants_ref)
    slab = slots * PLANE
    rows = BE * slab
    part = rows // 2

    def product(group, start):
        lanes = slice(3 * group * channels, 3 * (group + 1) * channels)
        total = None
        for index_x in range(3):
            offset = start + (2 - index_x) * slab
            term = lax.dot_general(
                win_ref[offset : offset + part, lanes],
                taps_ref[index_x, :, lanes],
                (((1,), (1,)), ((), ())),
                preferred_element_type=F32,
            )
            total = term if total is None else total + term
        if group > 0:
            total = total + acc_ref[start : start + part, :]
        acc_ref[start : start + part, :] = total

    def products(group):
        return [functools.partial(product, group, start) for start in range(0, rows, part)]

    sources = (links_ref, own_wide, low_wide, high_wide, win_ref)
    place_z = lax.broadcasted_iota(jnp.int32, (BE // 2, BE, channels), 1)
    targets = []
    for slot in range(slots):
        group = jnp.int32(3 * groups)
        for row in range(3):
            for place in range(groups):
                group = jnp.where(
                    routes_ref[row, 0, 8 * place] == 8 * slot, row * groups + place, group
                )
        targets.append(group)

    def finish(x, slot):
        start = x * slab + slot * PLANE
        value = acc_ref[start : start + PLANE, :]
        pre = pre_ref[slot, x * PLANE : (x + 1) * PLANE, :].astype(F32)
        value = jnp.where(pre > 0, value, 0.0).reshape(BE // 2, 2, BE, channels)
        even, odd = value[:, 0], value[:, 1]
        near = jnp.where(place_z < HALF, even, pltpu.roll(odd, HALF, axis=1))
        far = jnp.where(place_z < HALF, pltpu.roll(even, HALF, axis=1), odd)
        side, row = x // HALF, x % HALF * 16
        for side_y in range(2):
            for side_z, piece in enumerate((near, far)):
                block = piece[2 * side_y : 2 * side_y + 2].reshape(16, channels).astype(BF16)
                start = (4 * side + 2 * side_y + side_z) * PLANE + row
                octants_ref[targets[slot], start : start + 16, :] = block

    def finishes(planes):
        return [functools.partial(finish, x, slot) for x in planes for slot in range(slots)]

    for call in builders(*sources, GROUPS[0]):
        call()
    pre_copy.wait()
    interleave(products(0), builders(*sources, GROUPS[1]))
    interleave(products(1), builders(*sources, GROUPS[2]))
    last = products(2)
    last[0]()
    interleave(last[1:], finishes(range(HALF)))
    for call in finishes(range(HALF, BE)):
        call()
    outs = []
    for row, ref in enumerate((to_lower_ref, stay_ref, to_upper_ref)):
        outs.append(started(octants_ref.at[pl.ds(row * groups, groups)], ref, out_sems.at[row]))
    for copy in outs:
        copy.wait()


def input_gradient(links, routes, own_wide, low, high, pre, taps):
    _, slots, voxels, channels = pre.shape
    groups = routes.shape[-1] // 8
    rows = slots * voxels
    out = jax.ShapeDtypeStruct((groups, voxels, channels), BF16)
    windows = jax.ShapeDtypeStruct((slots * PLANE * (BE + 2), 9 * channels), BF16)
    return pl.pallas_call(
        input_kernel,
        out_shape=(out, out, out, windows),
        in_specs=[SMEM, SMEM, VMEM, VMEM, VMEM, HBM, VMEM],
        out_specs=(ANY, ANY, ANY, VMEM),
        scratch_shapes=[
            pltpu.VMEM((slots + 1, *low.shape[1:]), BF16),
            pltpu.VMEM((slots + 1, *low.shape[1:]), BF16),
            pltpu.VMEM((rows, channels), F32),
            pltpu.VMEM((3 * groups + 1, voxels, channels), BF16),
            pltpu.VMEM((slots, voxels, channels), BF16),
            pltpu.SemaphoreType.DMA((3,)),
            pltpu.SemaphoreType.DMA,
        ],
        compiler_params=params(20),
        cost_estimate=pl.CostEstimate(
            flops=2 * rows * 27 * channels * channels, bytes_accessed=8 * MIB, transcendentals=0
        ),
        name="input_gradient",
    )(links, routes, own_wide, low, high, in_hbm(pre), taps)


def filter_kernel(
    shard_rows, win_ref, act_ref, keep_ref, send_ref
):
    channels, rows = act_ref.shape
    slab = rows // BE
    lanes = channels // 2
    first = lax.rem(lax.axis_index("dom"), 2) == 0
    unit = math.gcd(channels, shard_rows)

    def product(tap):
        offset = (2 - tap // 9) * slab
        column = column_of(tap) * channels
        total = jnp.dot(
            act_ref[...],
            win_ref[offset : offset + rows, column : column + channels],
            preferred_element_type=F32,
        )
        left, right = total[:, :lanes], total[:, lanes:]
        keep = jnp.where(first, left, right).astype(BF16)
        send = jnp.where(first, right, left).astype(BF16)
        for part in range(channels // unit):
            shard, start = divmod(tap * channels + part * unit, shard_rows)
            span = slice(part * unit, (part + 1) * unit)
            keep_ref[shard, start : start + unit, :] = keep[span]
            send_ref[shard, start : start + unit, :] = send[span]

    for tap in sorted(range(27), key=column_of):
        product(tap)


def filter_gradient(shards, windows, act):
    channels, rows = act.shape
    shard_rows = 27 * channels // shards
    out = jax.ShapeDtypeStruct((shards, shard_rows, channels // 2), BF16)
    return pl.pallas_call(
        functools.partial(filter_kernel, shard_rows),
        out_shape=(out, out),
        in_specs=[VMEM, VMEM],
        out_specs=(VMEM, VMEM),
        compiler_params=params(12),
        cost_estimate=pl.CostEstimate(
            flops=2 * rows * 27 * channels * channels, bytes_accessed=8 * MIB, transcendentals=0
        ),
        name="filter_gradient",
    )(windows, act)


def down_kernel(
    groups, upper_ref, stay_ref, lower_ref, act_ref, keep_ref, send_ref, acc_ref
):
    step = pl.program_id(0)
    fine = act_ref.shape[0]
    channels = upper_ref.shape[-1]
    cells = upper_ref.shape[1] // fine
    taps = act_ref.shape[1] // cells

    @pl.when(step == 0)
    def _():
        acc_ref[...] = jnp.zeros_like(acc_ref)

    def work(ref):
        wide = []
        for place in range(fine):
            wide.append(
                jnp.concatenate(
                    [act_ref[place, tap * cells : (tap + 1) * cells, :] for tap in range(taps)],
                    axis=1,
                )
            )
        acc_ref[...] += jnp.dot(
            ref[0].T, jnp.concatenate(wide, axis=0), preferred_element_type=F32
        )

    for row, ref in enumerate((upper_ref, stay_ref, lower_ref)):
        pl.when(step // groups == row)(functools.partial(work, ref))

    @pl.when(step == pl.num_programs(0) - 1)
    def _():
        total = acc_ref[...].T
        first = lax.rem(lax.axis_index("dom"), 2) == 0
        lanes = channels // 2
        shards = keep_ref.shape[0]
        rows = total.shape[0] // shards
        left = total[:, :lanes].reshape(shards, rows, lanes)
        right = total[:, lanes:].reshape(shards, rows, lanes)
        keep_ref[:, :rows, :] = jnp.where(first, left, right).astype(BF16)
        send_ref[:, :rows, :] = jnp.where(first, right, left).astype(BF16)


def down_gradient(shards, count, from_upper, stay, from_lower, taps, fine_act):
    fine, voxels, fine_channels = fine_act.shape
    groups, _, channels = stay.shape
    whole = pl.BlockSpec((1, voxels, channels), lambda i: (i % groups, 0, 0))
    rows = count * piece_rows(taps * fine_channels // shards, count)
    down = jax.ShapeDtypeStruct((shards, rows, channels // 2), BF16)
    same = pl.BlockSpec(down.shape, lambda i: (0, 0, 0))
    return pl.pallas_call(
        functools.partial(down_kernel, groups),
        grid=(3 * groups,),
        out_shape=(down, down),
        in_specs=[
            whole, whole, whole, pl.BlockSpec((8, voxels, fine_channels), lambda i: (i, 0, 0))
        ],
        out_specs=(same, same),
        scratch_shapes=[pltpu.VMEM((channels, taps * fine_channels), F32)],
        compiler_params=params(40),
        cost_estimate=pl.CostEstimate(
            flops=64 * fine * voxels * fine_channels * channels, bytes_accessed=8 * MIB,
            transcendentals=0,
        ),
        name="down_gradient",
    )(from_upper, stay, from_lower, fine_act)


def fine_kernel(groups, upper_ref, stay_ref, lower_ref, weight_ref, grad_ref):
    step = pl.program_id(0)
    taps, fine_channels, channels = weight_ref.shape
    fine, voxels, _ = grad_ref.shape
    cells = voxels // taps

    def work(ref):
        product = lax.dot_general(
            ref[0],
            weight_ref[...].reshape(taps * fine_channels, channels),
            (((1,), (1,)), ((), ())),
            preferred_element_type=F32,
        ).astype(BF16)
        for place in range(fine):
            for tap in range(taps):
                grad_ref[place, tap * cells : (tap + 1) * cells, :] = product[
                    place * cells : (place + 1) * cells,
                    tap * fine_channels : (tap + 1) * fine_channels,
                ]

    for row, ref in enumerate((upper_ref, stay_ref, lower_ref)):
        pl.when(step // groups == row)(functools.partial(work, ref))


def fine_gradient(from_upper, stay, from_lower, weight):
    groups, voxels, channels = stay.shape
    whole = pl.BlockSpec((1, voxels, channels), lambda i: (i % groups, 0, 0))
    return pl.pallas_call(
        functools.partial(fine_kernel, groups),
        grid=(3 * groups,),
        out_shape=jax.ShapeDtypeStruct((24 * groups, voxels, weight.shape[1]), BF16),
        in_specs=[whole, whole, whole, pl.BlockSpec(weight.shape, lambda i: (0, 0, 0))],
        out_specs=pl.BlockSpec((8, voxels, weight.shape[1]), lambda i: (i, 0, 0)),
        compiler_params=params(40),
        cost_estimate=pl.CostEstimate(
            flops=2 * 24 * groups * voxels * weight.shape[1] * channels, bytes_accessed=4 * MIB,
            transcendentals=0,
        ),
        name="fine_gradient",
    )(from_upper, stay, from_lower, weight)


def piece_rows(rows, count):
    return -(-rows // (16 * count)) * 16


def tree(values):
    while len(values) > 1:
        values = [
            values[i] + values[i + 1] if i + 1 < len(values) else values[i]
            for i in range(0, len(values), 2)
        ]
    return values[0]


def cost(*arrays):
    moved = sum(math.prod(x.shape) * jnp.dtype(x.dtype).itemsize for x in arrays)
    return pl.CostEstimate(flops=moved, bytes_accessed=moved, transcendentals=0)


def shapes_of(count, shape):
    return [jax.ShapeDtypeStruct(shape, F32 if step == 0 else BF16) for step in range(count)]


def farthest_then_nearest(count):
    return [0, count - 1, *range(1, count - 1)]


def far_first(count):
    return [0, *range(count - 1, 0, -1)]


def pair_kernel(count, conv_ref, conv_got_ref, down_ref, down_got_ref, *outs):
    planes, slabs = outs[:count], outs[count:]
    shards, rows, _ = conv_ref.shape
    down_piece = down_ref.shape[1] // count
    piece = planes[0].shape[1] - down_piece
    cut = count * piece
    for step, ref in zip(farthest_then_nearest(shards), slabs):
        shard = relative(lax.axis_index("dp"), step, shards)
        total = conv_ref[shard, cut:, :].astype(F32) + conv_got_ref[shard, cut:, :].astype(F32)
        ref[...] = total.astype(ref.dtype)
    high = lax.axis_index("dom") // 2
    for step, ref in zip(far_first(count), planes):
        place = relative(high, step, count)
        for keep_ref, got_ref, size, start in (
            (conv_ref, conv_got_ref, piece, 0),
            (down_ref, down_got_ref, down_piece, piece),
        ):
            span = pl.ds(pl.multiple_of(place * size, 16), size)
            total = keep_ref[:, span, :].astype(F32) + got_ref[:, span, :].astype(F32)
            ref[:, start : start + size, :] = total.astype(ref.dtype)


def pair_sum(count, conv, conv_got, down, down_got):
    shards, rows, lanes = conv.shape
    down_piece = down.shape[1] // count
    unit = 16 * count
    piece = 16 * round((PLANE_FIRST * (rows + down.shape[1]) - down.shape[1]) / unit)
    outs = shapes_of(count, (shards, piece + down_piece, lanes))
    outs += shapes_of(shards, (rows - count * piece, lanes))
    outs = pl.pallas_call(
        functools.partial(pair_kernel, count),
        out_shape=outs,
        in_specs=[VMEM] * 4,
        out_specs=[VMEM] * len(outs),
        compiler_params=params(32),
        cost_estimate=cost(conv, conv_got, *outs),
        name="pair_sum",
    )(conv, conv_got, down, down_got)
    return outs[:count], outs[count:], (piece, down_piece)


def middle_kernel(count, shards, *refs):
    planes, slabs = refs[:count], refs[count : count + shards]
    to_slabs, mine_ref = refs[count + shards : -1], refs[-1]
    mine_ref[...] = tree([part[...].astype(F32) for part in slabs]).astype(BF16)
    for step, ref in zip(far_first(shards), to_slabs):
        shard = relative(lax.axis_index("dp"), step, shards)
        ref[...] = tree([part[shard].astype(F32) for part in planes]).astype(ref.dtype)


def middle_sum(planes, slabs):
    count, shards = len(planes), len(slabs)
    _, piece, lanes = planes[0].shape
    outs = shapes_of(shards, (piece, lanes)) + [jax.ShapeDtypeStruct(slabs[0].shape, BF16)]
    parts = [*planes, *slabs]
    outs = pl.pallas_call(
        functools.partial(middle_kernel, count, shards),
        out_shape=outs,
        in_specs=[VMEM] * len(parts),
        out_specs=[VMEM] * len(outs),
        compiler_params=params(32),
        cost_estimate=cost(*parts, *outs),
        name="middle_sum",
    )(*parts)
    return outs[:shards], outs[shards]


def last_kernel(factor, count, *refs):
    *refs, _, planes_ref, slabs_ref = refs
    total = tree([part[...].astype(F32) for part in refs[count:]])
    planes_ref[...] = (total * factor).astype(BF16)
    steps = far_first(count)
    total = tree([refs[steps.index(step)][...].astype(F32) for step in range(count)])
    slabs_ref[...] = (total * factor).astype(BF16)


def last_sum(factor, slabs, planes, after):
    parts = [*planes, *slabs]
    return pl.pallas_call(
        functools.partial(last_kernel, factor, len(planes)),
        out_shape=[
            jax.ShapeDtypeStruct(slabs[0].shape, BF16), jax.ShapeDtypeStruct(planes[0].shape, BF16)
        ],
        in_specs=[VMEM] * len(parts) + [HBM],
        out_specs=[VMEM] * 2,
        compiler_params=params(32),
        cost_estimate=cost(*parts),
        name="last_sum",
    )(*parts, in_hbm(after))


def gather_kernel(count, piece, down_piece, *refs):
    near, far = refs[:count], refs[count : 2 * count]
    rest_ref, rest_far_ref, conv_ref, down_ref, conv_whole, down_whole, sems = refs[2 * count :]
    lanes = rest_ref.shape[1]
    cut = count * piece
    high = lax.axis_index("dom") // 2
    low = lax.rem(lax.axis_index("dom"), 2)
    own = pl.ds(pl.multiple_of(low * lanes, lanes), lanes)
    other = pl.ds(pl.multiple_of((1 - low) * lanes, lanes), lanes)
    conv_whole[cut:, own] = rest_ref[...].astype(F32)
    conv_whole[cut:, other] = rest_far_ref[...].astype(F32)
    tail = pl.ds(cut, conv_ref.shape[0] - cut)
    copies = [started(conv_whole.at[tail], conv_ref.at[tail], sems.at[0])]
    for index, step in enumerate(far_first(count)):
        place = source_of(high, step, count)
        rows = pl.ds(pl.multiple_of(place * piece, 16), piece)
        down_rows = pl.ds(pl.multiple_of(place * down_piece, 16), down_piece)
        for lane, ref in ((own, near[index]), (other, far[index])):
            conv_whole[rows, lane] = ref[:piece, :].astype(F32)
            down_whole[down_rows, lane] = ref[piece:, :].astype(F32)
        copies.append(started(conv_whole.at[rows], conv_ref.at[rows], sems.at[index + 1]))
    copies.append(
        started(down_whole.at[pl.ds(0, down_ref.shape[0])], down_ref, sems.at[count + 1])
    )
    for copy in copies:
        copy.wait()


def gather_up(conv_rows, down_rows, pieces, near, far, rest, rest_far):
    count = len(near)
    lanes = rest.shape[1]
    outs = [jax.ShapeDtypeStruct((rows, 2 * lanes), F32) for rows in (conv_rows, down_rows)]
    return pl.pallas_call(
        functools.partial(gather_kernel, count, *pieces),
        out_shape=outs,
        in_specs=[VMEM] * (2 * count + 2),
        out_specs=[ANY] * 2,
        scratch_shapes=[
            pltpu.VMEM((conv_rows, 2 * lanes), F32),
            pltpu.VMEM((count * pieces[1], 2 * lanes), F32),
            pltpu.SemaphoreType.DMA((count + 2,)),
        ],
        compiler_params=params(32),
        cost_estimate=cost(*near, *far, *outs),
        name="gather_up",
    )(*near, *far, rest, rest_far)


def body(grad_out, pre_act, conv_weight, down_weight, fine_act, neighbours, octant_routes):
    own = grad_out[0]
    links = neighbours.transpose(1, 0, 2)
    routes = octant_routes.transpose(0, 2, 1, 3)[0]
    slots, voxels, channels = own.shape
    devices = lax.axis_size("dom")
    shards = lax.axis_size("dp")
    count = devices // 2
    factor = 1.0 / math.sqrt(shards * devices * slots * voxels)

    forward = [(i, i + 1) for i in range(devices - 1)]
    backward = [(i + 1, i) for i in range(devices - 1)]
    ring = [(i, (i + 1) % devices) for i in range(devices)]
    swap = [(i, i ^ 1) for i in range(devices)]

    def spread_out(parts, axis, stride, steps=None):
        steps = steps or list(range(len(parts)))
        return [parts[0]] + [
            exchange(part, axis, step, stride) for step, part in zip(steps[1:], parts[1:])
        ]

    low = lax.ppermute(own[:, voxels - PLANE :], "dom", forward)
    high = lax.ppermute(own[:, :PLANE], "dom", backward)
    own_wide, act, taps = prepare(grad_out, pre_act, conv_weight)
    to_lower, stay, to_upper, windows = input_gradient(
        links, routes, own_wide, low, high, pre_act, taps
    )
    from_upper = lax.ppermute(to_lower, "dom", [(b, a) for a, b in ring])
    from_lower = lax.ppermute(to_upper, "dom", ring)
    conv_keep, conv_send = filter_gradient(shards, windows, act)
    down_keep, down_send = down_gradient(
        shards, count, from_upper, stay, from_lower, down_weight.shape[0], fine_act[0]
    )
    fine_grad = fine_gradient(from_upper, stay, from_lower, down_weight)
    conv_got = lax.ppermute(conv_send, "dom", swap)
    down_got = lax.ppermute(down_send, "dom", swap)

    planes, slabs, pieces = pair_sum(count, conv_keep, conv_got, down_keep, down_got)
    slabs = spread_out(slabs, "dp", 1, farthest_then_nearest(shards))
    planes = spread_out(planes, "dom", 2, far_first(count))
    to_slabs, rest = middle_sum(planes, slabs)
    to_slabs = spread_out(to_slabs, "dp", 1, far_first(shards))
    mine, rest = last_sum(factor, to_slabs, spread_out([rest] * count, "dom", 2, far_first(count)), fine_grad)
    near = spread_out([mine] * count, "dom", 2, far_first(count))
    far = [lax.ppermute(value, "dom", swap) for value in near]
    rest_far = lax.ppermute(rest, "dom", swap)
    conv_rows = 27 * channels // shards
    down_rows = down_weight.shape[0] * down_weight.shape[1] // shards
    conv_grad, down_grad = gather_up(conv_rows, down_rows, pieces, near, far, rest, rest_far)
    return (fine_grad[None], conv_grad, down_grad)


def solution(mesh):
    return jax.shard_map(
        body,
        mesh=mesh,
        in_specs=(
            P("dp", "dom", None, None),
            P("dp", "dom", None, None),
            P(),
            P(),
            P("dp", "dom", None, None),
            P("dp", "dom", None),
            P("dp", "dom", None, None),
        ),
        out_specs=(P("dp", "dom", None, None), P("dp", None), P("dp", None)),
        check_vma=False,
    )
```
